32 devices in a mesh: batch: 8 (over z, y), chan: 4 (over x, core).
Axes of the slice: x: 2, y: 2, z: 4, core: 2. Of those that a mesh axis runs over, the one named last changes fastest.
Arguments:
- entry_activation: bfloat16 [64, 14, 14, 1024], P('batch', None, None, 'chan'), may hold values from -16 to 16
- image_bounds: int32 [64, 2], P('batch'), may hold values from 8 to 14, as said below
- loss_sensitivity: bfloat16 [64, 7, 7, 2048], P('batch', None, None, 'chan'), may hold values from -6 to 6
- first_contract_kernel: bfloat16 [1024, 512], P(None, 'chan'), may hold values from -0.1875 to 0.1875
- first_strided_kernel: bfloat16 [3, 3, 512, 512], P(None, None, None, 'chan'), may hold values from -0.09375 to 0.09375
- first_enlarge_kernel: bfloat16 [512, 2048], P(None, 'chan'), may hold values from -0.25 to 0.25
- projection_kernel: bfloat16 [1024, 2048], P(None, 'chan'), may hold values from -0.1875 to 0.1875
- second_contract_kernel: bfloat16 [2048, 512], P(None, 'chan'), may hold values from -0.125 to 0.125
- second_spatial_kernel: bfloat16 [3, 3, 512, 512], P(None, None, None, 'chan'), may hold values from -0.09375 to 0.09375
- second_enlarge_kernel: bfloat16 [512, 2048], P(None, 'chan'), may hold values from -0.25 to 0.25
- bottleneck_gains: float32 [4, 512], P(None, 'chan'), may hold values from 0.5 to 1.5
- bottleneck_biases: float32 [4, 512], P(None, 'chan'), may hold values from -2 to 2
- wide_gain_vector: float32 [3, 2048], P(None, 'chan'), may hold values from 0.5 to 1.5
- wide_bias_vector: float32 [3, 2048], P(None, 'chan'), may hold values from -2 to 2
Outputs:
- result: bfloat16 [64, 7, 7, 2048], P('batch', None, None, 'chan')
- inputs_grad: bfloat16 [64, 14, 14, 1024], P('batch', None, None, 'chan')
- reducing_grad: float32 [1024, 512], P(None, 'chan')
- spatial_grad: float32 [3, 3, 512, 512], P(None, None, None, 'chan')
- widening_grad: float32 [512, 2048], P(None, 'chan')
- shortcut_grad: float32 [1024, 2048], P(None, 'chan')
- narrowing_grad: float32 [2048, 512], P(None, 'chan')
- middle_grad: float32 [3, 3, 512, 512], P(None, None, None, 'chan')
- expanding_grad: float32 [512, 2048], P(None, 'chan')
- scale_gradient: float32 [4, 512], P(None, 'chan')
- offset_gradient: float32 [4, 512], P(None, 'chan')
- amplitude_gradient: float32 [3, 2048], P(None, 'chan')
- baseline_gradient: float32 [3, 2048], P(None, 'chan')
The draws below stay inside these ranges and needn't reach their ends.
Inputs may be any that keep to these rules, and one draw needn't show every extreme that they name: `image_bounds`: each image's valid region is the top-left corner of the padded 14 x 14 grid; rows and columns are even.
All inputs are finite; a program needn't handle non-finite values.
Results may differ from the reference program's by a relative error of at most 0.025.
Values may be sent and summed in bfloat16 or wider, within the bound.
No kernel may reach another device: no remote copies, remote signals or barrier semaphores. Data moves between devices by JAX's collectives and lax.ppermute only.
A program may use at most 128 MiB of HBM per device.

```python
import jax
import jax.numpy as jnp
from jax import lax

C_IN = 1024
MID = 512
EXIT_FEATURE_DIM = 2048
SIDE = 14
IMAGES = 64


def draw_image_bounds(key, part):
    key = jax.random.fold_in(key, 11)
    cuts = jnp.array([[0, 0], [0, 2], [2, 0], [0, 4], [4, 0], [0, 6], [6, 0], [2, 2], [4, 4]], dtype=jnp.int32)
    picked = jax.random.randint(key, (IMAGES,), 0, 9)
    picked = picked.at[0].set(0).at[1].set(6)
    return (SIDE - cuts[picked]).astype(jnp.int32)


def draw_entry_activation(key, part):
    key = jax.random.fold_in(key, 12)
    shape = (IMAGES, SIDE, SIDE, C_IN)
    steps = jnp.arange(IMAGES, dtype=jnp.float32) / max(IMAGES - 1, 1)
    base = jax.random.truncated_normal(key, -3.0, 3.0, shape, jnp.float32)
    ramp = 1.0 + 2.0 * steps
    return (base * ramp[:, None, None, None]).astype(jnp.bfloat16)


def steps_of(own_key, dims, pieces, smallest, top_value):
    def one(dim, parts):
        heights = jax.random.uniform(jax.random.fold_in(jax.random.fold_in(own_key, 6), dim), (parts,), jnp.float32, smallest / len(pieces), top_value / len(pieces))
        return jnp.repeat(jnp.exp(heights), dims[dim] // parts).reshape((-1,) + (1,) * (len(dims) - dim - 1))

    loudness = one(*pieces[0])
    for cut in pieces[1:]:
        loudness = loudness * one(*cut)
    return loudness


def scatter_about(rng, dims, scale, most, shards=(), kind=jnp.bfloat16):
    values = scale * jax.random.normal(rng, dims, jnp.float32)
    if shards:
        values = values * steps_of(rng, dims, shards, -0.22, 0.18)
    return jnp.clip(values, -most, most).astype(kind)


def setup_inputs(seed: int = 0) -> dict:
    keys = jax.random.split(jax.random.key(seed), 15)
    return {
        "entry_activation": draw_entry_activation(jax.random.fold_in(keys[14], 71), 0),
        "image_bounds": draw_image_bounds(jax.random.fold_in(keys[14], 71), 0),
        "loss_sensitivity": scatter_about(keys[2], (IMAGES, SIDE // 2, SIDE // 2, EXIT_FEATURE_DIM), 1.0, 6.0, ((0, 8), (3, 4))),
        "first_contract_kernel": scatter_about(keys[3], (C_IN, MID), C_IN ** -0.5, 0.1875, ((1, 4),)),
        "first_strided_kernel": scatter_about(keys[4], (3, 3, MID, MID), (9 * MID) ** -0.5, 0.09375, ((3, 4),)),
        "first_enlarge_kernel": scatter_about(keys[5], (MID, EXIT_FEATURE_DIM), MID ** -0.5, 0.25, ((1, 4),)),
        "projection_kernel": scatter_about(keys[6], (C_IN, EXIT_FEATURE_DIM), C_IN ** -0.5, 0.1875, ((1, 4),)),
        "second_contract_kernel": scatter_about(keys[7], (EXIT_FEATURE_DIM, MID), EXIT_FEATURE_DIM ** -0.5, 0.125, ((1, 4),)),
        "second_spatial_kernel": scatter_about(keys[8], (3, 3, MID, MID), (9 * MID) ** -0.5, 0.09375, ((3, 4),)),
        "second_enlarge_kernel": scatter_about(keys[9], (MID, EXIT_FEATURE_DIM), MID ** -0.5, 0.25, ((1, 4),)),
        "bottleneck_gains": jnp.clip(1.0 + 0.1 * jax.random.normal(keys[10], (4, MID), jnp.float32), 0.5, 1.5),
        "bottleneck_biases": scatter_about(keys[11], (4, MID), 0.3, 2.0, ((1, 4),), jnp.float32),
        "wide_gain_vector": jnp.clip(1.0 + 0.1 * jax.random.normal(keys[12], (3, EXIT_FEATURE_DIM), jnp.float32), 0.5, 1.5),
        "wide_bias_vector": scatter_about(keys[13], (3, EXIT_FEATURE_DIM), 0.3, 2.0, ((1, 4),), jnp.float32),
    }


@jax.custom_vjp
def low(v):
    return lax.optimization_barrier(v.astype(jnp.bfloat16)).astype(jnp.float32)

@jax.custom_vjp
def low_back(v):
    return v

def low_keep(v):
    return (low(v), None)

def low_pass(retained_values, grad):
    return (grad,)

def back_keep(v):
    return (v, None)

def back_low(retained_values, grad):
    return (low(grad),)
low.defvjp(low_keep, low_pass)
low_back.defvjp(back_keep, back_low)
epsilon = 1e-05
precise = lax.Precision.HIGHEST

def masks_of(image_bounds, side, stride):
    images = image_bounds.shape[0]
    rows = lax.broadcasted_iota(jnp.int32, (images, side, side, 1), 1) * stride
    cols = lax.broadcasted_iota(jnp.int32, (images, side, side, 1), 2) * stride
    inside = (rows < image_bounds[:, 0][:, None, None, None]) & (cols < image_bounds[:, 1][:, None, None, None])
    return inside.astype(jnp.float32)

def standardize_batch(z, valid, count, gain, shift):
    total = lax.optimization_barrier(jnp.sum(z * valid, axis=(0, 1, 2)))
    squares = lax.optimization_barrier(jnp.sum(z * z * valid, axis=(0, 1, 2)))
    mean = total / count
    inverse = lax.rsqrt(squares / count - mean * mean + epsilon)
    return (z - mean) * inverse * gain + shift

def pointwise_layer(block_entry_tensor, weight):
    return jnp.einsum('nhwc,cd->nhwd', block_entry_tensor, weight, precision=precise)

def spatial_conv(block_entry_tensor, weight, stride):
    return lax.conv_general_dilated(block_entry_tensor, weight, (stride, stride), ((1, 1), (1, 1)), dimension_numbers=('NHWC', 'HWIO', 'NHWC'), precision=precise)

def reference(entry_activation, image_bounds, loss_sensitivity, first_contract_kernel, first_strided_kernel, first_enlarge_kernel, projection_kernel, second_contract_kernel, second_spatial_kernel, second_enlarge_kernel, bottleneck_gains, bottleneck_biases, wide_gain_vector, wide_bias_vector):
    side = entry_activation.shape[1]
    valid_in = masks_of(image_bounds, side, 1)
    emitted_pixel_filter = masks_of(image_bounds, side // 2, 2)
    count_in = jnp.sum(valid_in)
    emitted_total = jnp.sum(emitted_pixel_filter)

    def evaluate_network(block_entry_tensor, first_contract_kernel, first_strided_kernel, first_enlarge_kernel, projection_kernel, second_contract_kernel, second_spatial_kernel, second_enlarge_kernel, bottleneck_gains, bottleneck_biases, wide_gain_vector, wide_bias_vector):
        masked = block_entry_tensor * valid_in
        z_one = low_back(pointwise_layer(masked, first_contract_kernel))
        first = low(valid_in * jax.nn.gelu(standardize_batch(z_one, valid_in, count_in, bottleneck_gains[0], bottleneck_biases[0])))
        z_two = low_back(spatial_conv(first, first_strided_kernel, 2))
        second = low(emitted_pixel_filter * jax.nn.gelu(standardize_batch(z_two, emitted_pixel_filter, emitted_total, bottleneck_gains[1], bottleneck_biases[1])))
        first_block_standardized = low_back(pointwise_layer(second, first_enlarge_kernel))
        bypass_standardized = low_back(pointwise_layer(masked[:, ::2, ::2, :], projection_kernel))
        summed_result = standardize_batch(first_block_standardized, emitted_pixel_filter, emitted_total, wide_gain_vector[0], wide_bias_vector[0]) + standardize_batch(bypass_standardized, emitted_pixel_filter, emitted_total, wide_gain_vector[1], wide_bias_vector[1])
        running_residue = emitted_pixel_filter * jax.nn.gelu(summed_result)
        carry_low = low(running_residue)
        z_four = low_back(pointwise_layer(carry_low, second_contract_kernel))
        fourth = low(emitted_pixel_filter * jax.nn.gelu(standardize_batch(z_four, emitted_pixel_filter, emitted_total, bottleneck_gains[2], bottleneck_biases[2])))
        z_five = low_back(spatial_conv(fourth, second_spatial_kernel, 1))
        fifth_layer = low(emitted_pixel_filter * jax.nn.gelu(standardize_batch(z_five, emitted_pixel_filter, emitted_total, bottleneck_gains[3], bottleneck_biases[3])))
        final_standardized = low_back(pointwise_layer(fifth_layer, second_enlarge_kernel))
        return emitted_pixel_filter * jax.nn.gelu(standardize_batch(final_standardized, emitted_pixel_filter, emitted_total, wide_gain_vector[2], wide_bias_vector[2]) + running_residue)
    real_number_array = (entry_activation.astype(jnp.float32), first_contract_kernel.astype(jnp.float32), first_strided_kernel.astype(jnp.float32), first_enlarge_kernel.astype(jnp.float32), projection_kernel.astype(jnp.float32), second_contract_kernel.astype(jnp.float32), second_spatial_kernel.astype(jnp.float32), second_enlarge_kernel.astype(jnp.float32), bottleneck_gains.astype(jnp.float32), bottleneck_biases.astype(jnp.float32), wide_gain_vector.astype(jnp.float32), wide_bias_vector.astype(jnp.float32))
    primal, pull = jax.vjp(evaluate_network, *real_number_array)
    grads = pull(loss_sensitivity.astype(jnp.float32))
    return (primal.astype(jnp.bfloat16), grads[0].astype(jnp.bfloat16), grads[1], grads[2], grads[3], grads[4], grads[5], grads[6], grads[7], grads[8], grads[9], grads[10], grads[11])
```

```python
import functools

import jax
import jax.numpy as jnp
from jax import lax
from jax.experimental import pallas as pl
from jax.experimental.pallas import tpu as pltpu
from jax.sharding import PartitionSpec as P

EPS = 1e-05
BF = jnp.bfloat16
F32 = jnp.float32
GELU_A = 0.7978845608028654
GELU_B = 0.044715
LANES = 128
IMAGES = 8
CELLS = 8
CHUNK = CELLS * IMAGES
VMEM_LIMIT = 56 * 1024 * 1024


def dot(a, b, dims=((1,), (0,))):
    return lax.dot_general(a, b, (dims, ((), ())), preferred_element_type=F32)


def gelu(v):
    return 0.5 * v * (1.0 + jnp.tanh(GELU_A * v * (1.0 + GELU_B * v * v)))


def gelu_slope(v):
    square = v * v
    t = jnp.tanh(GELU_A * v * (1.0 + GELU_B * square))
    return 0.5 * (1.0 + t) * (1.0 + v * (1.0 - t) * (GELU_A + 3.0 * GELU_A * GELU_B * square))


class Masks:
    def __init__(self, bounds):
        image = lax.broadcasted_iota(jnp.int32, (IMAGES, LANES), 0)
        high = jnp.zeros((IMAGES, LANES), jnp.int32)
        low = jnp.zeros((IMAGES, LANES), jnp.int32)
        inside = jnp.int32(0)
        outside = jnp.int32(0)
        for n in range(IMAGES):
            h, w = bounds[n, 0], bounds[n, 1]
            high = jnp.where(image == n, h, high)
            low = jnp.where(image == n, w, low)
            inside = inside + h * w
            outside = outside + lax.shift_right_logical(h + 1, 1) * lax.shift_right_logical(w + 1, 1)
        self.high = high[None]
        self.low = low[None]
        self.column = lax.broadcasted_iota(jnp.int32, (CELLS, IMAGES, LANES), 0) * 2
        self.local_in = inside.astype(F32)
        self.local_out = outside.astype(F32)

    def large(self, row, parity):
        return (row < self.high) & (self.column + parity < self.low)

    def small(self, row):
        return (2 * row < self.high) & (self.column < self.low)


def keep(mask, value):
    return jnp.where(mask, value, 0.0)


def cube(rows):
    return rows.astype(F32).reshape(CELLS, IMAGES, LANES)


def flat(value):
    return value.reshape(CHUNK, LANES)


def total_of(value):
    return jnp.sum(value, axis=0)


def row_sum(value):
    return jnp.sum(value, axis=0, keepdims=True)


def at(step, size):
    return pl.ds(pl.multiple_of(step * size, size), size)


def lane_block(index, width=LANES):
    return pl.ds(pl.multiple_of(index * width, width), width)


def push_left(value):
    return jnp.concatenate([value[1:], jnp.zeros((1, IMAGES, LANES), F32)], axis=0)


def push_right(value):
    return jnp.concatenate([jnp.zeros((1, IMAGES, LANES), F32), value[:-1]], axis=0)


def norm_of(got, who, batch, chan, k, row, local, count):
    column = who[0] ^ k
    total = got[column]
    for n in range(1, batch):
        total = total + got[n * chan + column]
    mine = got[who[1] * chan + column]
    mean = total[row : row + 1] / count
    inverse = lax.rsqrt(total[row + 1 : row + 2] / count - mean * mean + EPS)
    return mine[row : row + 1] / local - mean, inverse


def whole(got):
    total = got[0]
    for n in range(1, got.shape[0]):
        total = total + got[n]
    return total


def in_vmem(kernel, ins, outs, scratch=(), flops=0, name=None):
    specs = [
        pl.BlockSpec(memory_space=pltpu.SMEM if v.dtype == jnp.int32 else pltpu.VMEM) for v in ins
    ]
    size = sum(v.size * v.dtype.itemsize for v in ins)
    return pl.pallas_call(
        kernel,
        out_shape=[jax.ShapeDtypeStruct(s, d) for s, d in outs],
        in_specs=specs,
        out_specs=[pl.BlockSpec(memory_space=pltpu.VMEM) for _ in outs],
        scratch_shapes=[pltpu.VMEM(s, d) for s, d in scratch],
        compiler_params=pltpu.CompilerParams(vmem_limit_bytes=VMEM_LIMIT),
        cost_estimate=pl.CostEstimate(flops=flops, bytes_accessed=size, transcendentals=0),
        name=name,
    )(*ins)


def sums_of(z, chunks, lanes, mask=None):
    def step(t, carry):
        value = cube(z[at(t, CHUNK), lanes])
        if mask is not None:
            value = keep(mask(t), value)
        return carry[0] + total_of(value), carry[1] + total_of(value * value)

    zero = jnp.zeros((IMAGES, LANES), F32)
    total, squares = lax.fori_loop(0, chunks, step, (zero, zero))
    return row_sum(total), row_sum(squares)


def centre_into(out, z, chunks, lanes, mean):
    def step(t, _):
        out[at(t, CHUNK), lanes] = (z[at(t, CHUNK), lanes] - mean).astype(BF)
        return 0

    lax.fori_loop(0, chunks, step, 0)


def broadcast_rows(out, rows):
    block = jnp.concatenate(
        list(rows) + [jnp.zeros((out.shape[1] - len(rows), LANES), F32)]
        if len(rows) < out.shape[1]
        else list(rows),
        axis=0,
    )
    out[...] = jnp.broadcast_to(block[None], out.shape)


def fill_rows(out, rows):
    for n, row in enumerate(rows):
        out[n : n + 1, :] = row
    if len(rows) < out.shape[0]:
        out[len(rows) :, :] = jnp.zeros((out.shape[0] - len(rows), LANES), F32)


def permutation(side, back):
    size = 16 * IMAGES if side else 8 * IMAGES
    one = lax.broadcasted_iota(jnp.int32, (size, size), 1 if back else 0)
    other = lax.broadcasted_iota(jnp.int32, (size, size), 0 if back else 1)
    image = one & 7
    column = (one >> 3) & 7
    if side:
        target = image * 16 + column * 2 + (one >> 6)
    else:
        target = image * 8 + column
    return (other == target).astype(F32).astype(BF)


def enter_kernel(bounds, x, out, held):
    masks = Masks(bounds)
    order = permutation(True, False)
    held[...] = jnp.zeros(held.shape, BF)
    width = x.shape[3]

    def step(r, _):
        for n in range(IMAGES):
            held[16 * n : 16 * n + x.shape[2], :] = x[n, r]
        moved = dot(order, held[...])
        for parity in range(2):
            mask = masks.large(r, parity)
            for q in range(width // LANES):
                part = moved[parity * CHUNK : (parity + 1) * CHUNK, q * LANES : (q + 1) * LANES]
                out[at(r * 2 + parity, CHUNK), q * LANES : (q + 1) * LANES] = flat(
                    keep(mask, cube(part))
                ).astype(BF)
        return 0

    lax.fori_loop(0, x.shape[1], step, 0)


def loss_kernel(x, out, held):
    order = permutation(False, False)
    held[...] = jnp.zeros(held.shape, F32)

    def step(i, _):
        for n in range(IMAGES):
            held[8 * n : 8 * n + x.shape[2], :] = x[n, i].astype(F32)
        out[at(i, CHUNK), :] = dot(order, held[...].astype(BF)).astype(BF)
        return 0

    lax.fori_loop(0, x.shape[1], step, 0)


def first_kernel(chan, bounds, who, *refs):
    source, (w, zc, stats, z) = refs[:chan], refs[chan:]
    masks = Masks(bounds)
    rows, depth = source[0].shape
    part = rows // 4

    def step(t, _):
        total = None
        for k in range(chan):
            term = dot(source[k][at(t, part), :], w[at(who[0] ^ k, depth), :])
            total = term if total is None else total + term
        z[at(t, part), :] = total
        return 0

    lax.fori_loop(0, 4, step, 0)
    chunks = rows // CHUNK
    total, squares = sums_of(z, chunks, slice(0, LANES))
    ones = jnp.ones((1, LANES), F32)
    broadcast_rows(stats, (total, squares, ones * masks.local_in, ones * masks.local_out))
    centre_into(zc, z, chunks, slice(0, LANES), total / masks.local_in)


def shortcut_kernel(chan, bounds, who, *refs):
    source, (w, even, zc, stats, z) = refs[:chan], refs[chan:]
    masks = Masks(bounds)
    rows, width = z.shape
    depth = source[0].shape[1]
    chunks = rows // CHUNK
    for k in range(chan):
        for t in range(chunks):
            even[t * CHUNK : (t + 1) * CHUNK, lane_block(who[0] ^ k, depth)] = source[k][
                4 * t * CHUNK : (4 * t + 1) * CHUNK, :
            ]
    z[...] = dot(even[...], w[...])
    blocks = width // LANES
    for q in range(blocks):
        lanes = slice(q * LANES, (q + 1) * LANES)
        total, squares = sums_of(z, chunks, lanes)
        stats[q : q + 1, :] = total
        stats[blocks + q : blocks + q + 1, :] = squares
        centre_into(zc, z, chunks, lanes, total / masks.local_out)


def strided_kernel(batch, chan, bounds, who, got, *refs):
    near, (tabs, w, extra, a, zc, stats, norms, counts, z) = refs[:chan], refs[chan:]
    masks = Masks(bounds)
    total = whole(got)
    count_in, count_out = total[2:3] / chan, total[3:4] / chan
    fill_rows(counts, (count_in, count_out))
    params = []
    for k in range(chan):
        norm = norm_of(got, who, batch, chan, k, 0, masks.local_in, count_in)
        params.append(norm)
        norms[2 * k : 2 * k + 1, :] = norm[0]
        norms[2 * k + 1 : 2 * k + 2, :] = norm[1]
    width = a.shape[3]
    for tap in range(3):
        a[tap, 0, 0:CHUNK, :] = jnp.zeros((CHUNK, width), BF)
    side = near[0].shape[0] // (2 * CHUNK)

    def step(r, _):
        line = r + 1
        half, place = line & 1, lax.shift_right_logical(line, 1)
        for k in range(chan):
            lanes = lane_block(who[0] ^ k)
            scale = params[k][1] * tabs[k, 0:1, :]
            shift = params[k][0] * scale + tabs[k, 4:5, :]
            for parity in range(2):
                pre = cube(near[k][at(r * 2 + parity, CHUNK), :]) * scale + shift
                value = keep(masks.large(r, parity), gelu(pre))
                a[1 + parity, half, at(place, CHUNK), lanes] = flat(value).astype(BF)
                if parity:
                    a[0, half, at(place, CHUNK), lanes] = flat(push_right(value)).astype(BF)
        return 0

    lax.fori_loop(0, side, step, 0)
    rows = z.shape[0]
    acc = None
    for i, (half, first) in enumerate(((0, 0), (1, 0), (0, CHUNK))):
        for j in range(3):
            term = dot(a[j, half, first : first + rows, :], w[i, j])
            acc = term if acc is None else acc + term
    z[...] = acc
    chunks = rows // CHUNK
    total, squares = sums_of(z, chunks, slice(0, LANES), masks.small)
    block = jnp.concatenate([total, squares, jnp.zeros((6, LANES), F32), extra[...]], axis=0)
    stats[...] = jnp.broadcast_to(block[None], stats.shape)
    centre_into(zc, z, chunks, slice(0, LANES), total / masks.local_out)


def activate_into(near, params, tabs, gain, chan, who, masks, chunks, store):
    def step(t, _):
        mask = masks.small(t)
        for k in range(chan):
            scale = params[k][1] * tabs[k, gain : gain + 1, :]
            shift = params[k][0] * scale + tabs[k, gain + 4 : gain + 5, :]
            value = keep(mask, gelu(cube(near[k][at(t, CHUNK), :]) * scale + shift))
            store(t, lane_block(who[0] ^ k), value)
        return 0

    lax.fori_loop(0, chunks, step, 0)


def store_norms(norms, params):
    for k, norm in enumerate(params):
        norms[2 * k : 2 * k + 1, :] = norm[0]
        norms[2 * k + 1 : 2 * k + 2, :] = norm[1]


def enlarge_kernel(batch, chan, bounds, who, got, *refs):
    near, (tabs, counts, w, a, zc, stats, norms, z) = refs[:chan], refs[chan:]
    masks = Masks(bounds)
    count = counts[1:2, :]
    params = [norm_of(got, who, batch, chan, k, 0, masks.local_out, count) for k in range(chan)]
    store_norms(norms, params)
    chunks = z.shape[0] // CHUNK

    def store(t, lanes, value):
        a[at(t, CHUNK), lanes] = flat(value).astype(BF)

    activate_into(near, params, tabs, 1, chan, who, masks, chunks, store)
    z[...] = dot(a[...], w[...])
    rows = wide_sums(z, zc, chunks, masks)
    broadcast_rows(stats, rows)


def wide_sums(z, zc, chunks, masks):
    blocks = z.shape[1] // LANES
    totals, squares = [], []
    for q in range(blocks):
        lanes = slice(q * LANES, (q + 1) * LANES)
        total, square = sums_of(z, chunks, lanes)
        totals.append(total)
        squares.append(square)
        if zc is not None:
            centre_into(zc, z, chunks, lanes, total / masks.local_out)
    return totals + squares


def wide_norm(got, who, batch, chan, k, row, blocks, local, count):
    column = who[0] ^ k
    total = got[column]
    for n in range(1, batch):
        total = total + got[n * chan + column]
    mine = got[who[1] * chan + column]
    mean = total[row : row + blocks] / count
    inverse = lax.rsqrt(total[row + blocks : row + 2 * blocks] / count - mean * mean + EPS)
    return mine[row : row + blocks] / local - mean, inverse


def merge_kernel(batch, chan, bounds, who, got3, got2, *refs):
    near3, nears = refs[:chan], refs[chan : 2 * chan]
    tabs, counts, w, y, own, zc, stats, norms, z = refs[2 * chan :]
    masks = Masks(bounds)
    count = counts[1:2, :]
    rows, width = near3[0].shape
    blocks = width // LANES
    chunks = rows // CHUNK
    lines = []
    for k in range(chan):
        one = wide_norm(got3, who, batch, chan, k, 0, blocks, masks.local_out, count)
        two = wide_norm(got2, who, batch, chan, k, 8, blocks, masks.local_out, count)
        if k == 0:
            for n, value in enumerate(one + two):
                norms[n * blocks : (n + 1) * blocks, :] = value
        gain, bias = 8, 8 + 3 * blocks
        scale3 = one[1] * tabs[k, gain : gain + blocks, :]
        scales = two[1] * tabs[k, gain + blocks : gain + 2 * blocks, :]
        shift = (
            one[0] * scale3
            + two[0] * scales
            + tabs[k, bias : bias + blocks, :]
            + tabs[k, bias + blocks : bias + 2 * blocks, :]
        )
        lines.append((scale3, scales, shift))

    def step(t, _):
        mask = masks.small(t)
        for k in range(chan):
            scale3, scales, shift = lines[k]
            for q in range(blocks):
                lanes = slice(q * LANES, (q + 1) * LANES)
                pre = (
                    cube(near3[k][at(t, CHUNK), lanes]) * scale3[q : q + 1]
                    + cube(nears[k][at(t, CHUNK), lanes]) * scales[q : q + 1]
                    + shift[q : q + 1]
                )
                value = flat(keep(mask, gelu(pre)))
                if k == 0:
                    own[at(t, CHUNK), lanes] = value
                y[at(t, CHUNK), lane_block((who[0] ^ k) * blocks + q)] = value.astype(BF)
        return 0

    lax.fori_loop(0, chunks, step, 0)
    z[...] = dot(y[...], w[...])
    total, squares = sums_of(z, chunks, slice(0, LANES))
    broadcast_rows(stats, (total, squares))
    centre_into(zc, z, chunks, slice(0, LANES), total / masks.local_out)


def spatial_kernel(batch, chan, bounds, who, got, *refs):
    near, (tabs, counts, w, a, zc, stats, norms, held, z) = refs[:chan], refs[chan:]
    masks = Masks(bounds)
    count = counts[1:2, :]
    params = [norm_of(got, who, batch, chan, k, 0, masks.local_out, count) for k in range(chan)]
    store_norms(norms, params)
    rows, width = a.shape
    chunks = rows // CHUNK
    for tap in range(3):
        held[tap, 0:CHUNK, :] = jnp.zeros((CHUNK, width), BF)
        held[tap, rows + CHUNK : rows + 2 * CHUNK, :] = jnp.zeros((CHUNK, width), BF)

    def store(t, lanes, value):
        plain = flat(value).astype(BF)
        a[at(t, CHUNK), lanes] = plain
        held[1, at(t + 1, CHUNK), lanes] = plain
        held[0, at(t + 1, CHUNK), lanes] = flat(push_right(value)).astype(BF)
        held[2, at(t + 1, CHUNK), lanes] = flat(push_left(value)).astype(BF)

    activate_into(near, params, tabs, 2, chan, who, masks, chunks, store)
    acc = None
    for i in range(3):
        for j in range(3):
            term = dot(held[j, i * CHUNK : i * CHUNK + rows, :], w[i, j])
            acc = term if acc is None else acc + term
    z[...] = acc
    total, squares = sums_of(z, chunks, slice(0, LANES), masks.small)
    broadcast_rows(stats, (total, squares))
    centre_into(zc, z, chunks, slice(0, LANES), total / masks.local_out)


def last_kernel(batch, chan, bounds, who, got, *refs):
    near, (tabs, counts, w, a, z, stats, norms) = refs[:chan], refs[chan:]
    masks = Masks(bounds)
    count = counts[1:2, :]
    params = [norm_of(got, who, batch, chan, k, 0, masks.local_out, count) for k in range(chan)]
    store_norms(norms, params)
    chunks = a.shape[0] // CHUNK

    def store(t, lanes, value):
        a[at(t, CHUNK), lanes] = flat(value).astype(BF)

    activate_into(near, params, tabs, 3, chan, who, masks, chunks, store)
    z[...] = dot(a[...], w[...])
    broadcast_rows(stats, wide_sums(z, None, chunks, masks))


def output_kernel(bounds, got, z, own, loss, tabs, counts, result, g, stats, norms):
    masks = Masks(bounds)
    count = counts[1:2, :]
    total = whole(got)
    rows, width = z.shape
    blocks = width // LANES
    chunks = rows // CHUNK
    mean = total[0:blocks] / count
    inverse = lax.rsqrt(total[blocks : 2 * blocks] / count - mean * mean + EPS)
    norms[0:blocks, :] = mean
    norms[blocks : 2 * blocks, :] = inverse
    gain = tabs[0, 8 + 2 * blocks : 8 + 3 * blocks, :]
    bias = tabs[0, 8 + 5 * blocks : 8 + 6 * blocks, :]
    order = permutation(False, True)
    small = result.shape[2]

    def step(t, carry):
        mask = masks.small(t)
        sums = []
        pieces = []
        for q in range(blocks):
            lanes = slice(q * LANES, (q + 1) * LANES)
            zhat = (cube(z[at(t, CHUNK), lanes]) - mean[q : q + 1]) * inverse[q : q + 1]
            pre = zhat * gain[q : q + 1] + bias[q : q + 1] + cube(own[at(t, CHUNK), lanes])
            pieces.append(flat(keep(mask, gelu(pre))).astype(BF))
            u = keep(mask, gelu_slope(pre)) * cube(loss[at(t, CHUNK), lanes])
            g[at(t, CHUNK), lanes] = flat(u)
            sums.append((carry[q][0] + total_of(u * zhat), carry[q][1] + total_of(u)))
        moved = dot(order, jnp.concatenate(pieces, axis=1))
        for n in range(IMAGES):
            result[n, t] = moved[n * 8 : n * 8 + small, :].astype(BF)
        return tuple(sums)

    zero = jnp.zeros((IMAGES, LANES), F32)
    sums = lax.fori_loop(0, chunks, step, ((zero, zero),) * blocks)
    broadcast_rows(stats, [row_sum(s[0]) for s in sums] + [row_sum(s[1]) for s in sums])


def share_stage(da, near, norms, tabs, gain, chan, batch, who, masks, chunks, pieces, stats):
    zero = jnp.zeros((IMAGES, LANES), F32)
    for k in range(chan):
        lanes = lane_block(who[0] ^ k)
        offset, inverse = norms[2 * k : 2 * k + 1, :], norms[2 * k + 1 : 2 * k + 2, :]
        scale, bias = tabs[k, gain : gain + 1, :], tabs[k, gain + 4 : gain + 5, :]

        def step(t, carry, k=k, lanes=lanes, offset=offset, inverse=inverse, scale=scale, bias=bias):
            share = da[at(t, CHUNK), lanes]
            zhat = (cube(near[k][at(t, CHUNK), :]) + offset) * inverse
            u = keep(masks.small(t), gelu_slope(zhat * scale + bias)) * cube(share)
            pieces[k][at(t, CHUNK), :] = share.astype(pieces[k].dtype)
            return carry[0] + total_of(u * zhat), carry[1] + total_of(u)

        first, second = lax.fori_loop(0, chunks, step, (zero, zero))
        block = jnp.concatenate(
            [row_sum(first), row_sum(second), jnp.zeros((stats.shape[1] - 2, LANES), F32)], axis=0
        )
        for n in range(batch):
            stats[n * chan + (who[0] ^ k)] = block


def own_stage(got, parts, near, norms, tabs, gain, count, masks, chunks, sums, store):
    total = whole(got)
    gg, gb = total[0:1], total[1:2]
    fill_rows(sums, (gg, gb))
    offset, inverse = norms[0:1, :], norms[1:2, :]
    scale, bias = tabs[0, gain : gain + 1, :], tabs[0, gain + 4 : gain + 5, :]
    per_cell, per_hat = gb / count, gg / count
    front = scale * inverse

    def step(t, _):
        mask = masks.small(t)
        da = cube(parts[0][at(t, CHUNK), :])
        for part in parts[1:]:
            da = da + cube(part[at(t, CHUNK), :])
        zhat = (cube(near[at(t, CHUNK), :]) + offset) * inverse
        u = gelu_slope(zhat * scale + bias) * da
        store(t, keep(mask, front * (u - (per_cell + zhat * per_hat))))
        return 0

    lax.fori_loop(0, chunks, step, 0)


def back_last_kernel(batch, chan, bounds, who, got, g, z, norms6, tabs, counts, w, *refs):
    near, (norms, dz, *pieces, stats, sums, da) = refs[:chan], refs[chan:]
    masks = Masks(bounds)
    count = counts[1:2, :]
    total = whole(got)
    rows, width = z.shape
    blocks = width // LANES
    chunks = rows // CHUNK
    gg, gb = total[0:blocks] / count, total[blocks : 2 * blocks] / count
    sums[...] = total
    mean, inverse = norms6[0:blocks, :], norms6[blocks : 2 * blocks, :]
    front = tabs[0, 8 + 2 * blocks : 8 + 3 * blocks, :] * inverse

    def step(t, _):
        mask = masks.small(t)
        for q in range(blocks):
            lanes = slice(q * LANES, (q + 1) * LANES)
            zhat = (cube(z[at(t, CHUNK), lanes]) - mean[q : q + 1]) * inverse[q : q + 1]
            value = cube(g[at(t, CHUNK), lanes]) - (gb[q : q + 1] + zhat * gg[q : q + 1])
            dz[at(t, CHUNK), lanes] = flat(keep(mask, front[q : q + 1] * value)).astype(BF)
        return 0

    lax.fori_loop(0, chunks, step, 0)
    da[...] = dot(dz[...], w[...], ((1,), (1,)))
    share_stage(da, near, norms, tabs, 3, chan, batch, who, masks, chunks, pieces, stats)


def back_spatial_kernel(batch, chan, bounds, who, got, *refs):
    parts, refs = refs[:chan], refs[chan:]
    own, norms5, tabs, counts, w = refs[:5]
    near, (norms, spread, *pieces, stats, sums, held, da) = refs[5 : 5 + chan], refs[5 + chan :]
    masks = Masks(bounds)
    rows = own.shape[0]
    chunks = rows // CHUNK
    for tap in range(3):
        held[tap, 0:CHUNK, :] = jnp.zeros((CHUNK, LANES), BF)
        held[tap, rows + CHUNK : rows + 2 * CHUNK, :] = jnp.zeros((CHUNK, LANES), BF)

    def store(t, value):
        held[1, at(t + 1, CHUNK), :] = flat(value).astype(BF)
        held[0, at(t + 1, CHUNK), :] = flat(push_left(value)).astype(BF)
        held[2, at(t + 1, CHUNK), :] = flat(push_right(value)).astype(BF)

    own_stage(got, parts, own, norms5, tabs, 3, counts[1:2, :], masks, chunks, sums, store)
    acc = None
    for i in range(3):
        for j in range(3):
            value = held[j, (2 - i) * CHUNK : (2 - i) * CHUNK + rows, :]
            spread[:, (3 * i + j) * LANES : (3 * i + j + 1) * LANES] = value
            term = dot(value, w[i, j], ((1,), (1,)))
            acc = term if acc is None else acc + term
    da[...] = acc
    share_stage(da, near, norms, tabs, 2, chan, batch, who, masks, chunks, pieces, stats)


def back_contract_kernel(bounds, got, *refs):
    *parts, own, norms, tabs, counts, dz, sums = refs
    masks = Masks(bounds)

    def store(t, value):
        dz[at(t, CHUNK), :] = flat(value).astype(BF)

    own_stage(got, parts, own, norms, tabs, 2, counts[1:2, :], masks, own.shape[0] // CHUNK, sums, store)


def back_merge_kernel(chan, bounds, *refs):
    dz, w = refs[:chan], refs[chan : 2 * chan]
    g, near3, nears, norms, tabs, g1, stats, dy = refs[2 * chan :]
    masks = Masks(bounds)
    rows, width = g.shape
    blocks = width // LANES
    chunks = rows // CHUNK
    acc = None
    for k in range(chan):
        term = dot(dz[k][...], w[k][...], ((1,), (1,)))
        acc = term if acc is None else acc + term
    dy[...] = acc
    zero = jnp.zeros((IMAGES, LANES), F32)
    lines = [[], [], []]
    for q in range(blocks):
        lanes = slice(q * LANES, (q + 1) * LANES)
        off3, inv3, offs, invs = (norms[n * blocks + q : n * blocks + q + 1, :] for n in range(4))
        gain, bias = 8, 8 + 3 * blocks
        gain3, gains = tabs[0, gain + q : gain + q + 1, :], tabs[0, gain + blocks + q : gain + blocks + q + 1, :]
        shift = tabs[0, bias + q : bias + q + 1, :] + tabs[0, bias + blocks + q : bias + blocks + q + 1, :]

        def step(t, carry):
            zhat3 = (cube(near3[at(t, CHUNK), lanes]) + off3) * inv3
            zhats = (cube(nears[at(t, CHUNK), lanes]) + offs) * invs
            pre = zhat3 * gain3 + zhats * gains + shift
            up = cube(g[at(t, CHUNK), lanes]) + cube(dy[at(t, CHUNK), lanes])
            u = keep(masks.small(t), gelu_slope(pre)) * up
            g1[at(t, CHUNK), lanes] = flat(u)
            return (
                carry[0] + total_of(u * zhat3),
                carry[1] + total_of(u * zhats),
                carry[2] + total_of(u),
            )

        done = lax.fori_loop(0, chunks, step, (zero, zero, zero))
        for n in range(3):
            lines[n].append(row_sum(done[n]))
    broadcast_rows(stats, lines[0] + lines[1] + lines[2])


def back_enlarge_kernel(batch, chan, bounds, who, got, g1, near3, nears, norms3, tabs, counts, w, *refs):
    near, (norms, dz3, dzs, *pieces, stats, sums, da) = refs[:chan], refs[chan:]
    masks = Masks(bounds)
    count = counts[1:2, :]
    total = whole(got)
    sums[...] = total
    rows, width = g1.shape
    blocks = width // LANES
    chunks = rows // CHUNK
    total = total / count
    gg3, ggs, gb = (total[n * blocks : (n + 1) * blocks] for n in range(3))
    off3, inv3, offs, invs = (norms3[n * blocks : (n + 1) * blocks, :] for n in range(4))
    front3 = tabs[0, 8 : 8 + blocks, :] * inv3
    fronts = tabs[0, 8 + blocks : 8 + 2 * blocks, :] * invs

    def step(t, _):
        mask = masks.small(t)
        for q in range(blocks):
            lanes = slice(q * LANES, (q + 1) * LANES)
            line = slice(q, q + 1)
            u = cube(g1[at(t, CHUNK), lanes]) - gb[line]
            zhat3 = (cube(near3[at(t, CHUNK), lanes]) + off3[line]) * inv3[line]
            zhats = (cube(nears[at(t, CHUNK), lanes]) + offs[line]) * invs[line]
            dz3[at(t, CHUNK), lanes] = flat(keep(mask, front3[line] * (u - zhat3 * gg3[line]))).astype(BF)
            dzs[at(t, CHUNK), lanes] = flat(keep(mask, fronts[line] * (u - zhats * ggs[line]))).astype(BF)
        return 0

    lax.fori_loop(0, chunks, step, 0)
    da[...] = dot(dz3[...], w[...], ((1,), (1,)))
    share_stage(da, near, norms, tabs, 1, chan, batch, who, masks, chunks, pieces, stats)


def back_strided_kernel(bounds, got, *refs):
    *parts, own, norms, tabs, counts, dz, moved, sums, held = refs
    masks = Masks(bounds)
    rows = own.shape[0]
    for tap in range(2):
        held[tap, rows : rows + CHUNK, :] = jnp.zeros((CHUNK, LANES), BF)

    def store(t, value):
        plain = flat(value).astype(BF)
        dz[at(t, CHUNK), :] = plain
        held[0, at(t, CHUNK), :] = plain
        held[1, at(t, CHUNK), :] = flat(push_left(value)).astype(BF)

    own_stage(got, parts, own, norms, tabs, 1, counts[1:2, :], masks, rows // CHUNK, sums, store)
    for down in range(2):
        for right in range(2):
            n = 2 * down + right
            moved[:, n * LANES : (n + 1) * LANES] = held[right, down * CHUNK : down * CHUNK + rows, :]


TAPS = {0: ((1, 0),), 1: ((2, 0), (0, 1))}


def back_first_kernel(chan, bounds, *refs):
    dz, (w, near, norms, tabs, u_out, stats, held, da) = refs[:chan], refs[chan:]
    masks = Masks(bounds)
    rows = dz[0].shape[0]
    chunks = rows // CHUNK
    for tap in range(2):
        held[tap, rows : rows + CHUNK, :] = jnp.zeros((CHUNK, chan * LANES), BF)

    def shift(t, _):
        for k in range(chan):
            lanes = slice(k * LANES, (k + 1) * LANES)
            value = dz[k][at(t, CHUNK), :]
            held[0, at(t, CHUNK), lanes] = value
            held[1, at(t, CHUNK), lanes] = flat(push_left(cube(value))).astype(BF)
        return 0

    lax.fori_loop(0, chunks, shift, 0)
    offset, inverse = norms[0:1, :], norms[1:2, :]
    scale, bias = tabs[0, 0:1, :], tabs[0, 4:5, :]
    zero = jnp.zeros((IMAGES, LANES), F32)
    sums = (zero, zero)
    for p in range(2):
        for q in range(2):
            acc = None
            for a, down in TAPS[p]:
                for b, right in TAPS[q]:
                    term = dot(held[right, down * CHUNK : down * CHUNK + rows, :], w[a, b], ((1,), (1,)))
                    acc = term if acc is None else acc + term
            da[...] = acc

            def step(t, carry, p=p, q=q):
                r = 2 * t + p
                place = at(r * 2 + q, CHUNK)
                zhat = (cube(near[place, :]) + offset) * inverse
                u = keep(masks.large(r, q), gelu_slope(zhat * scale + bias)) * cube(da[at(t, CHUNK), :])
                u_out[place, :] = flat(u)
                return carry[0] + total_of(u * zhat), carry[1] + total_of(u)

            sums = lax.fori_loop(0, chunks, step, sums)
    broadcast_rows(stats, (row_sum(sums[0]), row_sum(sums[1])))


def back_first_own_kernel(bounds, got, u, near, norms, tabs, counts, dz, sums):
    masks = Masks(bounds)
    count = counts[0:1, :]
    total = whole(got)
    gg, gb = total[0:1], total[1:2]
    fill_rows(sums, (gg, gb))
    per_cell, per_hat = gb / count, gg / count
    offset, inverse = norms[0:1, :], norms[1:2, :]
    front = tabs[0, 0:1, :] * inverse

    def step(r, _):
        for parity in range(2):
            place = at(r * 2 + parity, CHUNK)
            zhat = (cube(near[place, :]) + offset) * inverse
            value = front * (cube(u[place, :]) - (per_cell + zhat * per_hat))
            dz[place, :] = flat(keep(masks.large(r, parity), value)).astype(BF)
        return 0

    lax.fori_loop(0, u.shape[0] // (2 * CHUNK), step, 0)


def leave_kernel(chan, bounds, *refs):
    dz, dzs = refs[:chan], refs[chan : 2 * chan]
    w, ws, out, dm, extra = refs[2 * chan :]
    masks = Masks(bounds)
    order = permutation(True, True)
    wide = dzs[0].shape[1]
    acc = None
    for k in range(chan):
        term = dot(dzs[k][...], ws[:, k * wide : (k + 1) * wide], ((1,), (1,)))
        acc = term if acc is None else acc + term
    extra[...] = acc
    side, width = out.shape[1], out.shape[3]
    part = dm.shape[0] // 4

    def product(t, _):
        total = None
        for k in range(chan):
            term = dot(dz[k][at(t, part), :], w[:, k * LANES : (k + 1) * LANES], ((1,), (1,)))
            total = term if total is None else total + term
        dm[at(t, part), :] = total
        return 0

    lax.fori_loop(0, 4, product, 0)

    def step(i, _):
        for p in range(2):
            r = 2 * i + p
            line = []
            for parity in range(2):
                mask = masks.large(r, parity)
                blocks = []
                for q in range(width // LANES):
                    lanes = slice(q * LANES, (q + 1) * LANES)
                    value = cube(dm[at(r * 2 + parity, CHUNK), lanes])
                    if p == 0 and parity == 0:
                        value = value + cube(extra[at(i, CHUNK), lanes])
                    blocks.append(flat(keep(mask, value)).astype(BF))
                line.append(jnp.concatenate(blocks, axis=1))
            moved = dot(order, jnp.concatenate(line, axis=0))
            for n in range(IMAGES):
                out[n, r] = moved[n * 16 : n * 16 + out.shape[2], :].astype(BF)
        return 0

    lax.fori_loop(0, side // 2, step, 0)


def solution(mesh):
    batch = mesh.shape["batch"]
    chan = mesh.shape["chan"]
    everyone = ("batch", "chan")
    devices = batch * chan

    def swap(v, mask, axis="chan"):
        return lax.ppermute(v, axis, [(k, k ^ mask) for k in range(mesh.shape[axis])])

    def gather(v):
        found = {0: v}
        mask = chan // 2
        while mask:
            for k in list(found):
                found[k ^ mask] = swap(found[k], mask)
            mask //= 2
        return [found[k] for k in range(chan)]

    def gather_direct(v):
        return [v] + [swap(v, k) for k in range(1, chan)]

    def deliver(pieces):
        return [pieces[0]] + [swap(pieces[k], k) for k in range(1, chan)]

    def exchange(stats):
        return lax.all_to_all(stats, everyone, 0, 0)

    def exchange_batch(stats):
        return lax.all_to_all(stats, "batch", 0, 0)

    def local(
        entry_activation,
        image_bounds,
        loss_sensitivity,
        first_contract_kernel,
        first_strided_kernel,
        first_enlarge_kernel,
        projection_kernel,
        second_contract_kernel,
        second_spatial_kernel,
        second_enlarge_kernel,
        bottleneck_gains,
        bottleneck_biases,
        wide_gain_vector,
        wide_bias_vector,
    ):
        images, side, _, quarter = entry_activation.shape
        small = side // 2
        me = lax.axis_index("chan")
        who = jnp.stack([me, lax.axis_index("batch")]).astype(jnp.int32)
        wide = first_enlarge_kernel.shape[1]
        blocks = wide // LANES
        rows, large = small * CHUNK, side * 2 * CHUNK
        depth = quarter * chan
        mid = first_contract_kernel.shape[1] * chan
        bounds = image_bounds
        piece = ((rows, LANES), BF)

        table = jnp.concatenate(
            [
                bottleneck_gains,
                bottleneck_biases,
                wide_gain_vector.reshape(-1, LANES),
                wide_bias_vector.reshape(-1, LANES),
            ]
        )
        tabs = jnp.stack(gather_direct(table))

        def received_rows(v, axis=0):
            size = v.shape[axis] // chan
            cut = [lax.dynamic_slice_in_dim(v, (me ^ k) * size, size, axis) for k in range(chan)]
            return deliver(cut)

        w4t = received_rows(second_contract_kernel)
        w2t = jnp.concatenate(received_rows(first_strided_kernel, 2), axis=3)
        w1t = jnp.concatenate(received_rows(first_contract_kernel), axis=1)
        wpt = jnp.concatenate(received_rows(projection_kernel), axis=1)

        (own,) = in_vmem(
            enter_kernel,
            [bounds, entry_activation],
            [((large, quarter), BF)],
            [((16 * images, quarter), BF)],
        )
        (loss,) = in_vmem(
            loss_kernel, [loss_sensitivity], [((rows, wide), BF)], [((8 * images, wide), F32)]
        )
        source = gather(own)
        z1, stats1 = in_vmem(
            functools.partial(first_kernel, chan),
            [bounds, who, *source, first_contract_kernel],
            [((large, LANES), BF), ((devices, 8, LANES), F32)],
            [((large, LANES), F32)],
        )
        got1 = exchange(stats1)
        near1 = gather(z1)
        even, zs, stats_s = in_vmem(
            functools.partial(shortcut_kernel, chan),
            [bounds, who, *source, projection_kernel],
            [((rows, depth), BF), ((rows, wide), BF), ((2 * blocks, LANES), F32)],
            [((rows, wide), F32)],
        )
        nears = gather(zs)
        a1, z2, stats2, norms1, counts = in_vmem(
            functools.partial(strided_kernel, batch, chan),
            [bounds, who, got1, *near1, tabs, first_strided_kernel, stats_s],
            [
                ((3, 2, rows + CHUNK, mid), BF),
                piece,
                ((devices, 16, LANES), F32),
                ((2 * chan, LANES), F32),
                ((8, LANES), F32),
            ],
            [((rows, LANES), F32)],
        )
        got2 = exchange(stats2)
        near2 = gather_direct(z2)
        a2, z3, stats3, norms2 = in_vmem(
            functools.partial(enlarge_kernel, batch, chan),
            [bounds, who, got2, *near2, tabs, counts, first_enlarge_kernel],
            [
                ((rows, mid), BF),
                ((rows, wide), BF),
                ((devices, 2 * blocks, LANES), F32),
                ((2 * chan, LANES), F32),
            ],
            [((rows, wide), F32)],
        )
        got3 = exchange(stats3)
        near3 = gather(z3)
        y1, y1_own, z4, stats4, norms3 = in_vmem(
            functools.partial(merge_kernel, batch, chan),
            [bounds, who, got3, got2, *near3, *nears, tabs, counts, second_contract_kernel],
            [
                ((rows, wide * chan), BF),
                ((rows, wide), F32),
                piece,
                ((devices, 8, LANES), F32),
                ((4 * blocks, LANES), F32),
            ],
            [((rows, LANES), F32)],
        )
        got4 = exchange(stats4)
        near4 = gather_direct(z4)
        a4, z5, stats5, norms4 = in_vmem(
            functools.partial(spatial_kernel, batch, chan),
            [bounds, who, got4, *near4, tabs, counts, second_spatial_kernel],
            [((rows, mid), BF), piece, ((devices, 8, LANES), F32), ((2 * chan, LANES), F32)],
            [((3, rows + 2 * CHUNK, mid), BF), ((rows, LANES), F32)],
        )
        got5 = exchange(stats5)
        near5 = gather_direct(z5)
        a5, z6, stats6, norms5 = in_vmem(
            functools.partial(last_kernel, batch, chan),
            [bounds, who, got5, *near5, tabs, counts, second_enlarge_kernel],
            [
                ((rows, mid), BF),
                ((rows, wide), F32),
                ((batch, 2 * blocks, LANES), F32),
                ((2 * chan, LANES), F32),
            ],
        )
        got6 = exchange_batch(stats6)
        result, g2, stats7, norms6 = in_vmem(
            output_kernel,
            [bounds, got6, z6, y1_own, loss, tabs, counts],
            [
                ((images, small, small, wide), BF),
                ((rows, wide), F32),
                ((batch, 2 * blocks, LANES), F32),
                ((2 * blocks, LANES), F32),
            ],
        )

        shares = [((rows, LANES), F32)] + [piece] * (chan - 1)
        routed = ((devices, 8, LANES), F32)
        got7 = exchange_batch(stats7)
        dz6, *sent, stats8, sums6 = in_vmem(
            functools.partial(back_last_kernel, batch, chan),
            [bounds, who, got7, g2, z6, norms6, tabs, counts, second_enlarge_kernel, *near5, norms5],
            [((rows, wide), BF), *shares, routed, ((2 * blocks, LANES), F32)],
            [((rows, mid), F32)],
        )
        got8 = exchange(stats8)
        parts = deliver(sent)
        expanding_grad = dot(a5, dz6, ((0,), (0,)))
        spread5, *sent, stats9, sums5 = in_vmem(
            functools.partial(back_spatial_kernel, batch, chan),
            [
                bounds, who, got8, *parts, near5[0], norms5, tabs, counts,
                second_spatial_kernel, *near4, norms4,
            ],
            [((rows, 9 * LANES), BF), *shares, routed, ((8, LANES), F32)],
            [((3, rows + 2 * CHUNK, LANES), BF), ((rows, mid), F32)],
        )
        got9 = exchange(stats9)
        parts = deliver(sent)
        middle_grad = dot(a4, spread5, ((0,), (0,)))
        dz4, sums4 = in_vmem(
            back_contract_kernel,
            [bounds, got9, *parts, near4[0], norms4, tabs, counts],
            [piece, ((8, LANES), F32)],
        )
        dz4_all = gather_direct(dz4)
        narrowing_grad = dot(y1, dz4, ((0,), (0,)))
        g1, stats10 = in_vmem(
            functools.partial(back_merge_kernel, chan),
            [bounds, *dz4_all, *w4t, g2, near3[0], nears[0], norms3, tabs],
            [((rows, wide), F32), ((batch, 4 * blocks, LANES), F32)],
            [((rows, wide), F32)],
        )
        got10 = exchange_batch(stats10)
        dz3, dzs, *sent, stats11, sums3 = in_vmem(
            functools.partial(back_enlarge_kernel, batch, chan),
            [
                bounds, who, got10, g1, near3[0], nears[0], norms3, tabs, counts,
                first_enlarge_kernel, *near2, norms2,
            ],
            [((rows, wide), BF), ((rows, wide), BF), *shares, routed, ((4 * blocks, LANES), F32)],
            [((rows, mid), F32)],
        )
        got11 = exchange(stats11)
        parts = deliver(sent)
        dzs_all = gather(dzs)
        widening_grad = dot(a2, dz3, ((0,), (0,)))
        shortcut_grad = dot(even, dzs, ((0,), (0,)))
        dz2, moved2, sums2 = in_vmem(
            back_strided_kernel,
            [bounds, got11, *parts, near2[0], norms2, tabs, counts],
            [piece, ((rows, 4 * LANES), BF), ((8, LANES), F32)],
            [((2, rows + CHUNK, LANES), BF)],
        )
        dz2_all = gather_direct(dz2)
        u1, stats12 = in_vmem(
            functools.partial(back_first_kernel, chan),
            [bounds, *dz2_all, w2t, near1[0], norms1, tabs],
            [((large, LANES), F32), ((batch, 8, LANES), F32)],
            [((2, rows + CHUNK, mid), BF), ((rows, LANES), F32)],
        )
        got12 = exchange_batch(stats12)
        taps = {}
        for p in range(2):
            for q in range(2):
                plane = a1[1 + q, 1, :rows] if p == 0 else a1[1 + q, 0, CHUNK:]
                for a, down in TAPS[p]:
                    for b, right in TAPS[q]:
                        n = 2 * down + right
                        taps[(a, b)] = dot(plane, moved2[:, n * LANES : (n + 1) * LANES], ((0,), (0,)))
        spatial_grad = jnp.stack([jnp.stack([taps[(a, b)] for b in range(3)]) for a in range(3)])
        dz1, sums1 = in_vmem(
            back_first_own_kernel,
            [bounds, got12, u1, near1[0], norms1, tabs, counts],
            [((large, LANES), BF), ((8, LANES), F32)],
        )
        dz1_all = gather(dz1)
        reducing_grad = jnp.concatenate([dot(v, dz1, ((0,), (0,))) for v in source], axis=0)
        order = jnp.arange(chan) ^ me
        reducing_grad = reducing_grad.reshape(chan, quarter, LANES)[order].reshape(depth, LANES)
        (inputs_grad,) = in_vmem(
            functools.partial(leave_kernel, chan),
            [bounds, *dz1_all, *dzs_all, w1t, wpt],
            [((images, side, side, quarter), BF)],
            [((large, quarter), F32), ((rows, quarter), F32)],
        )
        middle_grad = jnp.stack(
            [
                jnp.stack([middle_grad[:, (3 * a + b) * LANES : (3 * a + b + 1) * LANES] for b in range(3)])
                for a in range(3)
            ]
        )
        grads = [
            reducing_grad, spatial_grad, widening_grad, shortcut_grad, narrowing_grad, middle_grad, expanding_grad
        ]
        grads = [lax.psum(v.astype(BF), "batch").astype(F32) for v in grads]
        gains3, gains_s, shift3 = (sums3[n * blocks : (n + 1) * blocks].reshape(-1) for n in range(3))
        gains6, shift6 = sums6[:blocks].reshape(-1), sums6[blocks:].reshape(-1)
        return (
            result,
            inputs_grad,
            *grads,
            jnp.stack([sums1[0], sums2[0], sums4[0], sums5[0]]),
            jnp.stack([sums1[1], sums2[1], sums4[1], sums5[1]]),
            jnp.stack([gains3, gains_s, gains6]),
            jnp.stack([shift3, shift3, shift6]),
        )

    wide_act = P("batch", None, None, "chan")
    cols = P(None, "chan")
    taps = P(None, None, None, "chan")
    return jax.shard_map(
        local,
        mesh=mesh,
        in_specs=(wide_act, P("batch", None), wide_act, cols, taps, cols, cols, cols, taps)
        + (cols,) * 5,
        out_specs=(wide_act, wide_act, cols, taps, cols, cols, cols, taps) + (cols,) * 5,
        check_vma=False,
    )
```

```python
import functools
import math

import jax
import jax.numpy as jnp
from jax import lax
from jax.experimental import pallas as pl
from jax.experimental.pallas import tpu as pltpu
from jax.sharding import PartitionSpec as P

EPS = 1e-05
BF = jnp.bfloat16
F32 = jnp.float32
GELU_A = 0.7978845608028654
GELU_B = 0.044715
LANES = 128
MID = 512
SIDE = 14
IMAGES = 8
CELLS = 8
CHUNK = CELLS * IMAGES
LINE = SIDE * IMAGES
VMEM_LIMIT = 20 * 1024 * 1024


def dot(a, b, dims=((1,), (0,))):
    return lax.dot_general(a, b, (dims, ((), ())), preferred_element_type=F32)


def gelu(v):
    return 0.5 * v * (1.0 + jnp.tanh(GELU_A * v * (1.0 + GELU_B * v * v)))


def gelu_slope(v):
    square = v * v
    t = jnp.tanh(GELU_A * v * (1.0 + GELU_B * square))
    return 0.5 * (1.0 + t) * (1.0 + v * (1.0 - t) * (GELU_A + 3.0 * GELU_A * GELU_B * square))


class Masks:
    def __init__(self, info):
        image = lax.broadcasted_iota(jnp.int32, (IMAGES, LANES), 0)
        high = jnp.zeros((IMAGES, LANES), jnp.int32)
        low = jnp.zeros((IMAGES, LANES), jnp.int32)
        inside = jnp.int32(0)
        outside = jnp.int32(0)
        for n in range(IMAGES):
            h, w = info[2 + n], info[2 + IMAGES + n]
            high = jnp.where(image == n, h, high)
            low = jnp.where(image == n, w, low)
            inside = inside + h * w
            outside = outside + lax.shift_right_logical(h + 1, 1) * lax.shift_right_logical(w + 1, 1)
        self.high = high[None]
        self.low = low[None]
        self.column = lax.broadcasted_iota(jnp.int32, (2 * CELLS, IMAGES, LANES), 0)
        self.local_in = inside.astype(F32)
        self.local_out = outside.astype(F32)

    def large(self, row):
        return (row < self.high) & (self.column[:SIDE] < self.low)

    def small(self, row):
        return (2 * row < self.high) & (2 * self.column[:CELLS] < self.low)


def keep(mask, value):
    return jnp.where(mask, value, 0.0)


def cube(rows):
    return rows.astype(F32).reshape(-1, IMAGES, LANES)


def flat(value):
    return value.reshape(-1, LANES)


def padded(value):
    return jnp.concatenate([value, jnp.zeros((1,) + value.shape[1:], F32)], axis=0)


def parted(value):
    pairs = value.reshape(CELLS - 1, 2, *value.shape[1:])
    return padded(pairs[:, 0]), padded(pairs[:, 1])


def merged(even, odd):
    pairs = jnp.stack([even[: CELLS - 1], odd[: CELLS - 1]], axis=1)
    return pairs.reshape(SIDE, *even.shape[1:])


def total_of(value):
    return jnp.sum(value, axis=0)


def row_sum(value):
    return jnp.sum(value, axis=0, keepdims=True)


def at(step, size):
    return pl.ds(pl.multiple_of(step * size, size), size)


def lane_block(index, width=LANES):
    return pl.ds(pl.multiple_of(index * width, width), width)


def push_left(value):
    return jnp.concatenate([value[1:], jnp.zeros((1, IMAGES, LANES), F32)], axis=0)


def push_right(value):
    return jnp.concatenate([jnp.zeros((1, IMAGES, LANES), F32), value[:-1]], axis=0)


def norm_of(got, info, batch, chan, k, row, local, count):
    column = info[0] ^ k
    total = got[column]
    for n in range(1, batch):
        total = total + got[n * chan + column]
    mine = got[info[1] * chan + column]
    mean = total[row : row + 1] / count
    inverse = lax.rsqrt(total[row + 1 : row + 2] / count - mean * mean + EPS)
    return mine[row : row + 1] / local - mean, inverse


def whole(got):
    total = got[0]
    for n in range(1, got.shape[0]):
        total = total + got[n]
    return total


class Late:
    def __init__(self, source, held, semaphore):
        self.copy = pltpu.make_async_copy(source, held, semaphore)
        self.held = held
        self.waiting = True
        self.copy.start()

    def use(self):
        if self.waiting:
            self.copy.wait()
            self.waiting = False
        return self.held


class Far:
    def __init__(self, held, target, semaphore):
        self.copy = pltpu.make_async_copy(held, target, semaphore)
        self.held = held
        self.sent = False
        self.shape = held.shape
        self.dtype = held.dtype

    def __getitem__(self, place):
        return self.held[place]

    def __setitem__(self, place, value):
        self.held[place] = value

    def send(self):
        self.sent = True
        self.copy.start()


def ready(value):
    if isinstance(value, (list, tuple)):
        return [ready(v) for v in value]
    return value.use() if isinstance(value, Late) else value


class far:
    def __init__(self, value):
        self.value = value


def fars(values):
    return [far(v) for v in values]


def in_vmem(kernel, ins, outs, scratch=(), after=(), save=()):
    anywhere = pl.BlockSpec(memory_space=pl.ANY)
    inside = pl.BlockSpec(memory_space=pltpu.VMEM)
    args = [pltpu.with_memory_space_constraint(v, pltpu.HBM) for v in after]
    specs, late, buffers = [anywhere] * len(after), [], []
    for n, v in enumerate(ins):
        if isinstance(v, far):
            late.append(n)
            buffers.append(pltpu.VMEM(v.value.shape, v.value.dtype))
            args.append(pltpu.with_memory_space_constraint(v.value, pltpu.HBM))
            specs.append(anywhere)
        elif v.dtype == jnp.int32:
            args.append(v)
            specs.append(pl.BlockSpec(memory_space=pltpu.SMEM))
        else:
            args.append(pltpu.with_memory_space_constraint(v, pltpu.VMEM))
            specs.append(inside)
    distant = [n for n, out in enumerate(outs) if len(out) > 2]
    buffers += [pltpu.VMEM(*outs[n][:2]) for n in distant]
    shapes = [(pltpu.HBM if len(out) > 2 else pltpu.VMEM)(*out[:2]) for out in outs]
    shapes += [pltpu.HBM(ins[n].shape, ins[n].dtype) for n in save]
    out_specs = [anywhere if len(out) > 2 else inside for out in outs] + [anywhere] * len(save)
    semaphores = len(buffers) + len(save)

    def body(*refs):
        refs = list(refs[len(after) :])
        given, refs = refs[: len(ins)], refs[len(ins) :]
        made, refs = refs[: len(outs)], refs[len(outs) :]
        saved, refs = refs[: len(save)], refs[len(save) :]
        free, refs = refs[: len(scratch)], refs[len(scratch) :]
        held, marks = refs[: len(buffers)], refs[len(buffers) :]
        for place, n in enumerate(late):
            given[n] = Late(given[n], held[place], marks[place])
        for place, n in enumerate(distant, len(late)):
            made[n] = Far(held[place], made[n], marks[place])
        copies = [
            pltpu.make_async_copy(given[n], out, mark)
            for n, out, mark in zip(save, saved, marks[len(buffers) :])
        ]
        for copy in copies:
            copy.start()
        kernel(*given, *made, *free)
        for n in distant:
            if not made[n].sent:
                made[n].send()
        for n in late:
            given[n].use()
        for n in distant:
            made[n].copy.wait()
        for copy in copies:
            copy.wait()

    return pl.pallas_call(
        body,
        out_shape=shapes,
        in_specs=specs,
        out_specs=out_specs,
        scratch_shapes=[pltpu.VMEM(*v) for v in scratch] + buffers + [pltpu.SemaphoreType.DMA] * semaphores,
        compiler_params=pltpu.CompilerParams(vmem_limit_bytes=VMEM_LIMIT),
        cost_estimate=pl.CostEstimate(flops=4 * 10**9, bytes_accessed=0, transcendentals=0),
    )(*args)


def sums_of(z, chunks, lanes, mask=None, size=CHUNK):
    def step(t, carry):
        value = cube(z[at(t, size), lanes])
        if mask is not None:
            value = keep(mask(t), value)
        return carry[0] + total_of(value), carry[1] + total_of(value * value)

    zero = jnp.zeros((IMAGES, LANES), F32)
    total, squares = lax.fori_loop(0, chunks, step, (zero, zero))
    return row_sum(total), row_sum(squares)


def centre_into(out, z, chunks, lanes, mean, size=CHUNK):
    def step(t, _):
        out[at(t, size), lanes] = (z[at(t, size), lanes] - mean).astype(BF)
        return 0

    lax.fori_loop(0, chunks, step, 0)


def broadcast_rows(out, rows):
    block = jnp.concatenate(
        list(rows) + [jnp.zeros((out.shape[1] - len(rows), LANES), F32)]
        if len(rows) < out.shape[1]
        else list(rows),
        axis=0,
    )
    out[...] = jnp.broadcast_to(block[None], out.shape)


def fill_rows(out, rows):
    for n, row in enumerate(rows):
        out[n : n + 1, :] = row
    if len(rows) < out.shape[0]:
        out[len(rows) :, :] = jnp.zeros((out.shape[0] - len(rows), LANES), F32)


def enter_kernel(info, x, out):
    masks = Masks(info)

    def step(r, _):
        mask = masks.large(r)
        for q in range(x.shape[3] // LANES):
            lanes = slice(q * LANES, (q + 1) * LANES)
            out[at(r, LINE), lanes] = flat(keep(mask, x[r, :, :, lanes].astype(F32))).astype(BF)
        return 0

    lax.fori_loop(0, SIDE, step, 0)


def first_kernel(chan, w, info, *refs):
    source, (zc, stats, z) = refs[:chan], refs[chan:]
    masks = Masks(info)
    rows, depth = source[0].shape
    part = 2 * LINE
    w = w.use()

    def step(t, _):
        total = None
        for k in range(chan):
            term = dot(source[k][at(t, part), :], w[at(info[0] ^ k, depth), :])
            total = term if total is None else total + term
        z[at(t, part), :] = total
        return 0

    lax.fori_loop(0, rows // part, step, 0)
    total, squares = sums_of(z, SIDE, slice(0, LANES), size=LINE)
    ones = jnp.ones((1, LANES), F32)
    broadcast_rows(stats, (total, squares, ones * masks.local_in, ones * masks.local_out))
    centre_into(zc, z, SIDE, slice(0, LANES), total / masks.local_in, LINE)


def shortcut_kernel(chan, w, info, *refs):
    source, (even, zc, stats, z) = refs[:chan], refs[chan:]
    masks = Masks(info)
    rows, width = z.shape
    depth = source[0].shape[1]
    chunks = rows // CHUNK

    def step(i, _):
        for k in range(chan):
            for q in range(depth // LANES):
                lanes = slice(q * LANES, (q + 1) * LANES)
                value, _ = parted(cube(source[k][at(2 * i, LINE), lanes]))
                place = lane_block((info[0] ^ k) * (depth // LANES) + q)
                even[at(i, CHUNK), place] = flat(value).astype(BF)
        return 0

    lax.fori_loop(0, chunks, step, 0)
    even.send()
    z[...] = dot(even[...], w.use()[...])
    blocks = width // LANES
    for q in range(blocks):
        lanes = slice(q * LANES, (q + 1) * LANES)
        total, squares = sums_of(z, chunks, lanes)
        stats[q : q + 1, :] = total
        stats[blocks + q : blocks + q + 1, :] = squares
        centre_into(zc, z, chunks, lanes, total / masks.local_out)


def first_act_kernel(batch, chan, pair, info, got, *refs):
    near, (tabs, *outs, norms, counts) = refs[: len(pair)], refs[len(pair) :]
    masks = Masks(info)
    total = whole(got)
    count_in, count_out = total[2:3] / chan, total[3:4] / chan
    fill_rows(counts, (count_in, count_out))
    params = [norm_of(got, info, batch, chan, k, 0, masks.local_in, count_in) for k in pair]
    norms[0:1, :] = params[0][0]
    norms[1:2, :] = params[0][1]

    def step(r, _):
        mask = masks.large(r)
        for n, k in enumerate(pair):
            scale = params[n][1] * tabs[k, 0:1, :]
            shift = params[n][0] * scale + tabs[k, 4:5, :]
            value = keep(mask, gelu(cube(near[n][at(r, LINE), :]) * scale + shift))
            outs[n][at(r, LINE), :] = flat(value).astype(BF)
        return 0

    lax.fori_loop(0, SIDE, step, 0)


def strided_kernel(chan, w, info, *refs):
    pieces, (extra, a, zc, stats, z) = refs[:chan], refs[chan:]
    masks = Masks(info)
    width = a.shape[3]
    for tap in range(3):
        a[tap, 0, 0:CHUNK, :] = jnp.zeros((CHUNK, width), BF)

    def step(r, _):
        line = r + 1
        half, place = line & 1, lax.shift_right_logical(line, 1)
        for k in range(chan):
            lanes = lane_block(info[0] ^ k)
            even, odd = parted(cube(pieces[k][at(r, LINE), :]))
            a[0, half, at(place, CHUNK), lanes] = flat(push_right(odd)).astype(BF)
            a[1, half, at(place, CHUNK), lanes] = flat(even).astype(BF)
            a[2, half, at(place, CHUNK), lanes] = flat(odd).astype(BF)
        return 0

    lax.fori_loop(0, SIDE, step, 0)
    a.send()
    rows = z.shape[0]
    acc = None
    w = w.use()
    for i, (half, first) in enumerate(((0, 0), (1, 0), (0, CHUNK))):
        for j in range(3):
            term = dot(a[j, half, first : first + rows, :], w[i, j])
            acc = term if acc is None else acc + term
    z[...] = acc
    chunks = rows // CHUNK
    total, squares = sums_of(z, chunks, slice(0, LANES), masks.small)
    block = jnp.concatenate([total, squares, jnp.zeros((6, LANES), F32), extra[...]], axis=0)
    stats[...] = jnp.broadcast_to(block[None], stats.shape)
    centre_into(zc, z, chunks, slice(0, LANES), total / masks.local_out)


def activate_into(near, params, tabs, gain, chan, info, masks, chunks, store):
    def step(t, _):
        mask = masks.small(t)
        for k in range(chan):
            scale = params[k][1] * tabs[k, gain : gain + 1, :]
            shift = params[k][0] * scale + tabs[k, gain + 4 : gain + 5, :]
            value = keep(mask, gelu(cube(near[k][at(t, CHUNK), :]) * scale + shift))
            store(t, lane_block(info[0] ^ k), value)
        return 0

    lax.fori_loop(0, chunks, step, 0)


def store_norms(norms, params):
    for k, norm in enumerate(params):
        norms[2 * k : 2 * k + 1, :] = norm[0]
        norms[2 * k + 1 : 2 * k + 2, :] = norm[1]


def enlarge_kernel(batch, chan, w, info, got, *refs):
    near, (tabs, counts, a, zc, stats, norms, z) = refs[:chan], refs[chan:]
    masks = Masks(info)
    count = counts[1:2, :]
    params = [norm_of(got, info, batch, chan, k, 0, masks.local_out, count) for k in range(chan)]
    store_norms(norms, params)
    chunks = z.shape[0] // CHUNK

    def store(t, lanes, value):
        a[at(t, CHUNK), lanes] = flat(value).astype(BF)

    activate_into(near, params, tabs, 1, chan, info, masks, chunks, store)
    a.send()
    z[...] = dot(a[...], w.use()[...])
    rows = wide_sums(z, zc, chunks, masks)
    broadcast_rows(stats, rows)


def wide_sums(z, zc, chunks, masks):
    blocks = z.shape[1] // LANES
    totals, squares = [], []
    for q in range(blocks):
        lanes = slice(q * LANES, (q + 1) * LANES)
        total, square = sums_of(z, chunks, lanes)
        totals.append(total)
        squares.append(square)
        if zc is not None:
            centre_into(zc, z, chunks, lanes, total / masks.local_out)
    return totals + squares


def wide_norm(got, info, batch, chan, k, row, blocks, local, count):
    column = info[0] ^ k
    total = got[column]
    for n in range(1, batch):
        total = total + got[n * chan + column]
    mine = got[info[1] * chan + column]
    mean = total[row : row + blocks] / count
    inverse = lax.rsqrt(total[row + blocks : row + 2 * blocks] / count - mean * mean + EPS)
    return mine[row : row + blocks] / local - mean, inverse


def merge_act_kernel(batch, chan, pair, info, got3, got2, *refs):
    size = len(pair)
    near3, nears = refs[:size], refs[size : 2 * size]
    tabs, counts, *outs, own, norms = refs[2 * size :]
    nears, got2 = ready(nears), ready(got2)
    masks = Masks(info)
    count = counts[1:2, :]
    rows, width = near3[0].shape
    blocks = width // LANES
    lines = []
    for k in pair:
        one = wide_norm(got3, info, batch, chan, k, 0, blocks, masks.local_out, count)
        two = wide_norm(got2, info, batch, chan, k, 8, blocks, masks.local_out, count)
        if k == 0:
            for n, value in enumerate(one + two):
                norms[n * blocks : (n + 1) * blocks, :] = value
        gain, bias = 8, 8 + 3 * blocks
        scale3 = one[1] * tabs[k, gain : gain + blocks, :]
        scales = two[1] * tabs[k, gain + blocks : gain + 2 * blocks, :]
        shift = (
            one[0] * scale3
            + two[0] * scales
            + tabs[k, bias : bias + blocks, :]
            + tabs[k, bias + blocks : bias + 2 * blocks, :]
        )
        lines.append((scale3, scales, shift))

    def step(t, _):
        mask = masks.small(t)
        for n, k in enumerate(pair):
            scale3, scales, shift = lines[n]
            for q in range(blocks):
                lanes = slice(q * LANES, (q + 1) * LANES)
                pre = (
                    cube(near3[n][at(t, CHUNK), lanes]) * scale3[q : q + 1]
                    + cube(nears[n][at(t, CHUNK), lanes]) * scales[q : q + 1]
                    + shift[q : q + 1]
                )
                value = flat(keep(mask, gelu(pre)))
                if k == 0:
                    own[at(t, CHUNK), lanes] = value
                outs[n][at(t, CHUNK), lanes] = value.astype(BF)
        return 0

    lax.fori_loop(0, rows // CHUNK, step, 0)


def contract_kernel(chan, w, info, *refs):
    y, (zc, stats, z) = refs[:chan], refs[chan:]
    masks = Masks(info)
    rows, width = y[0].shape
    chunks = rows // CHUNK
    w = w.use()
    total = None
    for k in range(chan):
        term = dot(y[k][...], w[at(info[0] ^ k, width), :])
        total = term if total is None else total + term
    z[...] = total
    total, squares = sums_of(z, chunks, slice(0, LANES))
    broadcast_rows(stats, (total, squares))
    centre_into(zc, z, chunks, slice(0, LANES), total / masks.local_out)


def spatial_kernel(batch, chan, w, info, got, *refs):
    near, (tabs, counts, a, zc, stats, norms, held, z) = refs[:chan], refs[chan:]
    masks = Masks(info)
    count = counts[1:2, :]
    params = [norm_of(got, info, batch, chan, k, 0, masks.local_out, count) for k in range(chan)]
    store_norms(norms, params)
    rows, width = a.shape
    chunks = rows // CHUNK
    for tap in range(3):
        held[tap, 0:CHUNK, :] = jnp.zeros((CHUNK, width), BF)
        held[tap, rows + CHUNK : rows + 2 * CHUNK, :] = jnp.zeros((CHUNK, width), BF)

    def store(t, lanes, value):
        plain = flat(value).astype(BF)
        a[at(t, CHUNK), lanes] = plain
        held[1, at(t + 1, CHUNK), lanes] = plain
        held[0, at(t + 1, CHUNK), lanes] = flat(push_right(value)).astype(BF)
        held[2, at(t + 1, CHUNK), lanes] = flat(push_left(value)).astype(BF)

    activate_into(near, params, tabs, 2, chan, info, masks, chunks, store)
    a.send()
    acc = None
    w = w.use()
    for i in range(3):
        for j in range(3):
            term = dot(held[j, i * CHUNK : i * CHUNK + rows, :], w[i, j])
            acc = term if acc is None else acc + term
    z[...] = acc
    total, squares = sums_of(z, chunks, slice(0, LANES), masks.small)
    broadcast_rows(stats, (total, squares))
    centre_into(zc, z, chunks, slice(0, LANES), total / masks.local_out)


def last_kernel(batch, chan, w, info, got, *refs):
    near, (tabs, counts, a, z, stats, norms) = refs[:chan], refs[chan:]
    masks = Masks(info)
    count = counts[1:2, :]
    params = [norm_of(got, info, batch, chan, k, 0, masks.local_out, count) for k in range(chan)]
    store_norms(norms, params)
    chunks = a.shape[0] // CHUNK

    def store(t, lanes, value):
        a[at(t, CHUNK), lanes] = flat(value).astype(BF)

    activate_into(near, params, tabs, 3, chan, info, masks, chunks, store)
    a.send()
    z[...] = dot(a[...], w.use()[...])
    broadcast_rows(stats, wide_sums(z, None, chunks, masks))


def output_kernel(info, got, z, own, loss, tabs, counts, result, g, stats, norms):
    masks = Masks(info)
    own, loss = ready(own), ready(loss)
    count = counts[1:2, :]
    total = whole(got)
    rows, width = z.shape
    blocks = width // LANES
    chunks = rows // CHUNK
    mean = total[0:blocks] / count
    inverse = lax.rsqrt(total[blocks : 2 * blocks] / count - mean * mean + EPS)
    norms[0:blocks, :] = mean
    norms[blocks : 2 * blocks, :] = inverse
    gain = tabs[0, 8 + 2 * blocks : 8 + 3 * blocks, :]
    bias = tabs[0, 8 + 5 * blocks : 8 + 6 * blocks, :]
    small = result.shape[1]

    def step(t, carry):
        mask = masks.small(t)
        sums = []
        for q in range(blocks):
            lanes = slice(q * LANES, (q + 1) * LANES)
            zhat = (cube(z[at(t, CHUNK), lanes]) - mean[q : q + 1]) * inverse[q : q + 1]
            pre = zhat * gain[q : q + 1] + bias[q : q + 1] + cube(own[at(t, CHUNK), lanes])
            result[t, :, :, lanes] = keep(mask, gelu(pre))[:small].astype(BF)
            u = keep(mask, gelu_slope(pre)) * padded(loss[t, :, :, lanes].astype(F32))
            g[at(t, CHUNK), lanes] = flat(u)
            sums.append((carry[q][0] + total_of(u * zhat), carry[q][1] + total_of(u)))
        return tuple(sums)

    zero = jnp.zeros((IMAGES, LANES), F32)
    sums = lax.fori_loop(0, chunks, step, ((zero, zero),) * blocks)
    broadcast_rows(stats, [row_sum(s[0]) for s in sums] + [row_sum(s[1]) for s in sums])


def share_stage(da, near, norms, tabs, gain, chan, batch, info, masks, chunks, pieces, stats):
    zero = jnp.zeros((IMAGES, LANES), F32)
    for k in range(chan):
        lanes = lane_block(info[0] ^ k)
        offset, inverse = norms[2 * k : 2 * k + 1, :], norms[2 * k + 1 : 2 * k + 2, :]
        scale, bias = tabs[k, gain : gain + 1, :], tabs[k, gain + 4 : gain + 5, :]

        def step(t, carry, k=k, lanes=lanes, offset=offset, inverse=inverse, scale=scale, bias=bias):
            share = da[at(t, CHUNK), lanes]
            zhat = (cube(near[k][at(t, CHUNK), :]) + offset) * inverse
            u = keep(masks.small(t), gelu_slope(zhat * scale + bias)) * cube(share)
            pieces[k][at(t, CHUNK), :] = share.astype(pieces[k].dtype)
            return carry[0] + total_of(u * zhat), carry[1] + total_of(u)

        first, second = lax.fori_loop(0, chunks, step, (zero, zero))
        block = jnp.concatenate(
            [row_sum(first), row_sum(second), jnp.zeros((stats.shape[1] - 2, LANES), F32)], axis=0
        )
        for n in range(batch):
            stats[n * chan + (info[0] ^ k)] = block


def own_stage(got, parts, near, norms, tabs, gain, count, masks, chunks, sums, store):
    total = whole(got)
    gg, gb = total[0:1], total[1:2]
    fill_rows(sums, (gg, gb))
    offset, inverse = norms[0:1, :], norms[1:2, :]
    scale, bias = tabs[0, gain : gain + 1, :], tabs[0, gain + 4 : gain + 5, :]
    per_cell, per_hat = gb / count, gg / count
    front = scale * inverse

    def step(t, _):
        mask = masks.small(t)
        da = cube(parts[0][at(t, CHUNK), :])
        for part in parts[1:]:
            da = da + cube(part[at(t, CHUNK), :])
        zhat = (cube(near[at(t, CHUNK), :]) + offset) * inverse
        u = gelu_slope(zhat * scale + bias) * da
        store(t, keep(mask, front * (u - (per_cell + zhat * per_hat))))
        return 0

    lax.fori_loop(0, chunks, step, 0)


def back_last_kernel(batch, chan, w, info, got, g, z, norms6, tabs, counts, *refs):
    near, (norms, dz, *pieces, stats, sums, da) = refs[:chan], refs[chan:]
    masks = Masks(info)
    z = ready(z)
    count = counts[1:2, :]
    total = whole(got)
    rows, width = z.shape
    blocks = width // LANES
    chunks = rows // CHUNK
    gg, gb = total[0:blocks] / count, total[blocks : 2 * blocks] / count
    sums[...] = total
    mean, inverse = norms6[0:blocks, :], norms6[blocks : 2 * blocks, :]
    front = tabs[0, 8 + 2 * blocks : 8 + 3 * blocks, :] * inverse

    def step(t, _):
        mask = masks.small(t)
        for q in range(blocks):
            lanes = slice(q * LANES, (q + 1) * LANES)
            zhat = (cube(z[at(t, CHUNK), lanes]) - mean[q : q + 1]) * inverse[q : q + 1]
            value = cube(g[at(t, CHUNK), lanes]) - (gb[q : q + 1] + zhat * gg[q : q + 1])
            dz[at(t, CHUNK), lanes] = flat(keep(mask, front[q : q + 1] * value)).astype(BF)
        return 0

    lax.fori_loop(0, chunks, step, 0)
    dz.send()
    da[...] = dot(dz[...], w.use()[...], ((1,), (1,)))
    near = ready(near)
    share_stage(da, near, norms, tabs, 3, chan, batch, info, masks, chunks, pieces, stats)


def back_spatial_kernel(batch, chan, w, info, got, *refs):
    parts, refs = refs[:chan], refs[chan:]
    own, norms5, tabs, counts = refs[:4]
    near, (norms, spread, *pieces, stats, sums, held, da) = refs[4 : 4 + chan], refs[4 + chan :]
    masks = Masks(info)
    own = ready(own)
    rows = own.shape[0]
    chunks = rows // CHUNK
    for tap in range(3):
        held[tap, 0:CHUNK, :] = jnp.zeros((CHUNK, LANES), BF)
        held[tap, rows + CHUNK : rows + 2 * CHUNK, :] = jnp.zeros((CHUNK, LANES), BF)

    def store(t, value):
        held[1, at(t + 1, CHUNK), :] = flat(value).astype(BF)
        held[0, at(t + 1, CHUNK), :] = flat(push_left(value)).astype(BF)
        held[2, at(t + 1, CHUNK), :] = flat(push_right(value)).astype(BF)

    own_stage(got, parts, own, norms5, tabs, 3, counts[1:2, :], masks, chunks, sums, store)
    acc = None
    w = w.use()
    for i in range(3):
        for j in range(3):
            value = held[j, (2 - i) * CHUNK : (2 - i) * CHUNK + rows, :]
            spread[:, (3 * i + j) * LANES : (3 * i + j + 1) * LANES] = value
            term = dot(value, w[i, j], ((1,), (1,)))
            acc = term if acc is None else acc + term
    da[...] = acc
    near = ready(near)
    share_stage(da, near, norms, tabs, 2, chan, batch, info, masks, chunks, pieces, stats)


def back_contract_kernel(info, got, *refs):
    *parts, own, norms, tabs, counts, dz, sums, copy = refs
    own = ready(own)
    masks = Masks(info)

    def store(t, value):
        plain = flat(value).astype(BF)
        dz[at(t, CHUNK), :] = plain
        copy[at(t, CHUNK), :] = plain

    own_stage(got, parts, own, norms, tabs, 2, counts[1:2, :], masks, own.shape[0] // CHUNK, sums, store)


def back_merge_kernel(chan, info, *refs):
    dz, w = refs[:chan], refs[chan : 2 * chan]
    g, near3, nears, norms, tabs, g1, stats, dy = refs[2 * chan :]
    masks = Masks(info)
    rows, width = dy.shape
    blocks = width // LANES
    chunks = rows // CHUNK
    acc = None
    for k in range(chan):
        term = dot(dz[k][...], ready(w[k])[...], ((1,), (1,)))
        acc = term if acc is None else acc + term
    dy[...] = acc
    g, near3, nears = ready(g), ready(near3), ready(nears)
    zero = jnp.zeros((IMAGES, LANES), F32)
    lines = [[], [], []]
    for q in range(blocks):
        lanes = slice(q * LANES, (q + 1) * LANES)
        off3, inv3, offs, invs = (norms[n * blocks + q : n * blocks + q + 1, :] for n in range(4))
        gain, bias = 8, 8 + 3 * blocks
        gain3, gains = tabs[0, gain + q : gain + q + 1, :], tabs[0, gain + blocks + q : gain + blocks + q + 1, :]
        shift = tabs[0, bias + q : bias + q + 1, :] + tabs[0, bias + blocks + q : bias + blocks + q + 1, :]

        def step(t, carry):
            zhat3 = (cube(near3[at(t, CHUNK), lanes]) + off3) * inv3
            zhats = (cube(nears[at(t, CHUNK), lanes]) + offs) * invs
            pre = zhat3 * gain3 + zhats * gains + shift
            up = cube(g[at(t, CHUNK), lanes]) + cube(dy[at(t, CHUNK), lanes])
            u = keep(masks.small(t), gelu_slope(pre)) * up
            g1[at(t, CHUNK), lanes] = flat(u)
            return (
                carry[0] + total_of(u * zhat3),
                carry[1] + total_of(u * zhats),
                carry[2] + total_of(u),
            )

        done = lax.fori_loop(0, chunks, step, (zero, zero, zero))
        for n in range(3):
            lines[n].append(row_sum(done[n]))
    broadcast_rows(stats, lines[0] + lines[1] + lines[2])


def back_enlarge_kernel(batch, chan, w, info, got, g1, near3, nears, norms3, tabs, counts, *refs):
    near, (norms, dz3, dzs, *pieces, stats, sums, da) = refs[:chan], refs[chan:]
    masks = Masks(info)
    near3, nears = ready(near3), ready(nears)
    count = counts[1:2, :]
    total = whole(got)
    sums[...] = total
    rows, width = g1.shape
    blocks = width // LANES
    chunks = rows // CHUNK
    total = total / count
    gg3, ggs, gb = (total[n * blocks : (n + 1) * blocks] for n in range(3))
    off3, inv3, offs, invs = (norms3[n * blocks : (n + 1) * blocks, :] for n in range(4))
    front3 = tabs[0, 8 : 8 + blocks, :] * inv3
    fronts = tabs[0, 8 + blocks : 8 + 2 * blocks, :] * invs

    def step(t, _):
        mask = masks.small(t)
        for q in range(blocks):
            lanes = slice(q * LANES, (q + 1) * LANES)
            line = slice(q, q + 1)
            u = cube(g1[at(t, CHUNK), lanes]) - gb[line]
            zhat3 = (cube(near3[at(t, CHUNK), lanes]) + off3[line]) * inv3[line]
            zhats = (cube(nears[at(t, CHUNK), lanes]) + offs[line]) * invs[line]
            dz3[at(t, CHUNK), lanes] = flat(keep(mask, front3[line] * (u - zhat3 * gg3[line]))).astype(BF)
            dzs[at(t, CHUNK), lanes] = flat(keep(mask, fronts[line] * (u - zhats * ggs[line]))).astype(BF)
        return 0

    lax.fori_loop(0, chunks, step, 0)
    da[...] = dot(dz3[...], w.use()[...], ((1,), (1,)))
    near = ready(near)
    share_stage(da, near, norms, tabs, 1, chan, batch, info, masks, chunks, pieces, stats)


def back_strided_kernel(info, got, *refs):
    *parts, own, norms, tabs, counts, dz, moved, sums, held = refs
    masks = Masks(info)
    own = ready(own)
    rows = own.shape[0]
    for tap in range(2):
        held[tap, rows : rows + CHUNK, :] = jnp.zeros((CHUNK, LANES), BF)

    def store(t, value):
        plain = flat(value).astype(BF)
        dz[at(t, CHUNK), :] = plain
        held[0, at(t, CHUNK), :] = plain
        held[1, at(t, CHUNK), :] = flat(push_left(value)).astype(BF)

    own_stage(got, parts, own, norms, tabs, 1, counts[1:2, :], masks, rows // CHUNK, sums, store)
    for down in range(2):
        for right in range(2):
            n = 2 * down + right
            moved[:, n * LANES : (n + 1) * LANES] = held[right, down * CHUNK : down * CHUNK + rows, :]


TAPS = {0: ((1, 0),), 1: ((2, 0), (0, 1))}


def back_first_kernel(chan, info, *refs):
    dz, w = refs[:chan], refs[chan : 2 * chan]
    near, norms, tabs, u_out, stats, held, joined, da = refs[2 * chan :]
    masks = Masks(info)
    rows = dz[0].shape[0]
    chunks = rows // CHUNK
    for tap in range(2):
        held[tap, rows : rows + CHUNK, :] = jnp.zeros((CHUNK, chan * LANES), BF)
    for k in range(chan):
        joined[:, :, :, k * LANES : (k + 1) * LANES] = ready(w[k])[...]
    near = ready(near)

    def shift(t, _):
        for k in range(chan):
            lanes = slice(k * LANES, (k + 1) * LANES)
            value = dz[k][at(t, CHUNK), :]
            held[0, at(t, CHUNK), lanes] = value
            held[1, at(t, CHUNK), lanes] = flat(push_left(cube(value))).astype(BF)
        return 0

    lax.fori_loop(0, chunks, shift, 0)
    offset, inverse = norms[0:1, :], norms[1:2, :]
    scale, bias = tabs[0, 0:1, :], tabs[0, 4:5, :]
    zero = jnp.zeros((IMAGES, LANES), F32)
    sums = (zero, zero)
    for p in range(2):
        for q in range(2):
            acc = None
            for a, down in TAPS[p]:
                for b, right in TAPS[q]:
                    term = dot(
                        held[right, down * CHUNK : down * CHUNK + rows, :], joined[a, b], ((1,), (1,))
                    )
                    acc = term if acc is None else acc + term
            da[q] = acc

        def step(t, carry, p=p):
            r = 2 * t + p
            place = at(r, LINE)
            zhat = (cube(near[place, :]) + offset) * inverse
            up = merged(cube(da[0, at(t, CHUNK), :]), cube(da[1, at(t, CHUNK), :]))
            u = keep(masks.large(r), gelu_slope(zhat * scale + bias)) * up
            u_out[place, :] = flat(u)
            return carry[0] + total_of(u * zhat), carry[1] + total_of(u)

        sums = lax.fori_loop(0, chunks, step, sums)
    broadcast_rows(stats, (row_sum(sums[0]), row_sum(sums[1])))


def back_first_own_kernel(info, got, u, near, norms, tabs, counts, dz, sums, copy):
    masks = Masks(info)
    count = counts[0:1, :]
    total = whole(got)
    gg, gb = total[0:1], total[1:2]
    fill_rows(sums, (gg, gb))
    per_cell, per_hat = gb / count, gg / count
    near = ready(near)
    offset, inverse = norms[0:1, :], norms[1:2, :]
    front = tabs[0, 0:1, :] * inverse

    def step(r, _):
        place = at(r, LINE)
        zhat = (cube(near[place, :]) + offset) * inverse
        value = front * (cube(u[place, :]) - (per_cell + zhat * per_hat))
        plain = flat(keep(masks.large(r), value)).astype(BF)
        dz[place, :] = plain
        copy[place, :] = plain
        return 0

    lax.fori_loop(0, SIDE, step, 0)


def leave_kernel(chan, info, *refs):
    dz, dzs = refs[:chan], refs[chan : 2 * chan]
    w, ws = refs[2 * chan : 3 * chan], refs[3 * chan : 4 * chan]
    out, dm, extra = refs[4 * chan :]
    masks = Masks(info)
    acc = None
    for k in range(chan):
        term = dot(ready(dzs[k])[...], ready(ws[k])[...], ((1,), (1,)))
        acc = term if acc is None else acc + term
    extra[...] = acc
    width = out.shape[3]
    part = 2 * LINE
    w = ready(w)

    def product(t, _):
        total = None
        for k in range(chan):
            term = dot(dz[k][at(t, part), :], w[k][...], ((1,), (1,)))
            total = term if total is None else total + term
        dm[at(t, part), :] = total
        return 0

    lax.fori_loop(0, dm.shape[0] // part, product, 0)

    def step(i, _):
        for p in range(2):
            r = 2 * i + p
            mask = masks.large(r)
            for q in range(width // LANES):
                lanes = slice(q * LANES, (q + 1) * LANES)
                value = cube(dm[at(r, LINE), lanes])
                if p == 0:
                    more = cube(extra[at(i, CHUNK), lanes])
                    value = value + merged(more, jnp.zeros_like(more))
                out[r, :, :, lanes] = keep(mask, value).astype(BF)
        return 0

    lax.fori_loop(0, SIDE // 2, step, 0)


def radices_of(batch):
    sizes, units, unit = [], [], 1
    while unit < batch:
        size = 2 if not sizes or batch // unit == 2 else 4
        sizes.append(size)
        units.append(unit)
        unit *= size
    return sizes, units


def numbers_of(sizes, units):
    numbers = [0]
    for size, unit in reversed(list(zip(sizes, units))):
        numbers = [r + m * unit for m in range(size) for r in numbers]
    return numbers


def early_products(chan, info, ins, outs):
    outs[0][...] = dot(ins[0][...], ins[1][...], ((0,), (0,)))
    outs[1][...] = dot(ins[2][...], ins[3][...], ((0,), (0,)))


def rows_products(chan, info, ins, outs):
    *pieces, right = ins
    size = pieces[0].shape[1]
    for k, piece in enumerate(pieces):
        outs[0][at(info[0] ^ k, size), :] = dot(piece[...], right[...], ((0,), (0,)))


def wide_products(chan, info, ins, outs):
    a2, dz3, even, dzs = ins
    outs[0][...] = dot(a2[...], dz3[...], ((0,), (0,)))
    outs[1][...] = dot(even[...], dzs[...], ((0,), (0,)))


def strided_products(chan, info, ins, outs):
    a1, moved = ins
    rows = moved.shape[0]
    for p in range(2):
        for q in range(2):
            start = CHUNK if p else 0
            plane = a1[1 + q, 1 - p, start : start + rows, :]
            for a, down in TAPS[p]:
                for b, right in TAPS[q]:
                    n = 2 * down + right
                    tap = 3 * a + b
                    outs[0][:, tap * LANES : (tap + 1) * LANES] = dot(
                        plane, moved[:, n * LANES : (n + 1) * LANES], ((0,), (0,))
                    )


def cut_product(ref, number, batch):
    rows = ref.shape[0] // batch
    size = MID // batch
    for n in range(rows // size):
        for lane in range(0, ref.shape[1], LANES):
            first = number * rows + n * size
            yield ref[pl.ds(pl.multiple_of(first, size), size), lane : lane + LANES]


def place_chunk(blocks, outs, layout, number):
    blocks = list(blocks)
    for out, (taps, repeats) in zip(outs, layout):
        size = blocks[0].shape[0]
        for n in range(taps * repeats):
            for lane in range(0, out.shape[-1], LANES):
                value = blocks.pop(0).astype(F32)
                if taps > 1:
                    out[n, at(number, size), lane : lane + LANES] = value
                else:
                    first = (number * repeats + n) * size
                    out[pl.ds(pl.multiple_of(first, size), size), lane : lane + LANES] = value


def slot_kernel(batch, chan, plan, info, *refs):
    ins, outs = refs[: plan["ins"]], refs[plan["ins"] :]
    for job in plan["jobs"]:
        if job["kind"] == "pack":
            products = [outs[n] for n in job["products"]]
            job["compute"](chan, info, ready([ins[n] for n in job["ins"]]), products)
            for place, r in enumerate(job["numbers"]):
                number = info[1] ^ r
                blocks = [v for ref in products for v in cut_product(ref, number, batch)]
                for n, block in enumerate(blocks):
                    put(outs, job["targets"], place * len(blocks) + n, block.astype(BF))
        else:
            sources = [(ready(ins[n]), first) for n, first in job["sources"]]
            size = job.get("size")
            if job["kind"] == "fold":
                for n in range(size):
                    total = None
                    for ref, first in sources:
                        value = ref[first + n].astype(F32)
                        total = value if total is None else total + value
                    put(outs, job["targets"], n, total.astype(BF))
            elif job["kind"] == "join":
                for m, (ref, first) in enumerate(sources):
                    for n in range(size):
                        put(outs, job["targets"], m * size + n, ref[first + n])
            else:
                width = job["width"]
                finals = [outs[n] for n in job["finals"]]
                for (ref, first), numbers in zip(sources, job["numbers"]):
                    for place, r in enumerate(numbers):
                        start = first + place * width
                        place_chunk(
                            [ref[start + n] for n in range(width)], finals, job["layout"], info[1] ^ r
                        )


def put(outs, targets, n, block):
    for out, place, first, count in targets:
        if first <= n < first + count:
            outs[out][place + n - first] = block


def solution(mesh):
    batch = mesh.shape["batch"]
    chan = mesh.shape["chan"]
    everyone = ("batch", "chan")
    devices = batch * chan
    half = chan // 2
    pair = (0, half)

    def swap(v, mask, axis="chan"):
        return lax.ppermute(v, axis, [(k, k ^ mask) for k in range(mesh.shape[axis])])

    def widen(found):
        found = dict(found)
        mask = half // 2
        while mask:
            for k in list(found):
                found[k ^ mask] = swap(found[k], mask)
            mask //= 2
        return [found[k] for k in range(chan)]

    def gather(v):
        return widen({0: v, half: swap(v, half)})

    def gather_direct(v):
        return [v] + [swap(v, k) for k in range(1, chan)]

    def deliver(pieces):
        return [pieces[0]] + [swap(pieces[k], k) for k in range(1, chan)]

    def exchange(stats):
        return lax.all_to_all(stats, everyone, 0, 0)

    def exchange_batch(stats):
        return lax.all_to_all(stats, "batch", 0, 0)

    def cut(v, axis):
        size = v.shape[axis] // chan
        me = lax.axis_index("chan")
        return [lax.dynamic_slice_in_dim(v, (me ^ k) * size, size, axis) for k in range(chan)]

    sizes, units = radices_of(batch)
    levels = len(sizes)

    class Gradient:
        def __init__(self, compute, ins, products, layout, shapes):
            self.compute, self.ins, self.products = compute, ins, products
            self.layout, self.shapes = layout, shapes
            self.width = sum(math.prod(v) for v in products) // (MID * LANES)
            self.started = 0
            self.result = None

        def partners(self, step):
            level = step if step < levels else 2 * levels - 1 - step
            return [m * units[level] for m in range(1, sizes[level])]

    def slot(info, gradients, last):
        ins, outs, scratch, jobs = [], [], [], []
        bundles = {}
        received = [v for g in gradients if g.started for v, _ in g.got]
        size = MID // batch

        def give(array):
            for n, v in enumerate(ins):
                if v is array:
                    return n
            ins.append(array)
            return len(ins) - 1

        for g in gradients:
            job = {"targets": []}
            if not g.started:
                job.update(kind="pack", compute=g.compute, numbers=numbers_of(sizes, units))
                job["ins"] = [give(v) for v in g.ins]
                total = batch * g.width
            else:
                done = g.started - 1
                sources = [(give(g.kept), 0)] + [(give(v), first) for v, first in g.got]
                if done < levels:
                    total = g.amount
                    job.update(kind="fold", sources=sources, size=total)
                elif g.started < 2 * levels:
                    total = g.amount * len(sources)
                    job.update(kind="join", sources=sources, size=g.amount)
                    masks = [0] + g.partners(done)
                    g.numbers = [r ^ m for m in masks for r in g.numbers]
                else:
                    masks = [0] + g.partners(done)
                    job.update(kind="place", sources=sources, layout=g.layout, width=g.width)
                    job["numbers"] = [[r ^ m for r in g.numbers] for m in masks]
                    job["finals"] = g
                    jobs.append((g, job, None))
                    continue
            jobs.append((g, job, total))
        for g, job, total in jobs:
            if total is None:
                job["finals"] = list(range(len(outs), len(outs) + len(g.shapes)))
                outs += [(v, F32, "far") for v in g.shapes]
                continue
            step = g.started
            masks = g.partners(step)
            if step < levels:
                share = total // (len(masks) + 1)
                firsts = [share * m for m in range(len(masks) + 1)]
            else:
                share = total
                firsts = [0] * (len(masks) + 1)
                if step == levels:
                    g.numbers = [0]
            g.amount = share
            job["targets"].append((len(outs), 0, firsts[0], share))
            g.kept = len(outs)
            outs.append(((share, size, LANES), BF, "far"))
            g.next = []
            for mask, first in zip(masks, firsts[1:]):
                place = bundles.get(mask, 0)
                g.next.append((mask, place))
                bundles[mask] = place + share
                job["targets"].append((mask, place, first, share))
        order = sorted(bundles)
        where = {mask: len(outs) + n for n, mask in enumerate(order)}
        outs += [((bundles[mask], size, LANES), BF, "far") for mask in order]
        for g, job, total in jobs:
            if total is not None:
                job["targets"] = [job["targets"][0]] + [(where[v[0]], *v[1:]) for v in job["targets"][1:]]
            if job["kind"] == "pack":
                job["products"] = list(range(len(outs) + len(scratch), len(outs) + len(scratch) + len(g.products)))
                scratch += [(v, F32) for v in g.products]
        plan = {"ins": len(ins), "jobs": [job for _, job, _ in jobs]}
        given = [v if any(v is w for w in received) else far(v) for v in ins]
        made = in_vmem(
            functools.partial(slot_kernel, batch, chan, plan), [info, *given], outs, scratch, after=[last]
        )
        moved = {mask: swap(made[where[mask]], mask, "batch") for mask in order}
        for g, job, total in jobs:
            if total is None:
                g.result = [made[n] for n in job["finals"]]
            else:
                g.kept = made[g.kept]
                g.got = [(moved[mask], place) for mask, place in g.next]
                g.started += 1
        return made[0]

    def local(
        entry_activation,
        image_bounds,
        loss_sensitivity,
        first_contract_kernel,
        first_strided_kernel,
        first_enlarge_kernel,
        projection_kernel,
        second_contract_kernel,
        second_spatial_kernel,
        second_enlarge_kernel,
        bottleneck_gains,
        bottleneck_biases,
        wide_gain_vector,
        wide_bias_vector,
    ):
        images, side, _, quarter = entry_activation.shape
        small = side // 2
        wide = first_enlarge_kernel.shape[1]
        blocks = wide // LANES
        rows, large = small * CHUNK, side * LINE
        depth = quarter * chan
        mid = first_contract_kernel.shape[1] * chan
        assert mid == MID and images == IMAGES and side == SIDE
        piece, full, line = ((rows, LANES), BF), ((rows, wide), BF), ((large, LANES), BF)
        f32s = lambda *shape: (shape, F32)

        info = jnp.concatenate(
            [lax.axis_index("chan")[None], lax.axis_index("batch")[None], image_bounds.T.reshape(-1)]
        ).astype(jnp.int32)
        (own,) = in_vmem(
            enter_kernel, [info, entry_activation.transpose(1, 2, 0, 3)], [((large, quarter), BF)]
        )
        source = gather(own)
        table = jnp.concatenate(
            [
                bottleneck_gains,
                bottleneck_biases,
                wide_gain_vector.reshape(-1, LANES),
                wide_bias_vector.reshape(-1, LANES),
            ]
        )
        tabs = jnp.stack(gather_direct(table))
        loss = loss_sensitivity.transpose(1, 2, 0, 3)

        z1, stats1 = in_vmem(
            functools.partial(first_kernel, chan),
            [far(first_contract_kernel), info, *source],
            [line, f32s(devices, 8, LANES)],
            [f32s(large, LANES)],
        )
        got1 = exchange(stats1)
        z1_far = swap(z1, pair[1])
        even, zs, stats_s, *source_far = in_vmem(
            functools.partial(shortcut_kernel, chan),
            [far(projection_kernel), info, *source],
            [((rows, depth), BF, "far"), (*full, "far"), f32s(2 * blocks, LANES)],
            [f32s(rows, wide)],
            save=range(2, 2 + chan),
        )
        zs_far = swap(zs, pair[1])
        *acts, norms1, counts, z1 = in_vmem(
            functools.partial(first_act_kernel, batch, chan, pair),
            [info, got1, z1, z1_far, tabs],
            [line, line, f32s(8, LANES), f32s(8, LANES)],
            after=[zs],
            save=[2],
        )
        acts = widen(dict(zip(pair, acts)))
        a1, z2, stats2 = in_vmem(
            functools.partial(strided_kernel, chan),
            [far(first_strided_kernel), info, *acts, stats_s],
            [((3, 2, rows + CHUNK, mid), BF, "far"), piece, f32s(devices, 16, LANES)],
            [f32s(rows, LANES)],
        )
        got2 = exchange(stats2)
        near2 = gather_direct(z2)
        a2, z3, stats3, norms2, got2, *near2 = in_vmem(
            functools.partial(enlarge_kernel, batch, chan),
            [far(first_enlarge_kernel), info, got2, *near2, tabs, counts],
            [((rows, mid), BF, "far"), full, f32s(devices, 2 * blocks, LANES), f32s(2 * chan, LANES)],
            [f32s(rows, wide)],
            save=range(2, 3 + chan),
        )
        got3 = exchange(stats3)
        z3_far = swap(z3, pair[1])
        *y1, y1_own, norms3, z3 = in_vmem(
            functools.partial(merge_act_kernel, batch, chan, pair),
            [info, got3, far(got2), z3, z3_far, far(zs), far(zs_far), tabs, counts],
            [full, full, ((rows, wide), F32, "far"), f32s(4 * blocks, LANES)],
            save=[3],
        )
        y1 = widen(dict(zip(pair, y1)))
        z4, stats4, *y1 = in_vmem(
            functools.partial(contract_kernel, chan),
            [far(second_contract_kernel), info, *y1],
            [piece, f32s(devices, 8, LANES)],
            [f32s(rows, LANES)],
            save=range(2, 2 + chan),
        )

        got4 = exchange(stats4)
        near4 = gather_direct(z4)
        a4, z5, stats5, norms4, *near4 = in_vmem(
            functools.partial(spatial_kernel, batch, chan),
            [far(second_spatial_kernel), info, got4, *near4, tabs, counts],
            [((rows, mid), BF, "far"), piece, f32s(devices, 8, LANES), f32s(2 * chan, LANES)],
            [((3, rows + 2 * CHUNK, mid), BF), f32s(rows, LANES)],
            save=range(3, 3 + chan),
        )
        got5 = exchange(stats5)
        near5 = gather_direct(z5)
        a5, z6, stats6, norms5, *near5 = in_vmem(
            functools.partial(last_kernel, batch, chan),
            [far(second_enlarge_kernel), info, got5, *near5, tabs, counts],
            [
                ((rows, mid), BF, "far"),
                f32s(rows, wide),
                f32s(batch, 2 * blocks, LANES),
                f32s(2 * chan, LANES),
            ],
            save=range(3, 3 + chan),
        )
        got6 = exchange_batch(stats6)
        w1t = deliver(cut(first_contract_kernel, 0))
        w2t = deliver(cut(first_strided_kernel, 2))
        wpt = deliver(cut(projection_kernel, 0))
        w4t = deliver(cut(second_contract_kernel, 0))
        result, g2, stats7, norms6, z6 = in_vmem(
            output_kernel,
            [info, got6, z6, far(y1_own), far(loss), tabs, counts],
            [
                ((small, small, images, wide), BF, "far"),
                f32s(rows, wide),
                f32s(batch, 2 * blocks, LANES),
                f32s(2 * blocks, LANES),
            ],
            save=[2],
        )

        shares = [f32s(rows, LANES)] + [piece] * (chan - 1)
        routed = f32s(devices, 8, LANES)
        tap_lanes = 9 * LANES
        got7 = exchange_batch(stats7)
        dz6, *sent, stats8, sums6, g2 = in_vmem(
            functools.partial(back_last_kernel, batch, chan),
            [far(second_enlarge_kernel), info, got7, g2, far(z6), norms6, tabs, counts, *fars(near5), norms5],
            [(*full, "far"), *shares, routed, f32s(2 * blocks, LANES)],
            [f32s(rows, mid)],
            after=[*w2t, *w1t, *w4t],
            save=[3],
        )
        got8 = exchange(stats8)
        parts = deliver(sent)
        spread5, *sent, stats9, sums5 = in_vmem(
            functools.partial(back_spatial_kernel, batch, chan),
            [
                far(second_spatial_kernel), info, got8, *parts, far(near5[0]), norms5, tabs, counts,
                *fars(near4), norms4,
            ],
            [((rows, tap_lanes), BF, "far"), *shares, routed, f32s(8, LANES)],
            [((3, rows + 2 * CHUNK, LANES), BF), f32s(rows, mid)],
            after=[*wpt],
        )
        got9 = exchange(stats9)
        parts = deliver(sent)
        early = Gradient(
            early_products,
            [a5, dz6, a4, spread5],
            [(mid, wide), (mid, tap_lanes)],
            ((1, 1), (9, 1)),
            [(mid, wide), (9, mid, LANES)],
        )
        last = slot(info, [early], sums5)
        dz4, sums4, dz4_far = in_vmem(
            back_contract_kernel,
            [info, got9, *parts, far(near4[0]), norms4, tabs, counts],
            [piece, f32s(8, LANES), (*piece, "far")],
            after=[last],
        )
        dz4_all = gather_direct(dz4)
        narrowing = Gradient(
            rows_products, [*y1, dz4_far], [(wide * chan, LANES)], ((1, 4),), [(wide * chan, LANES)]
        )
        last = slot(info, [narrowing], sums4)
        g1, stats10 = in_vmem(
            functools.partial(back_merge_kernel, chan),
            [info, *dz4_all, *fars(w4t), far(g2), far(z3), far(zs), norms3, tabs],
            [f32s(rows, wide), f32s(batch, 4 * blocks, LANES)],
            [f32s(rows, wide)],
            after=[last],
        )
        got10 = exchange_batch(stats10)
        last = slot(info, [early, narrowing], dz4_far)
        dz3, dzs, *sent, stats11, sums3 = in_vmem(
            functools.partial(back_enlarge_kernel, batch, chan),
            [
                far(first_enlarge_kernel), info, got10, g1, far(z3), far(zs), norms3, tabs, counts,
                *fars(near2), norms2,
            ],
            [(*full, "far"), (*full, "far"), *shares, routed, f32s(4 * blocks, LANES)],
            [f32s(rows, mid)],
            after=[last],
        )
        got11 = exchange(stats11)
        parts = deliver(sent)
        widening = Gradient(
            wide_products,
            [a2, dz3, even, dzs],
            [(mid, wide), (depth, wide)],
            ((1, 1), (1, 2)),
            [(mid, wide), (depth, wide)],
        )
        last = slot(info, [widening, early, narrowing], dz3)
        dz2, moved2, sums2 = in_vmem(
            back_strided_kernel,
            [info, got11, *parts, far(near2[0]), norms2, tabs, counts],
            [piece, ((rows, 4 * LANES), BF, "far"), f32s(8, LANES)],
            [((2, rows + CHUNK, LANES), BF)],
            after=[last],
        )
        dz2_all = gather_direct(dz2)
        last = slot(info, [widening, early, narrowing], moved2)
        u1, stats12 = in_vmem(
            functools.partial(back_first_kernel, chan),
            [info, *dz2_all, *fars(w2t), far(z1), norms1, tabs],
            [f32s(large, LANES), f32s(batch, 8, LANES)],
            [((2, rows + CHUNK, mid), BF), ((3, 3, LANES, mid), BF), f32s(2, rows, LANES)],
            after=[last],
        )
        got12 = exchange_batch(stats12)
        strided = Gradient(
            strided_products, [a1, moved2], [(mid, tap_lanes)], ((9, 1),), [(9, mid, LANES)]
        )
        last = slot(info, [strided, widening], moved2)
        dz1, sums1, dz1_far = in_vmem(
            back_first_own_kernel,
            [info, got12, u1, far(z1), norms1, tabs, counts],
            [line, f32s(8, LANES), (*line, "far")],
            after=[last],
        )
        dz1_all = gather(dz1)
        dzs_all = gather(dzs)
        reducing = Gradient(
            rows_products, [*source_far, dz1_far], [(depth, LANES)], ((1, 2),), [(depth, LANES)]
        )
        last = slot(info, [reducing, strided, widening], dz1_far)
        (inputs_grad,) = in_vmem(
            functools.partial(leave_kernel, chan),
            [info, *dz1_all, *fars(dzs_all), *fars(w1t), *fars(wpt)],
            [((side, side, images, quarter), BF, "far")],
            [f32s(large, quarter), f32s(rows, quarter)],
            after=[last],
        )
        last = slot(info, [strided, reducing, early, narrowing], inputs_grad)
        everything = [strided, widening, reducing, early, narrowing]
        while any(g.result is None for g in everything):
            last = slot(info, [g for g in everything if g.result is None], last)
        (expanding_grad, middle_grad), (narrowing_grad,) = early.result, narrowing.result
        (widening_grad, shortcut_grad), (spatial_grad,), (reducing_grad,) = (
            g.result for g in (widening, strided, reducing)
        )
        tapped = (3, 3, mid, LANES)
        gains3, gains_s, shift3 = (sums3[n * blocks : (n + 1) * blocks].reshape(-1) for n in range(3))
        gains6, shift6 = sums6[:blocks].reshape(-1), sums6[blocks:].reshape(-1)
        return (
            result.transpose(2, 0, 1, 3),
            inputs_grad.transpose(2, 0, 1, 3),
            reducing_grad,
            spatial_grad.reshape(tapped),
            widening_grad,
            shortcut_grad,
            narrowing_grad,
            middle_grad.reshape(tapped),
            expanding_grad,
            jnp.stack([sums1[0], sums2[0], sums4[0], sums5[0]]),
            jnp.stack([sums1[1], sums2[1], sums4[1], sums5[1]]),
            jnp.stack([gains3, gains_s, gains6]),
            jnp.stack([shift3, shift3, shift6]),
        )

    wide_act = P("batch", None, None, "chan")
    cols = P(None, "chan")
    taps = P(None, None, None, "chan")
    return jax.shard_map(
        local,
        mesh=mesh,
        in_specs=(wide_act, P("batch", None), wide_act, cols, taps, cols, cols, cols, taps)
        + (cols,) * 5,
        out_specs=(wide_act, wide_act, cols, taps, cols, cols, cols, taps) + (cols,) * 5,
        check_vma=False,
    )
```

```python
import functools
import math

import jax
import jax.numpy as jnp
from jax import lax
from jax.experimental import pallas as pl
from jax.experimental.pallas import tpu as pltpu
from jax.sharding import PartitionSpec as P

EPS = 1e-05
BF = jnp.bfloat16
F32 = jnp.float32
GELU_A = 0.7978845608028654
GELU_B = 0.044715
LANES = 128
MID = 512
SIDE = 14
IMAGES = 8
CELLS = 8
CHUNK = CELLS * IMAGES
LINE = SIDE * IMAGES
SLOT_COST = 10**6
VMEM_LIMIT = 20 * 1024 * 1024


def dot(a, b, dims=((1,), (0,))):
    return lax.dot_general(a, b, (dims, ((), ())), preferred_element_type=F32)


def gelu(v):
    return 0.5 * v * (1.0 + jnp.tanh(GELU_A * v * (1.0 + GELU_B * v * v)))


def gelu_slope(v):
    square = v * v
    t = jnp.tanh(GELU_A * v * (1.0 + GELU_B * square))
    return 0.5 * (1.0 + t) * (1.0 + v * (1.0 - t) * (GELU_A + 3.0 * GELU_A * GELU_B * square))


class Masks:
    def __init__(self, info):
        image = lax.broadcasted_iota(jnp.int32, (IMAGES, LANES), 0)
        high = jnp.zeros((IMAGES, LANES), jnp.int32)
        low = jnp.zeros((IMAGES, LANES), jnp.int32)
        inside = jnp.int32(0)
        outside = jnp.int32(0)
        for n in range(IMAGES):
            h, w = info[2 + n], info[2 + IMAGES + n]
            high = jnp.where(image == n, h, high)
            low = jnp.where(image == n, w, low)
            inside = inside + h * w
            outside = outside + lax.shift_right_logical(h + 1, 1) * lax.shift_right_logical(w + 1, 1)
        self.high = high[None]
        self.low = low[None]
        self.column = lax.broadcasted_iota(jnp.int32, (2 * CELLS, IMAGES, LANES), 0)
        self.local_in = inside.astype(F32)
        self.local_out = outside.astype(F32)

    def large(self, row):
        return (row < self.high) & (self.column[:SIDE] < self.low)

    def small(self, row):
        return (2 * row < self.high) & (2 * self.column[:CELLS] < self.low)


def repeat(count, step, init):
    return lax.fori_loop(0, count, step, init, unroll=count if count <= 7 else 2)


def keep(mask, value):
    return jnp.where(mask, value, 0.0)


def cube(rows):
    return rows.astype(F32).reshape(-1, IMAGES, LANES)


def flat(value):
    return value.reshape(-1, LANES)


def padded(value):
    return jnp.concatenate([value, jnp.zeros((1,) + value.shape[1:], F32)], axis=0)


def parted(value):
    pairs = value.reshape(CELLS - 1, 2, *value.shape[1:])
    return padded(pairs[:, 0]), padded(pairs[:, 1])


def merged(even, odd):
    pairs = jnp.stack([even[: CELLS - 1], odd[: CELLS - 1]], axis=1)
    return pairs.reshape(SIDE, *even.shape[1:])


def total_of(value):
    return jnp.sum(value, axis=0)


def row_sum(value):
    return jnp.sum(value, axis=0, keepdims=True)


def at(step, size):
    return pl.ds(pl.multiple_of(step * size, size), size)


def lane_block(index, width=LANES):
    return pl.ds(pl.multiple_of(index * width, width), width)


def push_left(value):
    return jnp.concatenate([value[1:], jnp.zeros((1, IMAGES, LANES), F32)], axis=0)


def push_right(value):
    return jnp.concatenate([jnp.zeros((1, IMAGES, LANES), F32), value[:-1]], axis=0)


def norm_of(got, info, batch, chan, k, row, local, count):
    column = info[0] ^ k
    total = got[column]
    for n in range(1, batch):
        total = total + got[n * chan + column]
    mine = got[info[1] * chan + column]
    mean = total[row : row + 1] / count
    inverse = lax.rsqrt(total[row + 1 : row + 2] / count - mean * mean + EPS)
    return mine[row : row + 1] / local - mean, inverse


def whole(got):
    total = got[0]
    for n in range(1, got.shape[0]):
        total = total + got[n]
    return total


class Late:
    def __init__(self, source, held, semaphore):
        self.copy = pltpu.make_async_copy(source, held, semaphore)
        self.held = held
        self.waiting = True
        self.copy.start()

    def use(self):
        if self.waiting:
            self.copy.wait()
            self.waiting = False
        return self.held


class Far:
    def __init__(self, held, target, semaphore):
        self.copy = pltpu.make_async_copy(held, target, semaphore)
        self.held = held
        self.sent = False
        self.shape = held.shape
        self.dtype = held.dtype

    def __getitem__(self, place):
        return self.held[place]

    def __setitem__(self, place, value):
        self.held[place] = value

    def send(self):
        self.sent = True
        self.copy.start()


def ready(value):
    if isinstance(value, (list, tuple)):
        return [ready(v) for v in value]
    return value.use() if isinstance(value, Late) else value


class far:
    def __init__(self, value):
        self.value = value


def fars(values):
    return [far(v) for v in values]


def in_vmem(kernel, ins, outs, scratch=(), after=(), save=(), cost=4 * 10**9):
    anywhere = pl.BlockSpec(memory_space=pl.ANY)
    inside = pl.BlockSpec(memory_space=pltpu.VMEM)
    args = [
        pltpu.with_memory_space_constraint(v.value, pltpu.HBM)
        if isinstance(v, far)
        else pltpu.with_memory_space_constraint(v, pltpu.VMEM)
        for v in after
    ]
    specs, late, buffers = [anywhere] * len(after), [], []
    for n, v in enumerate(ins):
        if isinstance(v, far):
            late.append(n)
            buffers.append(pltpu.VMEM(v.value.shape, v.value.dtype))
            args.append(pltpu.with_memory_space_constraint(v.value, pltpu.HBM))
            specs.append(anywhere)
        elif v.dtype == jnp.int32:
            args.append(v)
            specs.append(pl.BlockSpec(memory_space=pltpu.SMEM))
        else:
            args.append(pltpu.with_memory_space_constraint(v, pltpu.VMEM))
            specs.append(inside)
    distant = [n for n, out in enumerate(outs) if len(out) > 2]
    buffers += [pltpu.VMEM(*outs[n][:2]) for n in distant]
    shapes = [(pltpu.HBM if len(out) > 2 else pltpu.VMEM)(*out[:2]) for out in outs]
    shapes += [pltpu.HBM(ins[n].shape, ins[n].dtype) for n in save]
    out_specs = [anywhere if len(out) > 2 else inside for out in outs] + [anywhere] * len(save)
    semaphores = len(buffers) + len(save)

    def body(*refs):
        refs = list(refs[len(after) :])
        given, refs = refs[: len(ins)], refs[len(ins) :]
        made, refs = refs[: len(outs)], refs[len(outs) :]
        saved, refs = refs[: len(save)], refs[len(save) :]
        free, refs = refs[: len(scratch)], refs[len(scratch) :]
        held, marks = refs[: len(buffers)], refs[len(buffers) :]
        for place, n in enumerate(late):
            given[n] = Late(given[n], held[place], marks[place])
        for place, n in enumerate(distant, len(late)):
            made[n] = Far(held[place], made[n], marks[place])
        copies = [
            pltpu.make_async_copy(given[n], out, mark)
            for n, out, mark in zip(save, saved, marks[len(buffers) :])
        ]
        for copy in copies:
            copy.start()
        kernel(*given, *made, *free)
        for n in distant:
            if not made[n].sent:
                made[n].send()
        for n in late:
            given[n].use()
        for n in distant:
            made[n].copy.wait()
        for copy in copies:
            copy.wait()

    return pl.pallas_call(
        body,
        out_shape=shapes,
        in_specs=specs,
        out_specs=out_specs,
        scratch_shapes=[pltpu.VMEM(*v) for v in scratch] + buffers + [pltpu.SemaphoreType.DMA] * semaphores,
        compiler_params=pltpu.CompilerParams(vmem_limit_bytes=VMEM_LIMIT),
        cost_estimate=pl.CostEstimate(flops=cost, bytes_accessed=0, transcendentals=0),
    )(*args)


def sums_of(z, chunks, lanes, mask=None, size=CHUNK):
    def step(t, carry):
        value = cube(z[at(t, size), lanes])
        if mask is not None:
            value = keep(mask(t), value)
        return carry[0] + total_of(value), carry[1] + total_of(value * value)

    zero = jnp.zeros((IMAGES, LANES), F32)
    total, squares = repeat(chunks, step, (zero, zero))
    return row_sum(total), row_sum(squares)


def centre_into(out, z, chunks, lanes, mean, size=CHUNK):
    def step(t, _):
        out[at(t, size), lanes] = (z[at(t, size), lanes] - mean).astype(BF)
        return 0

    repeat(chunks, step, 0)


def broadcast_rows(out, rows):
    block = jnp.concatenate(
        list(rows) + [jnp.zeros((out.shape[1] - len(rows), LANES), F32)]
        if len(rows) < out.shape[1]
        else list(rows),
        axis=0,
    )
    out[...] = jnp.broadcast_to(block[None], out.shape)


def fill_rows(out, rows):
    for n, row in enumerate(rows):
        out[n : n + 1, :] = row
    if len(rows) < out.shape[0]:
        out[len(rows) :, :] = jnp.zeros((out.shape[0] - len(rows), LANES), F32)


def enter_kernel(info, x, out):
    masks = Masks(info)

    def step(r, _):
        mask = masks.large(r)
        for q in range(x.shape[3] // LANES):
            lanes = slice(q * LANES, (q + 1) * LANES)
            out[at(r, LINE), lanes] = flat(keep(mask, x[r, :, :, lanes].astype(F32))).astype(BF)
        return 0

    repeat(SIDE, step, 0)


def first_kernel(chan, w, info, *refs):
    source, (zc, stats, z) = refs[:chan], refs[chan:]
    masks = Masks(info)
    rows, depth = source[0].shape
    part = 2 * LINE
    w = w.use()

    def step(t, _):
        total = None
        for k in range(chan):
            term = dot(source[k][at(t, part), :], w[at(info[0] ^ k, depth), :])
            total = term if total is None else total + term
        z[at(t, part), :] = total
        return 0

    repeat(rows // part, step, 0)
    total, squares = sums_of(z, SIDE, slice(0, LANES), size=LINE)
    ones = jnp.ones((1, LANES), F32)
    broadcast_rows(stats, (total, squares, ones * masks.local_in, ones * masks.local_out))
    centre_into(zc, z, SIDE, slice(0, LANES), total / masks.local_in, LINE)


def shortcut_kernel(chan, w, info, *refs):
    source, (even, zc, stats, z) = refs[:chan], refs[chan:]
    masks = Masks(info)
    rows, width = z.shape
    depth = source[0].shape[1]
    chunks = rows // CHUNK

    def step(i, _):
        for k in range(chan):
            for q in range(depth // LANES):
                lanes = slice(q * LANES, (q + 1) * LANES)
                value, _ = parted(cube(source[k][at(2 * i, LINE), lanes]))
                place = lane_block((info[0] ^ k) * (depth // LANES) + q)
                even[at(i, CHUNK), place] = flat(value).astype(BF)
        return 0

    repeat(chunks, step, 0)
    even.send()
    z[...] = dot(even[...], w.use()[...])
    blocks = width // LANES
    for q in range(blocks):
        lanes = slice(q * LANES, (q + 1) * LANES)
        total, squares = sums_of(z, chunks, lanes)
        stats[q : q + 1, :] = total
        stats[blocks + q : blocks + q + 1, :] = squares
        centre_into(zc, z, chunks, lanes, total / masks.local_out)


def first_act_kernel(batch, chan, pair, info, got, *refs):
    near, (tabs, *outs, norms, counts) = refs[: len(pair)], refs[len(pair) :]
    masks = Masks(info)
    total = whole(got)
    count_in, count_out = total[2:3] / chan, total[3:4] / chan
    fill_rows(counts, (count_in, count_out))
    params = [norm_of(got, info, batch, chan, k, 0, masks.local_in, count_in) for k in pair]
    norms[0:1, :] = params[0][0]
    norms[1:2, :] = params[0][1]

    def step(r, _):
        mask = masks.large(r)
        for n, k in enumerate(pair):
            scale = params[n][1] * tabs[k, 0:1, :]
            shift = params[n][0] * scale + tabs[k, 4:5, :]
            value = keep(mask, gelu(cube(near[n][at(r, LINE), :]) * scale + shift))
            outs[n][at(r, LINE), :] = flat(value).astype(BF)
        return 0

    repeat(SIDE, step, 0)


def strided_kernel(chan, w, info, *refs):
    pieces, (extra, a, zc, stats, z) = refs[:chan], refs[chan:]
    masks = Masks(info)
    width = a.shape[3]
    for tap in range(3):
        a[tap, 0, 0:CHUNK, :] = jnp.zeros((CHUNK, width), BF)

    def step(r, _):
        line = r + 1
        half, place = line & 1, lax.shift_right_logical(line, 1)
        for k in range(chan):
            lanes = lane_block(info[0] ^ k)
            even, odd = parted(cube(pieces[k][at(r, LINE), :]))
            a[0, half, at(place, CHUNK), lanes] = flat(push_right(odd)).astype(BF)
            a[1, half, at(place, CHUNK), lanes] = flat(even).astype(BF)
            a[2, half, at(place, CHUNK), lanes] = flat(odd).astype(BF)
        return 0

    repeat(SIDE, step, 0)
    a.send()
    rows = z.shape[0]
    acc = None
    w = w.use()
    for i, (half, first) in enumerate(((0, 0), (1, 0), (0, CHUNK))):
        for j in range(3):
            term = dot(a[j, half, first : first + rows, :], w[i, j])
            acc = term if acc is None else acc + term
    z[...] = acc
    chunks = rows // CHUNK
    total, squares = sums_of(z, chunks, slice(0, LANES), masks.small)
    block = jnp.concatenate([total, squares, jnp.zeros((6, LANES), F32), extra[...]], axis=0)
    stats[...] = jnp.broadcast_to(block[None], stats.shape)
    centre_into(zc, z, chunks, slice(0, LANES), total / masks.local_out)


def activate_into(near, params, tabs, gain, chan, info, masks, chunks, store):
    def step(t, _):
        mask = masks.small(t)
        for k in range(chan):
            scale = params[k][1] * tabs[k, gain : gain + 1, :]
            shift = params[k][0] * scale + tabs[k, gain + 4 : gain + 5, :]
            value = keep(mask, gelu(cube(near[k][at(t, CHUNK), :]) * scale + shift))
            store(t, lane_block(info[0] ^ k), value)
        return 0

    repeat(chunks, step, 0)


def store_norms(norms, params):
    for k, norm in enumerate(params):
        norms[2 * k : 2 * k + 1, :] = norm[0]
        norms[2 * k + 1 : 2 * k + 2, :] = norm[1]


def enlarge_kernel(batch, chan, w, info, got, *refs):
    near, (tabs, counts, a, zc, stats, norms, z) = refs[:chan], refs[chan:]
    masks = Masks(info)
    count = counts[1:2, :]
    params = [norm_of(got, info, batch, chan, k, 0, masks.local_out, count) for k in range(chan)]
    store_norms(norms, params)
    chunks = z.shape[0] // CHUNK

    def store(t, lanes, value):
        a[at(t, CHUNK), lanes] = flat(value).astype(BF)

    activate_into(near, params, tabs, 1, chan, info, masks, chunks, store)
    a.send()
    z[...] = dot(a[...], w.use()[...])
    rows = wide_sums(z, zc, chunks, masks)
    broadcast_rows(stats, rows)


def wide_sums(z, zc, chunks, masks):
    blocks = z.shape[1] // LANES
    totals, squares = [], []
    for q in range(blocks):
        lanes = slice(q * LANES, (q + 1) * LANES)
        total, square = sums_of(z, chunks, lanes)
        totals.append(total)
        squares.append(square)
        if zc is not None:
            centre_into(zc, z, chunks, lanes, total / masks.local_out)
    return totals + squares


def wide_norm(got, info, batch, chan, k, row, blocks, local, count):
    column = info[0] ^ k
    total = got[column]
    for n in range(1, batch):
        total = total + got[n * chan + column]
    mine = got[info[1] * chan + column]
    mean = total[row : row + blocks] / count
    inverse = lax.rsqrt(total[row + blocks : row + 2 * blocks] / count - mean * mean + EPS)
    return mine[row : row + blocks] / local - mean, inverse


def merge_act_kernel(batch, chan, pair, info, got3, got2, *refs):
    size = len(pair)
    near3, nears = refs[:size], refs[size : 2 * size]
    tabs, counts, *outs, own, norms = refs[2 * size :]
    nears, got2 = ready(nears), ready(got2)
    masks = Masks(info)
    count = counts[1:2, :]
    rows, width = near3[0].shape
    blocks = width // LANES
    lines = []
    for k in pair:
        one = wide_norm(got3, info, batch, chan, k, 0, blocks, masks.local_out, count)
        two = wide_norm(got2, info, batch, chan, k, 8, blocks, masks.local_out, count)
        if k == 0:
            for n, value in enumerate(one + two):
                norms[n * blocks : (n + 1) * blocks, :] = value
        gain, bias = 8, 8 + 3 * blocks
        scale3 = one[1] * tabs[k, gain : gain + blocks, :]
        scales = two[1] * tabs[k, gain + blocks : gain + 2 * blocks, :]
        shift = (
            one[0] * scale3
            + two[0] * scales
            + tabs[k, bias : bias + blocks, :]
            + tabs[k, bias + blocks : bias + 2 * blocks, :]
        )
        lines.append((scale3, scales, shift))

    def step(t, _):
        mask = masks.small(t)
        for n, k in enumerate(pair):
            scale3, scales, shift = lines[n]
            for q in range(blocks):
                lanes = slice(q * LANES, (q + 1) * LANES)
                pre = (
                    cube(near3[n][at(t, CHUNK), lanes]) * scale3[q : q + 1]
                    + cube(nears[n][at(t, CHUNK), lanes]) * scales[q : q + 1]
                    + shift[q : q + 1]
                )
                value = flat(keep(mask, gelu(pre)))
                if k == 0:
                    own[at(t, CHUNK), lanes] = value
                outs[n][at(t, CHUNK), lanes] = value.astype(BF)
        return 0

    repeat(rows // CHUNK, step, 0)


def contract_kernel(chan, w, info, *refs):
    y, (zc, stats, z) = refs[:chan], refs[chan:]
    masks = Masks(info)
    rows, width = y[0].shape
    chunks = rows // CHUNK
    w = w.use()
    total = None
    for k in range(chan):
        term = dot(y[k][...], w[at(info[0] ^ k, width), :])
        total = term if total is None else total + term
    z[...] = total
    total, squares = sums_of(z, chunks, slice(0, LANES))
    broadcast_rows(stats, (total, squares))
    centre_into(zc, z, chunks, slice(0, LANES), total / masks.local_out)


def spatial_kernel(batch, chan, w, info, got, *refs):
    near, (tabs, counts, a, zc, stats, norms, held, z) = refs[:chan], refs[chan:]
    masks = Masks(info)
    count = counts[1:2, :]
    params = [norm_of(got, info, batch, chan, k, 0, masks.local_out, count) for k in range(chan)]
    store_norms(norms, params)
    rows, width = a.shape
    chunks = rows // CHUNK
    for tap in range(3):
        held[tap, 0:CHUNK, :] = jnp.zeros((CHUNK, width), BF)
        held[tap, rows + CHUNK : rows + 2 * CHUNK, :] = jnp.zeros((CHUNK, width), BF)

    def store(t, lanes, value):
        plain = flat(value).astype(BF)
        a[at(t, CHUNK), lanes] = plain
        held[1, at(t + 1, CHUNK), lanes] = plain
        held[0, at(t + 1, CHUNK), lanes] = flat(push_right(value)).astype(BF)
        held[2, at(t + 1, CHUNK), lanes] = flat(push_left(value)).astype(BF)

    activate_into(near, params, tabs, 2, chan, info, masks, chunks, store)
    a.send()
    acc = None
    w = w.use()
    for i in range(3):
        for j in range(3):
            term = dot(held[j, i * CHUNK : i * CHUNK + rows, :], w[i, j])
            acc = term if acc is None else acc + term
    z[...] = acc
    total, squares = sums_of(z, chunks, slice(0, LANES), masks.small)
    broadcast_rows(stats, (total, squares))
    centre_into(zc, z, chunks, slice(0, LANES), total / masks.local_out)


def last_kernel(batch, chan, w, info, got, *refs):
    near, (tabs, counts, a, z, stats, norms) = refs[:chan], refs[chan:]
    masks = Masks(info)
    count = counts[1:2, :]
    params = [norm_of(got, info, batch, chan, k, 0, masks.local_out, count) for k in range(chan)]
    store_norms(norms, params)
    chunks = a.shape[0] // CHUNK

    def store(t, lanes, value):
        a[at(t, CHUNK), lanes] = flat(value).astype(BF)

    activate_into(near, params, tabs, 3, chan, info, masks, chunks, store)
    a.send()
    z[...] = dot(a[...], w.use()[...])
    broadcast_rows(stats, wide_sums(z, None, chunks, masks))


def output_kernel(info, got, z, own, loss, tabs, counts, result, g, stats, norms):
    masks = Masks(info)
    own, loss = ready(own), ready(loss)
    count = counts[1:2, :]
    total = whole(got)
    rows, width = z.shape
    blocks = width // LANES
    chunks = rows // CHUNK
    mean = total[0:blocks] / count
    inverse = lax.rsqrt(total[blocks : 2 * blocks] / count - mean * mean + EPS)
    norms[0:blocks, :] = mean
    norms[blocks : 2 * blocks, :] = inverse
    gain = tabs[0, 8 + 2 * blocks : 8 + 3 * blocks, :]
    bias = tabs[0, 8 + 5 * blocks : 8 + 6 * blocks, :]
    small = result.shape[1]

    def step(t, carry):
        mask = masks.small(t)
        sums = []
        for q in range(blocks):
            lanes = slice(q * LANES, (q + 1) * LANES)
            zhat = (cube(z[at(t, CHUNK), lanes]) - mean[q : q + 1]) * inverse[q : q + 1]
            pre = zhat * gain[q : q + 1] + bias[q : q + 1] + cube(own[at(t, CHUNK), lanes])
            result[t, :, :, lanes] = keep(mask, gelu(pre))[:small].astype(BF)
            u = keep(mask, gelu_slope(pre)) * padded(loss[t, :, :, lanes].astype(F32))
            g[at(t, CHUNK), lanes] = flat(u)
            sums.append((carry[q][0] + total_of(u * zhat), carry[q][1] + total_of(u)))
        return tuple(sums)

    zero = jnp.zeros((IMAGES, LANES), F32)
    sums = repeat(chunks, step, ((zero, zero),) * blocks)
    broadcast_rows(stats, [row_sum(s[0]) for s in sums] + [row_sum(s[1]) for s in sums])


def share_stage(da, near, norms, tabs, gain, chan, batch, info, masks, chunks, pieces, stats):
    zero = jnp.zeros((IMAGES, LANES), F32)
    for k in range(chan):
        lanes = lane_block(info[0] ^ k)
        offset, inverse = norms[2 * k : 2 * k + 1, :], norms[2 * k + 1 : 2 * k + 2, :]
        scale, bias = tabs[k, gain : gain + 1, :], tabs[k, gain + 4 : gain + 5, :]

        def step(t, carry, k=k, lanes=lanes, offset=offset, inverse=inverse, scale=scale, bias=bias):
            share = da[at(t, CHUNK), lanes]
            zhat = (cube(near[k][at(t, CHUNK), :]) + offset) * inverse
            u = keep(masks.small(t), gelu_slope(zhat * scale + bias)) * cube(share)
            pieces[k][at(t, CHUNK), :] = share.astype(pieces[k].dtype)
            return carry[0] + total_of(u * zhat), carry[1] + total_of(u)

        first, second = repeat(chunks, step, (zero, zero))
        block = jnp.concatenate(
            [row_sum(first), row_sum(second), jnp.zeros((stats.shape[1] - 2, LANES), F32)], axis=0
        )
        for n in range(batch):
            stats[n * chan + (info[0] ^ k)] = block


def own_stage(got, parts, near, norms, tabs, gain, count, masks, chunks, sums, store):
    total = whole(got)
    gg, gb = total[0:1], total[1:2]
    fill_rows(sums, (gg, gb))
    offset, inverse = norms[0:1, :], norms[1:2, :]
    scale, bias = tabs[0, gain : gain + 1, :], tabs[0, gain + 4 : gain + 5, :]
    per_cell, per_hat = gb / count, gg / count
    front = scale * inverse

    def step(t, _):
        mask = masks.small(t)
        da = cube(parts[0][at(t, CHUNK), :])
        for part in parts[1:]:
            da = da + cube(part[at(t, CHUNK), :])
        zhat = (cube(near[at(t, CHUNK), :]) + offset) * inverse
        u = gelu_slope(zhat * scale + bias) * da
        store(t, keep(mask, front * (u - (per_cell + zhat * per_hat))))
        return 0

    repeat(chunks, step, 0)


def back_last_kernel(batch, chan, w, info, got, g, z, norms6, tabs, counts, *refs):
    near, (norms, dz, *pieces, stats, sums, da) = refs[:chan], refs[chan:]
    masks = Masks(info)
    z = ready(z)
    count = counts[1:2, :]
    total = whole(got)
    rows, width = z.shape
    blocks = width // LANES
    chunks = rows // CHUNK
    gg, gb = total[0:blocks] / count, total[blocks : 2 * blocks] / count
    sums[...] = total
    mean, inverse = norms6[0:blocks, :], norms6[blocks : 2 * blocks, :]
    front = tabs[0, 8 + 2 * blocks : 8 + 3 * blocks, :] * inverse

    def step(t, _):
        mask = masks.small(t)
        for q in range(blocks):
            lanes = slice(q * LANES, (q + 1) * LANES)
            zhat = (cube(z[at(t, CHUNK), lanes]) - mean[q : q + 1]) * inverse[q : q + 1]
            value = cube(g[at(t, CHUNK), lanes]) - (gb[q : q + 1] + zhat * gg[q : q + 1])
            dz[at(t, CHUNK), lanes] = flat(keep(mask, front[q : q + 1] * value)).astype(BF)
        return 0

    repeat(chunks, step, 0)
    dz.send()
    da[...] = dot(dz[...], w.use()[...], ((1,), (1,)))
    near = ready(near)
    share_stage(da, near, norms, tabs, 3, chan, batch, info, masks, chunks, pieces, stats)


def back_spatial_kernel(batch, chan, w, info, got, *refs):
    parts, refs = refs[:chan], refs[chan:]
    own, norms5, tabs, counts = refs[:4]
    near, (norms, spread, *pieces, stats, sums, held, da) = refs[4 : 4 + chan], refs[4 + chan :]
    masks = Masks(info)
    own = ready(own)
    rows = own.shape[0]
    chunks = rows // CHUNK
    for tap in range(3):
        held[tap, 0:CHUNK, :] = jnp.zeros((CHUNK, LANES), BF)
        held[tap, rows + CHUNK : rows + 2 * CHUNK, :] = jnp.zeros((CHUNK, LANES), BF)

    def store(t, value):
        held[1, at(t + 1, CHUNK), :] = flat(value).astype(BF)
        held[0, at(t + 1, CHUNK), :] = flat(push_left(value)).astype(BF)
        held[2, at(t + 1, CHUNK), :] = flat(push_right(value)).astype(BF)

    own_stage(got, parts, own, norms5, tabs, 3, counts[1:2, :], masks, chunks, sums, store)
    acc = None
    w = w.use()
    for i in range(3):
        for j in range(3):
            value = held[j, (2 - i) * CHUNK : (2 - i) * CHUNK + rows, :]
            spread[:, (3 * i + j) * LANES : (3 * i + j + 1) * LANES] = value
            term = dot(value, w[i, j], ((1,), (1,)))
            acc = term if acc is None else acc + term
    da[...] = acc
    spread.send()
    near = ready(near)
    share_stage(da, near, norms, tabs, 2, chan, batch, info, masks, chunks, pieces, stats)


def back_contract_kernel(info, got, *refs):
    *parts, own, norms, tabs, counts, dz, sums, copy = refs
    own = ready(own)
    masks = Masks(info)

    def store(t, value):
        plain = flat(value).astype(BF)
        dz[at(t, CHUNK), :] = plain
        copy[at(t, CHUNK), :] = plain

    own_stage(got, parts, own, norms, tabs, 2, counts[1:2, :], masks, own.shape[0] // CHUNK, sums, store)


def back_merge_kernel(chan, info, *refs):
    dz, w = refs[:chan], refs[chan : 2 * chan]
    g, near3, nears, norms, tabs, g1, stats, dy = refs[2 * chan :]
    masks = Masks(info)
    rows, width = dy.shape
    blocks = width // LANES
    chunks = rows // CHUNK
    acc = None
    for k in range(chan):
        term = dot(dz[k][...], ready(w[k])[...], ((1,), (1,)))
        acc = term if acc is None else acc + term
    dy[...] = acc
    g, near3, nears = ready(g), ready(near3), ready(nears)
    zero = jnp.zeros((IMAGES, LANES), F32)
    lines = [[], [], []]
    for q in range(blocks):
        lanes = slice(q * LANES, (q + 1) * LANES)
        off3, inv3, offs, invs = (norms[n * blocks + q : n * blocks + q + 1, :] for n in range(4))
        gain, bias = 8, 8 + 3 * blocks
        gain3, gains = tabs[0, gain + q : gain + q + 1, :], tabs[0, gain + blocks + q : gain + blocks + q + 1, :]
        shift = tabs[0, bias + q : bias + q + 1, :] + tabs[0, bias + blocks + q : bias + blocks + q + 1, :]

        def step(t, carry):
            zhat3 = (cube(near3[at(t, CHUNK), lanes]) + off3) * inv3
            zhats = (cube(nears[at(t, CHUNK), lanes]) + offs) * invs
            pre = zhat3 * gain3 + zhats * gains + shift
            up = cube(g[at(t, CHUNK), lanes]) + cube(dy[at(t, CHUNK), lanes])
            u = keep(masks.small(t), gelu_slope(pre)) * up
            g1[at(t, CHUNK), lanes] = flat(u)
            return (
                carry[0] + total_of(u * zhat3),
                carry[1] + total_of(u * zhats),
                carry[2] + total_of(u),
            )

        done = repeat(chunks, step, (zero, zero, zero))
        for n in range(3):
            lines[n].append(row_sum(done[n]))
    broadcast_rows(stats, lines[0] + lines[1] + lines[2])


def back_enlarge_kernel(batch, chan, w, info, got, g1, near3, nears, norms3, tabs, counts, *refs):
    near, (norms, dz3, dzs, *pieces, stats, sums, da) = refs[:chan], refs[chan:]
    masks = Masks(info)
    near3, nears = ready(near3), ready(nears)
    count = counts[1:2, :]
    total = whole(got)
    sums[...] = total
    rows, width = g1.shape
    blocks = width // LANES
    chunks = rows // CHUNK
    total = total / count
    gg3, ggs, gb = (total[n * blocks : (n + 1) * blocks] for n in range(3))
    off3, inv3, offs, invs = (norms3[n * blocks : (n + 1) * blocks, :] for n in range(4))
    front3 = tabs[0, 8 : 8 + blocks, :] * inv3
    fronts = tabs[0, 8 + blocks : 8 + 2 * blocks, :] * invs

    def step(t, _):
        mask = masks.small(t)
        for q in range(blocks):
            lanes = slice(q * LANES, (q + 1) * LANES)
            line = slice(q, q + 1)
            u = cube(g1[at(t, CHUNK), lanes]) - gb[line]
            zhat3 = (cube(near3[at(t, CHUNK), lanes]) + off3[line]) * inv3[line]
            zhats = (cube(nears[at(t, CHUNK), lanes]) + offs[line]) * invs[line]
            dz3[at(t, CHUNK), lanes] = flat(keep(mask, front3[line] * (u - zhat3 * gg3[line]))).astype(BF)
            dzs[at(t, CHUNK), lanes] = flat(keep(mask, fronts[line] * (u - zhats * ggs[line]))).astype(BF)
        return 0

    repeat(chunks, step, 0)
    dz3.send()
    dzs.send()
    da[...] = dot(dz3[...], w.use()[...], ((1,), (1,)))
    near = ready(near)
    share_stage(da, near, norms, tabs, 1, chan, batch, info, masks, chunks, pieces, stats)


def back_strided_kernel(info, got, *refs):
    *parts, own, norms, tabs, counts, dz, moved, sums, held = refs
    masks = Masks(info)
    own = ready(own)
    rows = own.shape[0]
    for tap in range(2):
        held[tap, rows : rows + CHUNK, :] = jnp.zeros((CHUNK, LANES), BF)

    def store(t, value):
        plain = flat(value).astype(BF)
        dz[at(t, CHUNK), :] = plain
        held[0, at(t, CHUNK), :] = plain
        held[1, at(t, CHUNK), :] = flat(push_left(value)).astype(BF)

    own_stage(got, parts, own, norms, tabs, 1, counts[1:2, :], masks, rows // CHUNK, sums, store)
    for down in range(2):
        for right in range(2):
            n = 2 * down + right
            moved[:, n * LANES : (n + 1) * LANES] = held[right, down * CHUNK : down * CHUNK + rows, :]


TAPS = {0: ((1, 0),), 1: ((2, 0), (0, 1))}


def back_first_kernel(chan, info, *refs):
    dz, w = refs[:chan], refs[chan : 2 * chan]
    near, norms, tabs, u_out, stats, held, joined, da = refs[2 * chan :]
    masks = Masks(info)
    rows = dz[0].shape[0]
    chunks = rows // CHUNK
    for tap in range(2):
        held[tap, rows : rows + CHUNK, :] = jnp.zeros((CHUNK, chan * LANES), BF)
    for k in range(chan):
        joined[:, :, :, k * LANES : (k + 1) * LANES] = ready(w[k])[...]
    near = ready(near)

    def shift(t, _):
        for k in range(chan):
            lanes = slice(k * LANES, (k + 1) * LANES)
            value = dz[k][at(t, CHUNK), :]
            held[0, at(t, CHUNK), lanes] = value
            held[1, at(t, CHUNK), lanes] = flat(push_left(cube(value))).astype(BF)
        return 0

    repeat(chunks, shift, 0)
    offset, inverse = norms[0:1, :], norms[1:2, :]
    scale, bias = tabs[0, 0:1, :], tabs[0, 4:5, :]
    zero = jnp.zeros((IMAGES, LANES), F32)
    sums = (zero, zero)
    for p in range(2):
        for q in range(2):
            acc = None
            for a, down in TAPS[p]:
                for b, right in TAPS[q]:
                    term = dot(
                        held[right, down * CHUNK : down * CHUNK + rows, :], joined[a, b], ((1,), (1,))
                    )
                    acc = term if acc is None else acc + term
            da[q] = acc

        def step(t, carry, p=p):
            r = 2 * t + p
            place = at(r, LINE)
            zhat = (cube(near[place, :]) + offset) * inverse
            up = merged(cube(da[0, at(t, CHUNK), :]), cube(da[1, at(t, CHUNK), :]))
            u = keep(masks.large(r), gelu_slope(zhat * scale + bias)) * up
            u_out[place, :] = flat(u)
            return carry[0] + total_of(u * zhat), carry[1] + total_of(u)

        sums = repeat(chunks, step, sums)
    broadcast_rows(stats, (row_sum(sums[0]), row_sum(sums[1])))


def back_first_own_kernel(info, got, u, near, norms, tabs, counts, dz, sums):
    masks = Masks(info)
    count = counts[0:1, :]
    total = whole(got)
    gg, gb = total[0:1], total[1:2]
    fill_rows(sums, (gg, gb))
    per_cell, per_hat = gb / count, gg / count
    near = ready(near)
    offset, inverse = norms[0:1, :], norms[1:2, :]
    front = tabs[0, 0:1, :] * inverse

    def step(r, _):
        place = at(r, LINE)
        zhat = (cube(near[place, :]) + offset) * inverse
        value = front * (cube(u[place, :]) - (per_cell + zhat * per_hat))
        dz[place, :] = flat(keep(masks.large(r), value)).astype(BF)
        return 0

    repeat(SIDE, step, 0)


def leave_kernel(chan, info, *refs):
    dz, dzs = refs[:chan], refs[chan : 2 * chan]
    w, ws = refs[2 * chan : 3 * chan], refs[3 * chan : 4 * chan]
    out, dm, extra = refs[4 * chan :]
    masks = Masks(info)
    acc = None
    for k in range(chan):
        term = dot(ready(dzs[k])[...], ready(ws[k])[...], ((1,), (1,)))
        acc = term if acc is None else acc + term
    extra[...] = acc
    width = out.shape[3]
    part = 2 * LINE
    w = ready(w)

    def product(t, _):
        total = None
        for k in range(chan):
            term = dot(dz[k][at(t, part), :], w[k][...], ((1,), (1,)))
            total = term if total is None else total + term
        dm[at(t, part), :] = total
        return 0

    repeat(dm.shape[0] // part, product, 0)

    def step(i, _):
        for p in range(2):
            r = 2 * i + p
            mask = masks.large(r)
            for q in range(width // LANES):
                lanes = slice(q * LANES, (q + 1) * LANES)
                value = cube(dm[at(r, LINE), lanes])
                if p == 0:
                    more = cube(extra[at(i, CHUNK), lanes])
                    value = value + merged(more, jnp.zeros_like(more))
                out[r, :, :, lanes] = keep(mask, value).astype(BF)
        return 0

    repeat(SIDE // 2, step, 0)


def radices_of(batch):
    sizes, units, unit = [], [], 1
    while unit < batch:
        size = 2 if not sizes or batch // unit == 2 else 4
        sizes.append(size)
        units.append(unit)
        unit *= size
    return sizes, units


def numbers_of(sizes, units):
    numbers = [0]
    for size, unit in reversed(list(zip(sizes, units))):
        numbers = [r + m * unit for m in range(size) for r in numbers]
    return numbers


def early_products(chan, info, ins, outs):
    outs[0][...] = dot(ins[0][...], ins[1][...], ((0,), (0,)))
    outs[1][...] = dot(ins[2][...], ins[3][...], ((0,), (0,)))


def rows_products(chan, info, ins, outs):
    *pieces, right = ins
    size = pieces[0].shape[1]
    for k, piece in enumerate(pieces):
        outs[0][at(info[0] ^ k, size), :] = dot(piece[...], right[...], ((0,), (0,)))


def wide_products(chan, info, ins, outs):
    a2, dz3, even, dzs = ins
    outs[0][...] = dot(a2[...], dz3[...], ((0,), (0,)))
    outs[1][...] = dot(even[...], dzs[...], ((0,), (0,)))


def strided_products(chan, info, ins, outs):
    a1, moved = ins
    rows = moved.shape[0]
    for p in range(2):
        for q in range(2):
            start = CHUNK if p else 0
            plane = a1[1 + q, 1 - p, start : start + rows, :]
            for a, down in TAPS[p]:
                for b, right in TAPS[q]:
                    n = 2 * down + right
                    tap = 3 * a + b
                    outs[0][:, tap * LANES : (tap + 1) * LANES] = dot(
                        plane, moved[:, n * LANES : (n + 1) * LANES], ((0,), (0,))
                    )


def cut_product(ref, number, batch):
    rows = ref.shape[0] // batch
    size = MID // batch
    for n in range(rows // size):
        for lane in range(0, ref.shape[1], LANES):
            first = number * rows + n * size
            yield ref[pl.ds(pl.multiple_of(first, size), size), lane : lane + LANES]


def place_chunk(blocks, outs, layout, number):
    blocks = list(blocks)
    for out, (taps, repeats) in zip(outs, layout):
        size = blocks[0].shape[0]
        for n in range(taps * repeats):
            for lane in range(0, out.shape[-1], LANES):
                value = blocks.pop(0).astype(F32)
                if taps > 1:
                    out[n, at(number, size), lane : lane + LANES] = value
                else:
                    first = (number * repeats + n) * size
                    out[pl.ds(pl.multiple_of(first, size), size), lane : lane + LANES] = value


def slot_kernel(batch, chan, plan, info, *refs):
    ins, outs = refs[: plan["ins"]], refs[plan["ins"] :]
    for job in plan["jobs"]:
        if job["kind"] == "pack":
            products = [outs[n] for n in job["products"]]
            job["compute"](chan, info, ready([ins[n] for n in job["ins"]]), products)
            for place, r in enumerate(job["numbers"]):
                number = info[1] ^ r
                blocks = [v for ref in products for v in cut_product(ref, number, batch)]
                for n, block in enumerate(blocks):
                    put(outs, job["targets"], place * len(blocks) + n, block.astype(BF))
        else:
            sources = [(ready(ins[n]), first) for n, first in job["sources"]]
            size = job.get("size")
            if job["kind"] == "fold":
                for n in range(size):
                    total = None
                    for ref, first in sources:
                        value = ref[first + n].astype(F32)
                        total = value if total is None else total + value
                    put(outs, job["targets"], n, total.astype(BF))
            elif job["kind"] == "join":
                for m, (ref, first) in enumerate(sources):
                    for n in range(size):
                        put(outs, job["targets"], m * size + n, ref[first + n])
            else:
                width = job["width"]
                finals = [outs[n] for n in job["finals"]]
                for (ref, first), numbers in zip(sources, job["numbers"]):
                    for place, r in enumerate(numbers):
                        start = first + place * width
                        place_chunk(
                            [ref[start + n] for n in range(width)], finals, job["layout"], info[1] ^ r
                        )


def put(outs, targets, n, block):
    for out, place, first, count in targets:
        if first <= n < first + count:
            outs[out][place + n - first] = block


def solution(mesh):
    batch = mesh.shape["batch"]
    chan = mesh.shape["chan"]
    everyone = ("batch", "chan")
    devices = batch * chan
    half = chan // 2
    pair = (0, half)

    def swap(v, mask, axis="chan"):
        return lax.ppermute(v, axis, [(k, k ^ mask) for k in range(mesh.shape[axis])])

    def widen(found):
        found = dict(found)
        mask = half // 2
        while mask:
            for k in list(found):
                found[k ^ mask] = swap(found[k], mask)
            mask //= 2
        return [found[k] for k in range(chan)]

    def gather(v):
        return widen({0: v, half: swap(v, half)})

    def gather_direct(v):
        return [v] + [swap(v, k) for k in range(1, chan)]

    def deliver(pieces):
        return [pieces[0]] + [swap(pieces[k], k) for k in range(1, chan)]

    def exchange(stats):
        return lax.all_to_all(stats, everyone, 0, 0)

    def exchange_batch(stats):
        return lax.all_to_all(stats, "batch", 0, 0)

    def cut(v, axis):
        size = v.shape[axis] // chan
        me = lax.axis_index("chan")
        return [lax.dynamic_slice_in_dim(v, (me ^ k) * size, size, axis) for k in range(chan)]

    sizes, units = radices_of(batch)
    levels = len(sizes)

    class Gradient:
        def __init__(self, compute, ins, products, layout, shapes, close=()):
            self.compute, self.ins, self.products = compute, ins, products
            self.layout, self.shapes = layout, shapes
            self.width = sum(math.prod(v) for v in products) // (MID * LANES)
            self.close = close
            self.started = 0
            self.result = None

        def partners(self, step):
            level = step if step < levels else 2 * levels - 1 - step
            return [m * units[level] for m in range(1, sizes[level])]

    def slot(info, gradients, last):
        ins, outs, scratch, jobs = [], [], [], []
        bundles = {}
        received = [v for g in gradients if g.started for v, _ in g.got] + [
            g.kept for g in gradients if g.started
        ] + [v for g in gradients if not g.started for v in g.close]
        size = MID // batch

        def give(array):
            for n, v in enumerate(ins):
                if v is array:
                    return n
            ins.append(array)
            return len(ins) - 1

        for g in gradients:
            job = {"targets": []}
            if not g.started:
                job.update(kind="pack", compute=g.compute, numbers=numbers_of(sizes, units))
                job["ins"] = [give(v) for v in g.ins]
                total = batch * g.width
            else:
                done = g.started - 1
                sources = [(give(g.kept), 0)] + [(give(v), first) for v, first in g.got]
                if done < levels:
                    total = g.amount
                    job.update(kind="fold", sources=sources, size=total)
                elif g.started < 2 * levels:
                    total = g.amount * len(sources)
                    job.update(kind="join", sources=sources, size=g.amount)
                    masks = [0] + g.partners(done)
                    g.numbers = [r ^ m for m in masks for r in g.numbers]
                else:
                    masks = [0] + g.partners(done)
                    job.update(kind="place", sources=sources, layout=g.layout, width=g.width)
                    job["numbers"] = [[r ^ m for r in g.numbers] for m in masks]
                    job["finals"] = g
                    jobs.append((g, job, None))
                    continue
            jobs.append((g, job, total))
        for g, job, total in jobs:
            if total is None:
                job["finals"] = list(range(len(outs), len(outs) + len(g.shapes)))
                outs += [(v, F32, "far") for v in g.shapes]
                continue
            step = g.started
            masks = g.partners(step)
            if step < levels:
                share = total // (len(masks) + 1)
                firsts = [share * m for m in range(len(masks) + 1)]
            else:
                share = total
                firsts = [0] * (len(masks) + 1)
                if step == levels:
                    g.numbers = [0]
            g.amount = share
            job["targets"].append((len(outs), 0, firsts[0], share))
            g.kept = len(outs)
            outs.append(((share, size, LANES), BF))
            g.next = []
            for mask, first in zip(masks, firsts[1:]):
                place = bundles.get(mask, 0)
                g.next.append((mask, place))
                bundles[mask] = place + share
                job["targets"].append((mask, place, first, share))
        order = sorted(bundles)
        where = {mask: len(outs) + n for n, mask in enumerate(order)}
        outs += [((bundles[mask], size, LANES), BF) for mask in order]
        for g, job, total in jobs:
            if total is not None:
                job["targets"] = [job["targets"][0]] + [(where[v[0]], *v[1:]) for v in job["targets"][1:]]
            if job["kind"] == "pack":
                job["products"] = list(range(len(outs) + len(scratch), len(outs) + len(scratch) + len(g.products)))
                scratch += [(v, F32) for v in g.products]
        plan = {"ins": len(ins), "jobs": [job for _, job, _ in jobs]}
        given = [v if any(v is w for w in received) else far(v) for v in ins]
        made = in_vmem(
            functools.partial(slot_kernel, batch, chan, plan),
            [info, *given],
            outs,
            scratch,
            after=[last],
            cost=SLOT_COST,
        )
        moved = {mask: swap(made[where[mask]], mask, "batch") for mask in order}
        for g, job, total in jobs:
            if total is None:
                g.result = [made[n] for n in job["finals"]]
            else:
                g.kept = made[g.kept]
                g.got = [(moved[mask], place) for mask, place in g.next]
                g.started += 1
        return made[0] if len(outs[0]) == 2 else far(made[0])

    def local(
        entry_activation,
        image_bounds,
        loss_sensitivity,
        first_contract_kernel,
        first_strided_kernel,
        first_enlarge_kernel,
        projection_kernel,
        second_contract_kernel,
        second_spatial_kernel,
        second_enlarge_kernel,
        bottleneck_gains,
        bottleneck_biases,
        wide_gain_vector,
        wide_bias_vector,
    ):
        images, side, _, quarter = entry_activation.shape
        small = side // 2
        wide = first_enlarge_kernel.shape[1]
        blocks = wide // LANES
        rows, large = small * CHUNK, side * LINE
        depth = quarter * chan
        mid = first_contract_kernel.shape[1] * chan
        assert mid == MID and images == IMAGES and side == SIDE
        piece, full, line = ((rows, LANES), BF), ((rows, wide), BF), ((large, LANES), BF)
        f32s = lambda *shape: (shape, F32)

        info = jnp.concatenate(
            [lax.axis_index("chan")[None], lax.axis_index("batch")[None], image_bounds.T.reshape(-1)]
        ).astype(jnp.int32)
        (own,) = in_vmem(
            enter_kernel, [info, entry_activation.transpose(1, 2, 0, 3)], [((large, quarter), BF)]
        )
        source = gather(own)
        table = jnp.concatenate(
            [
                bottleneck_gains,
                bottleneck_biases,
                wide_gain_vector.reshape(-1, LANES),
                wide_bias_vector.reshape(-1, LANES),
            ]
        )
        tabs = jnp.stack(gather_direct(table))
        loss = loss_sensitivity.transpose(1, 2, 0, 3)

        z1, stats1 = in_vmem(
            functools.partial(first_kernel, chan),
            [far(first_contract_kernel), info, *source],
            [line, f32s(devices, 8, LANES)],
            [f32s(large, LANES)],
        )
        got1 = exchange(stats1)
        z1_far = swap(z1, pair[1])
        even, zs, stats_s, *source_far = in_vmem(
            functools.partial(shortcut_kernel, chan),
            [far(projection_kernel), info, *source],
            [((rows, depth), BF, "far"), (*full, "far"), f32s(2 * blocks, LANES)],
            [f32s(rows, wide)],
            save=range(2, 2 + chan),
        )
        zs_far = swap(zs, pair[1])
        *acts, norms1, counts, z1 = in_vmem(
            functools.partial(first_act_kernel, batch, chan, pair),
            [info, got1, z1, z1_far, tabs],
            [line, line, f32s(8, LANES), f32s(8, LANES)],
            after=[far(zs)],
            save=[2],
        )
        acts = widen(dict(zip(pair, acts)))
        a1, z2, stats2 = in_vmem(
            functools.partial(strided_kernel, chan),
            [far(first_strided_kernel), info, *acts, stats_s],
            [((3, 2, rows + CHUNK, mid), BF, "far"), piece, f32s(devices, 16, LANES)],
            [f32s(rows, LANES)],
        )
        got2 = exchange(stats2)
        near2 = gather_direct(z2)
        a2, z3, stats3, norms2, got2, *near2 = in_vmem(
            functools.partial(enlarge_kernel, batch, chan),
            [far(first_enlarge_kernel), info, got2, *near2, tabs, counts],
            [((rows, mid), BF, "far"), full, f32s(devices, 2 * blocks, LANES), f32s(2 * chan, LANES)],
            [f32s(rows, wide)],
            save=range(2, 3 + chan),
        )
        got3 = exchange(stats3)
        z3_far = swap(z3, pair[1])
        *y1, y1_own, norms3, z3 = in_vmem(
            functools.partial(merge_act_kernel, batch, chan, pair),
            [info, got3, far(got2), z3, z3_far, far(zs), far(zs_far), tabs, counts],
            [full, full, ((rows, wide), F32, "far"), f32s(4 * blocks, LANES)],
            save=[3],
        )
        y1 = widen(dict(zip(pair, y1)))
        z4, stats4, *y1 = in_vmem(
            functools.partial(contract_kernel, chan),
            [far(second_contract_kernel), info, *y1],
            [piece, f32s(devices, 8, LANES)],
            [f32s(rows, LANES)],
            save=range(2, 2 + chan),
        )

        got4 = exchange(stats4)
        near4 = gather_direct(z4)
        a4, z5, stats5, norms4, *near4 = in_vmem(
            functools.partial(spatial_kernel, batch, chan),
            [far(second_spatial_kernel), info, got4, *near4, tabs, counts],
            [((rows, mid), BF, "far"), piece, f32s(devices, 8, LANES), f32s(2 * chan, LANES)],
            [((3, rows + 2 * CHUNK, mid), BF), f32s(rows, LANES)],
            save=range(3, 3 + chan),
        )
        got5 = exchange(stats5)
        near5 = gather_direct(z5)
        a5, z6, stats6, norms5, *near5 = in_vmem(
            functools.partial(last_kernel, batch, chan),
            [far(second_enlarge_kernel), info, got5, *near5, tabs, counts],
            [
                ((rows, mid), BF, "far"),
                f32s(rows, wide),
                f32s(batch, 2 * blocks, LANES),
                f32s(2 * chan, LANES),
            ],
            save=range(3, 3 + chan),
        )
        got6 = exchange_batch(stats6)
        w1t = deliver(cut(first_contract_kernel, 0))
        w2t = deliver(cut(first_strided_kernel, 2))
        wpt = deliver(cut(projection_kernel, 0))
        w4t = deliver(cut(second_contract_kernel, 0))
        result, g2, stats7, norms6, z6 = in_vmem(
            output_kernel,
            [info, got6, z6, far(y1_own), far(loss), tabs, counts],
            [
                ((small, small, images, wide), BF, "far"),
                f32s(rows, wide),
                f32s(batch, 2 * blocks, LANES),
                f32s(2 * blocks, LANES),
            ],
            save=[2],
        )

        shares = [f32s(rows, LANES)] + [piece] * (chan - 1)
        routed = f32s(devices, 8, LANES)
        tap_lanes = 9 * LANES
        got7 = exchange_batch(stats7)
        dz6, *sent, stats8, sums6, g2 = in_vmem(
            functools.partial(back_last_kernel, batch, chan),
            [far(second_enlarge_kernel), info, got7, g2, far(z6), norms6, tabs, counts, *fars(near5), norms5],
            [(*full, "far"), *shares, routed, f32s(2 * blocks, LANES)],
            [f32s(rows, mid)],
            after=fars([*w2t, *w1t, *w4t]),
            save=[3],
        )
        got8 = exchange(stats8)
        parts = deliver(sent)
        spread5, *sent, stats9, sums5 = in_vmem(
            functools.partial(back_spatial_kernel, batch, chan),
            [
                far(second_spatial_kernel), info, got8, *parts, far(near5[0]), norms5, tabs, counts,
                *fars(near4), norms4,
            ],
            [((rows, tap_lanes), BF, "far"), *shares, routed, f32s(8, LANES)],
            [((3, rows + 2 * CHUNK, LANES), BF), f32s(rows, mid)],
            after=fars(wpt),
        )
        got9 = exchange(stats9)
        parts = deliver(sent)
        early = Gradient(
            early_products,
            [a5, dz6, a4, spread5],
            [(mid, wide), (mid, tap_lanes)],
            ((1, 1), (9, 1)),
            [(mid, wide), (9, mid, LANES)],
        )
        last = slot(info, [early], stats9)
        dz4, sums4, dz4_far = in_vmem(
            back_contract_kernel,
            [info, got9, *parts, far(near4[0]), norms4, tabs, counts],
            [piece, f32s(8, LANES), (*piece, "far")],
            after=[last],
        )
        dz4_all = gather_direct(dz4)
        narrowing = Gradient(
            rows_products, [*y1, dz4_far], [(wide * chan, LANES)], ((1, 4),), [(wide * chan, LANES)]
        )
        last = slot(info, [narrowing], dz4)
        g1, stats10 = in_vmem(
            functools.partial(back_merge_kernel, chan),
            [info, *dz4_all, *fars(w4t), far(g2), far(z3), far(zs), norms3, tabs],
            [f32s(rows, wide), f32s(batch, 4 * blocks, LANES)],
            [f32s(rows, wide)],
            after=[last],
        )
        got10 = exchange_batch(stats10)
        last = slot(info, [early, narrowing], stats10)
        dz3, dzs, *sent, stats11, sums3 = in_vmem(
            functools.partial(back_enlarge_kernel, batch, chan),
            [
                far(first_enlarge_kernel), info, got10, g1, far(z3), far(zs), norms3, tabs, counts,
                *fars(near2), norms2,
            ],
            [(*full, "far"), (*full, "far"), *shares, routed, f32s(4 * blocks, LANES)],
            [f32s(rows, mid)],
            after=[last],
        )
        got11 = exchange(stats11)
        parts = deliver(sent)
        widening = Gradient(
            wide_products,
            [a2, dz3, even, dzs],
            [(mid, wide), (depth, wide)],
            ((1, 1), (1, 2)),
            [(mid, wide), (depth, wide)],
        )
        last = slot(info, [widening], stats11)
        dz2, moved2, sums2 = in_vmem(
            back_strided_kernel,
            [info, got11, *parts, far(near2[0]), norms2, tabs, counts],
            [piece, ((rows, 4 * LANES), BF, "far"), f32s(8, LANES)],
            [((2, rows + CHUNK, LANES), BF)],
            after=[last],
        )
        dz2_all = gather_direct(dz2)
        last = slot(info, [early, narrowing], dz2)
        u1, stats12 = in_vmem(
            functools.partial(back_first_kernel, chan),
            [info, *dz2_all, *fars(w2t), far(z1), norms1, tabs],
            [f32s(large, LANES), f32s(batch, 8, LANES)],
            [((2, rows + CHUNK, mid), BF), ((3, 3, LANES, mid), BF), f32s(2, rows, LANES)],
            after=[last],
        )
        got12 = exchange_batch(stats12)
        strided = Gradient(
            strided_products, [a1, moved2], [(mid, tap_lanes)], ((9, 1),), [(9, mid, LANES)]
        )
        last = slot(info, [strided, widening], stats12)
        last = slot(info, [early, narrowing], last)
        dz1, sums1 = in_vmem(
            back_first_own_kernel,
            [info, got12, u1, far(z1), norms1, tabs, counts],
            [line, f32s(8, LANES)],
            after=[last],
        )
        dz1_all = gather(dz1)
        dzs_all = gather(dzs)
        reducing = Gradient(
            rows_products, [*source_far, dz1], [(depth, LANES)], ((1, 2),), [(depth, LANES)], [dz1]
        )
        last = slot(info, [reducing], dz1)
        last = slot(info, [strided], last)
        (inputs_grad,) = in_vmem(
            functools.partial(leave_kernel, chan),
            [info, *dz1_all, *fars(dzs_all), *fars(w1t), *fars(wpt)],
            [((side, side, images, quarter), BF, "far")],
            [f32s(large, quarter), f32s(rows, quarter)],
            after=[last],
            cost=SLOT_COST,
        )
        last = far(inputs_grad)
        for step in (
            [widening],
            [strided],
            [early, narrowing, reducing],
            [widening],
            [strided],
            [reducing],
            [widening],
            [reducing],
        ):
            last = slot(info, step, last)
        everything = [strided, widening, reducing, early, narrowing]
        while any(g.result is None for g in everything):
            last = slot(info, [g for g in everything if g.result is None], last)
        (expanding_grad, middle_grad), (narrowing_grad,) = early.result, narrowing.result
        (widening_grad, shortcut_grad), (spatial_grad,), (reducing_grad,) = (
            g.result for g in (widening, strided, reducing)
        )
        tapped = (3, 3, mid, LANES)
        gains3, gains_s, shift3 = (sums3[n * blocks : (n + 1) * blocks].reshape(-1) for n in range(3))
        gains6, shift6 = sums6[:blocks].reshape(-1), sums6[blocks:].reshape(-1)
        return (
            result.transpose(2, 0, 1, 3),
            inputs_grad.transpose(2, 0, 1, 3),
            reducing_grad,
            spatial_grad.reshape(tapped),
            widening_grad,
            shortcut_grad,
            narrowing_grad,
            middle_grad.reshape(tapped),
            expanding_grad,
            jnp.stack([sums1[0], sums2[0], sums4[0], sums5[0]]),
            jnp.stack([sums1[1], sums2[1], sums4[1], sums5[1]]),
            jnp.stack([gains3, gains_s, gains6]),
            jnp.stack([shift3, shift3, shift6]),
        )

    wide_act = P("batch", None, None, "chan")
    cols = P(None, "chan")
    taps = P(None, None, None, "chan")
    return jax.shard_map(
        local,
        mesh=mesh,
        in_specs=(wide_act, P("batch", None), wide_act, cols, taps, cols, cols, cols, taps)
        + (cols,) * 5,
        out_specs=(wide_act, wide_act, cols, taps, cols, cols, cols, taps) + (cols,) * 5,
        check_vma=False,
    )
```

```python
import functools
import math

import jax
import jax.numpy as jnp
from jax import lax
from jax.experimental import pallas as pl
from jax.experimental.pallas import tpu as pltpu
from jax.sharding import PartitionSpec as P

EPS = 1e-05
BF = jnp.bfloat16
F32 = jnp.float32
GELU_A = 0.7978845608028654
GELU_B = 0.044715
LANES = 128
MID = 512
SIDE = 14
IMAGES = 8
CELLS = 8
CHUNK = CELLS * IMAGES
LINE = SIDE * IMAGES
SLOT_COST = 10**6
LEAVE_COST = 10**6
STEP_COST = 4 * 10**9
SLOTS = {
    "fifth": [["early"]],
    "fourth": [["narrowing"]],
    "merge": [["early", "narrowing"]],
    "third": [["widening"]],
    "shares": [],
    "second": [["early", "narrowing"]],
    "strided": [["strided", "widening"], ["early", "narrowing"]],
    "first": [["reducing"], ["strided"]],
    "end": [["widening"], ["strided"], ["early", "narrowing", "reducing"], ["widening"], ["strided"], ["reducing"], ["widening"], ["reducing"]],
}
VMEM_LIMIT = 20 * 1024 * 1024


def dot(a, b, dims=((1,), (0,))):
    return lax.dot_general(a, b, (dims, ((), ())), preferred_element_type=F32)


def gelu(v):
    return 0.5 * v * (1.0 + jnp.tanh(GELU_A * v * (1.0 + GELU_B * v * v)))


def gelu_slope(v):
    square = v * v
    t = jnp.tanh(GELU_A * v * (1.0 + GELU_B * square))
    return 0.5 * (1.0 + t) * (1.0 + v * (1.0 - t) * (GELU_A + 3.0 * GELU_A * GELU_B * square))


class Masks:
    def __init__(self, info):
        image = lax.broadcasted_iota(jnp.int32, (IMAGES, LANES), 0)
        high = jnp.zeros((IMAGES, LANES), jnp.int32)
        low = jnp.zeros((IMAGES, LANES), jnp.int32)
        inside = jnp.int32(0)
        outside = jnp.int32(0)
        for n in range(IMAGES):
            h, w = info[2 + n], info[2 + IMAGES + n]
            high = jnp.where(image == n, h, high)
            low = jnp.where(image == n, w, low)
            inside = inside + h * w
            outside = outside + lax.shift_right_logical(h + 1, 1) * lax.shift_right_logical(w + 1, 1)
        self.high = high[None]
        self.low = low[None]
        self.column = lax.broadcasted_iota(jnp.int32, (2 * CELLS, IMAGES, LANES), 0)
        self.local_in = inside.astype(F32)
        self.local_out = outside.astype(F32)

    def large(self, row):
        return (row < self.high) & (self.column[:SIDE] < self.low)

    def small(self, row):
        return (2 * row < self.high) & (2 * self.column[:CELLS] < self.low)


def repeat(count, step, init):
    return lax.fori_loop(0, count, step, init, unroll=count if count <= 7 else 2)


def keep(mask, value):
    return jnp.where(mask, value, 0.0)


def cube(rows):
    return rows.astype(F32).reshape(-1, IMAGES, LANES)


def flat(value):
    return value.reshape(-1, LANES)


def padded(value):
    return jnp.concatenate([value, jnp.zeros((1,) + value.shape[1:], F32)], axis=0)


def parted(value):
    pairs = value.reshape(CELLS - 1, 2, *value.shape[1:])
    return padded(pairs[:, 0]), padded(pairs[:, 1])


def merged(even, odd):
    pairs = jnp.stack([even[: CELLS - 1], odd[: CELLS - 1]], axis=1)
    return pairs.reshape(SIDE, *even.shape[1:])


def total_of(value):
    return jnp.sum(value, axis=0)


def row_sum(value):
    return jnp.sum(value, axis=0, keepdims=True)


def at(step, size):
    return pl.ds(pl.multiple_of(step * size, size), size)


def lane_block(index, width=LANES):
    return pl.ds(pl.multiple_of(index * width, width), width)


def push_left(value):
    return jnp.concatenate([value[1:], jnp.zeros((1, IMAGES, LANES), F32)], axis=0)


def push_right(value):
    return jnp.concatenate([jnp.zeros((1, IMAGES, LANES), F32), value[:-1]], axis=0)


def norm_of(got, info, batch, chan, k, row, local, count):
    column = info[0] ^ k
    total = got[column]
    for n in range(1, batch):
        total = total + got[n * chan + column]
    mine = got[info[1] * chan + column]
    mean = total[row : row + 1] / count
    inverse = lax.rsqrt(total[row + 1 : row + 2] / count - mean * mean + EPS)
    return mine[row : row + 1] / local - mean, inverse


def whole(got):
    total = got[0]
    for n in range(1, got.shape[0]):
        total = total + got[n]
    return total


class Late:
    def __init__(self, source, held, semaphore):
        self.copy = pltpu.make_async_copy(source, held, semaphore)
        self.held = held
        self.waiting = True
        self.copy.start()

    def use(self):
        if self.waiting:
            self.copy.wait()
            self.waiting = False
        return self.held


class Far:
    def __init__(self, held, target, semaphore):
        self.copy = pltpu.make_async_copy(held, target, semaphore)
        self.held = held
        self.sent = False
        self.shape = held.shape
        self.dtype = held.dtype

    def __getitem__(self, place):
        return self.held[place]

    def __setitem__(self, place, value):
        self.held[place] = value

    def send(self):
        self.sent = True
        self.copy.start()


def ready(value):
    if isinstance(value, (list, tuple)):
        return [ready(v) for v in value]
    return value.use() if isinstance(value, Late) else value


class far:
    def __init__(self, value):
        self.value = value


def fars(values):
    return [far(v) for v in values]


def in_vmem(kernel, ins, outs, scratch=(), after=(), save=(), cost=None):
    anywhere = pl.BlockSpec(memory_space=pl.ANY)
    inside = pl.BlockSpec(memory_space=pltpu.VMEM)
    args = [
        pltpu.with_memory_space_constraint(v.value, pltpu.HBM)
        if isinstance(v, far)
        else pltpu.with_memory_space_constraint(v, pltpu.VMEM)
        for v in after
    ]
    specs, late, buffers = [anywhere] * len(after), [], []
    for n, v in enumerate(ins):
        if isinstance(v, far):
            late.append(n)
            buffers.append(pltpu.VMEM(v.value.shape, v.value.dtype))
            args.append(pltpu.with_memory_space_constraint(v.value, pltpu.HBM))
            specs.append(anywhere)
        elif v.dtype == jnp.int32:
            args.append(v)
            specs.append(pl.BlockSpec(memory_space=pltpu.SMEM))
        else:
            args.append(pltpu.with_memory_space_constraint(v, pltpu.VMEM))
            specs.append(inside)
    distant = [n for n, out in enumerate(outs) if len(out) > 2]
    buffers += [pltpu.VMEM(*outs[n][:2]) for n in distant]
    shapes = [(pltpu.HBM if len(out) > 2 else pltpu.VMEM)(*out[:2]) for out in outs]
    shapes += [pltpu.HBM(ins[n].shape, ins[n].dtype) for n in save]
    out_specs = [anywhere if len(out) > 2 else inside for out in outs] + [anywhere] * len(save)
    semaphores = len(buffers) + len(save)

    def body(*refs):
        refs = list(refs[len(after) :])
        given, refs = refs[: len(ins)], refs[len(ins) :]
        made, refs = refs[: len(outs)], refs[len(outs) :]
        saved, refs = refs[: len(save)], refs[len(save) :]
        free, refs = refs[: len(scratch)], refs[len(scratch) :]
        held, marks = refs[: len(buffers)], refs[len(buffers) :]
        for place, n in enumerate(late):
            given[n] = Late(given[n], held[place], marks[place])
        for place, n in enumerate(distant, len(late)):
            made[n] = Far(held[place], made[n], marks[place])
        copies = [
            pltpu.make_async_copy(given[n], out, mark)
            for n, out, mark in zip(save, saved, marks[len(buffers) :])
        ]
        for copy in copies:
            copy.start()
        kernel(*given, *made, *free)
        for n in distant:
            if not made[n].sent:
                made[n].send()
        for n in late:
            given[n].use()
        for n in distant:
            made[n].copy.wait()
        for copy in copies:
            copy.wait()

    return pl.pallas_call(
        body,
        out_shape=shapes,
        in_specs=specs,
        out_specs=out_specs,
        scratch_shapes=[pltpu.VMEM(*v) for v in scratch] + buffers + [pltpu.SemaphoreType.DMA] * semaphores,
        compiler_params=pltpu.CompilerParams(vmem_limit_bytes=VMEM_LIMIT),
        cost_estimate=pl.CostEstimate(flops=cost or STEP_COST, bytes_accessed=0, transcendentals=0),
    )(*args)


def held_back(value, after):
    def body(*refs):
        del refs

    args = [pltpu.with_memory_space_constraint(v, pltpu.VMEM) for v in (value, *after)]
    anywhere = pl.BlockSpec(memory_space=pl.ANY)
    return pl.pallas_call(
        body,
        out_shape=pltpu.VMEM(value.shape, value.dtype),
        in_specs=[anywhere] * len(args),
        out_specs=anywhere,
        input_output_aliases={0: 0},
    )(*args)


def sums_of(z, chunks, lanes, mask=None, size=CHUNK):
    def step(t, carry):
        value = cube(z[at(t, size), lanes])
        if mask is not None:
            value = keep(mask(t), value)
        return carry[0] + total_of(value), carry[1] + total_of(value * value)

    zero = jnp.zeros((IMAGES, LANES), F32)
    total, squares = repeat(chunks, step, (zero, zero))
    return row_sum(total), row_sum(squares)


def centre_into(out, z, chunks, lanes, mean, size=CHUNK):
    def step(t, _):
        out[at(t, size), lanes] = (z[at(t, size), lanes] - mean).astype(BF)
        return 0

    repeat(chunks, step, 0)


def broadcast_rows(out, rows):
    block = jnp.concatenate(
        list(rows) + [jnp.zeros((out.shape[1] - len(rows), LANES), F32)]
        if len(rows) < out.shape[1]
        else list(rows),
        axis=0,
    )
    out[...] = jnp.broadcast_to(block[None], out.shape)


def fill_rows(out, rows):
    for n, row in enumerate(rows):
        out[n : n + 1, :] = row
    if len(rows) < out.shape[0]:
        out[len(rows) :, :] = jnp.zeros((out.shape[0] - len(rows), LANES), F32)


def first_part_kernel(chan, ks, w, info, *refs):
    source, (z,) = refs[: len(ks)], refs[len(ks) :]
    rows, depth = source[0].shape
    part = 2 * LINE
    w = w.use()

    def step(t, _):
        total = None
        for n, k in enumerate(ks):
            term = dot(source[n][at(t, part), :], w[at(info[0] ^ k, depth), :])
            total = term if total is None else total + term
        z[at(t, part), :] = total
        return 0

    repeat(rows // part, step, 0)


def first_kernel(chan, ks, w, info, part_z, *refs):
    source, (zc, stats, z) = refs[: len(ks)], refs[len(ks) :]
    masks = Masks(info)
    rows, depth = source[0].shape
    part = 2 * LINE
    w = w.use()

    def step(t, _):
        total = part_z[at(t, part), :]
        for n, k in enumerate(ks):
            total = total + dot(source[n][at(t, part), :], w[at(info[0] ^ k, depth), :])
        z[at(t, part), :] = total
        return 0

    repeat(rows // part, step, 0)
    total, squares = sums_of(z, SIDE, slice(0, LANES), masks.large, LINE)
    ones = jnp.ones((1, LANES), F32)
    broadcast_rows(stats, (total, squares, ones * masks.local_in, ones * masks.local_out))
    centre_into(zc, z, SIDE, slice(0, LANES), total / masks.local_in, LINE)


def shortcut_kernel(chan, w, info, *refs):
    source, (even, zc, stats, z) = refs[:chan], refs[chan:]
    masks = Masks(info)
    rows, width = z.shape
    depth = source[0].shape[1]
    chunks = rows // CHUNK

    def step(i, _):
        for k in range(chan):
            for q in range(depth // LANES):
                lanes = slice(q * LANES, (q + 1) * LANES)
                value, _ = parted(cube(source[k][at(2 * i, LINE), lanes]))
                place = lane_block((info[0] ^ k) * (depth // LANES) + q)
                even[at(i, CHUNK), place] = flat(value).astype(BF)
        return 0

    repeat(chunks, step, 0)
    even.send()
    z[...] = dot(even[...], w.use()[...])
    blocks = width // LANES
    for q in range(blocks):
        lanes = slice(q * LANES, (q + 1) * LANES)
        total, squares = sums_of(z, chunks, lanes, masks.small)
        stats[q : q + 1, :] = total
        stats[blocks + q : blocks + q + 1, :] = squares
        centre_into(zc, z, chunks, lanes, total / masks.local_out)


def first_act_kernel(batch, chan, pair, info, got, *refs):
    near, (tabs, *outs, norms, counts) = refs[: len(pair)], refs[len(pair) :]
    masks = Masks(info)
    total = whole(got)
    count_in, count_out = total[2:3] / chan, total[3:4] / chan
    fill_rows(counts, (count_in, count_out))
    params = [norm_of(got, info, batch, chan, k, 0, masks.local_in, count_in) for k in pair]
    norms[0:1, :] = params[0][0]
    norms[1:2, :] = params[0][1]

    def step(r, _):
        mask = masks.large(r)
        for n, k in enumerate(pair):
            scale = params[n][1] * tabs[k, 0:1, :]
            shift = params[n][0] * scale + tabs[k, 4:5, :]
            value = keep(mask, gelu(cube(near[n][at(r, LINE), :]) * scale + shift))
            outs[n][at(r, LINE), :] = flat(value).astype(BF)
        return 0

    repeat(SIDE, step, 0)


def strided_kernel(chan, w, info, *refs):
    pieces, (extra, a, zc, stats, z) = refs[:chan], refs[chan:]
    masks = Masks(info)
    width = a.shape[3]
    for tap in range(3):
        a[tap, 0, 0:CHUNK, :] = jnp.zeros((CHUNK, width), BF)

    def step(r, _):
        line = r + 1
        half, place = line & 1, lax.shift_right_logical(line, 1)
        for k in range(chan):
            lanes = lane_block(info[0] ^ k)
            even, odd = parted(cube(pieces[k][at(r, LINE), :]))
            a[0, half, at(place, CHUNK), lanes] = flat(push_right(odd)).astype(BF)
            a[1, half, at(place, CHUNK), lanes] = flat(even).astype(BF)
            a[2, half, at(place, CHUNK), lanes] = flat(odd).astype(BF)
        return 0

    repeat(SIDE, step, 0)
    a.send()
    rows = z.shape[0]
    acc = None
    w = w.use()
    for i, (half, first) in enumerate(((0, 0), (1, 0), (0, CHUNK))):
        for j in range(3):
            term = dot(a[j, half, first : first + rows, :], w[i, j])
            acc = term if acc is None else acc + term
    z[...] = acc
    chunks = rows // CHUNK
    total, squares = sums_of(z, chunks, slice(0, LANES), masks.small)
    block = jnp.concatenate([total, squares, jnp.zeros((6, LANES), F32), extra[...]], axis=0)
    stats[...] = jnp.broadcast_to(block[None], stats.shape)
    centre_into(zc, z, chunks, slice(0, LANES), total / masks.local_out)


def activate_into(near, params, tabs, gain, chan, info, masks, chunks, store):
    def step(t, _):
        mask = masks.small(t)
        for k in range(chan):
            scale = params[k][1] * tabs[k, gain : gain + 1, :]
            shift = params[k][0] * scale + tabs[k, gain + 4 : gain + 5, :]
            value = keep(mask, gelu(cube(near[k][at(t, CHUNK), :]) * scale + shift))
            store(t, lane_block(info[0] ^ k), value)
        return 0

    repeat(chunks, step, 0)


def store_norms(norms, params):
    for k, norm in enumerate(params):
        norms[2 * k : 2 * k + 1, :] = norm[0]
        norms[2 * k + 1 : 2 * k + 2, :] = norm[1]


def enlarge_kernel(batch, chan, w, info, got, *refs):
    near, (tabs, counts, a, zc, stats, norms, z) = refs[:chan], refs[chan:]
    masks = Masks(info)
    count = counts[1:2, :]
    params = [norm_of(got, info, batch, chan, k, 0, masks.local_out, count) for k in range(chan)]
    store_norms(norms, params)
    chunks = z.shape[0] // CHUNK

    def store(t, lanes, value):
        a[at(t, CHUNK), lanes] = flat(value).astype(BF)

    activate_into(near, params, tabs, 1, chan, info, masks, chunks, store)
    a.send()
    z[...] = dot(a[...], w.use()[...])
    rows = wide_sums(z, zc, chunks, masks)
    broadcast_rows(stats, rows)


def wide_sums(z, zc, chunks, masks):
    blocks = z.shape[1] // LANES
    totals, squares = [], []
    for q in range(blocks):
        lanes = slice(q * LANES, (q + 1) * LANES)
        total, square = sums_of(z, chunks, lanes)
        totals.append(total)
        squares.append(square)
        if zc is not None:
            centre_into(zc, z, chunks, lanes, total / masks.local_out)
    return totals + squares


def wide_norm(got, info, batch, chan, k, row, blocks, local, count):
    column = info[0] ^ k
    total = got[column]
    for n in range(1, batch):
        total = total + got[n * chan + column]
    mine = got[info[1] * chan + column]
    mean = total[row : row + blocks] / count
    inverse = lax.rsqrt(total[row + blocks : row + 2 * blocks] / count - mean * mean + EPS)
    return mine[row : row + blocks] / local - mean, inverse


def merge_act_kernel(batch, chan, pair, info, got3, got2, *refs):
    size = len(pair)
    near3, nears = refs[:size], refs[size : 2 * size]
    tabs, counts, *outs, own, norms = refs[2 * size :]
    nears, got2 = ready(nears), ready(got2)
    masks = Masks(info)
    count = counts[1:2, :]
    rows, width = near3[0].shape
    blocks = width // LANES
    lines = []
    for k in pair:
        one = wide_norm(got3, info, batch, chan, k, 0, blocks, masks.local_out, count)
        two = wide_norm(got2, info, batch, chan, k, 8, blocks, masks.local_out, count)
        if k == 0:
            for n, value in enumerate(one + two):
                norms[n * blocks : (n + 1) * blocks, :] = value
        gain, bias = 8, 8 + 3 * blocks
        scale3 = one[1] * tabs[k, gain : gain + blocks, :]
        scales = two[1] * tabs[k, gain + blocks : gain + 2 * blocks, :]
        shift = (
            one[0] * scale3
            + two[0] * scales
            + tabs[k, bias : bias + blocks, :]
            + tabs[k, bias + blocks : bias + 2 * blocks, :]
        )
        lines.append((scale3, scales, shift))

    def step(t, _):
        mask = masks.small(t)
        for n, k in enumerate(pair):
            scale3, scales, shift = lines[n]
            for q in range(blocks):
                lanes = slice(q * LANES, (q + 1) * LANES)
                pre = (
                    cube(near3[n][at(t, CHUNK), lanes]) * scale3[q : q + 1]
                    + cube(nears[n][at(t, CHUNK), lanes]) * scales[q : q + 1]
                    + shift[q : q + 1]
                )
                value = flat(keep(mask, gelu(pre)))
                if k == 0:
                    own[at(t, CHUNK), lanes] = value
                outs[n][at(t, CHUNK), lanes] = value.astype(BF)
        return 0

    repeat(rows // CHUNK, step, 0)


def contract_kernel(chan, w, info, *refs):
    y, (zc, stats, z) = refs[:chan], refs[chan:]
    masks = Masks(info)
    rows, width = y[0].shape
    chunks = rows // CHUNK
    w = w.use()
    total = None
    for k in range(chan):
        term = dot(y[k][...], w[at(info[0] ^ k, width), :])
        total = term if total is None else total + term
    z[...] = total
    total, squares = sums_of(z, chunks, slice(0, LANES))
    broadcast_rows(stats, (total, squares))
    centre_into(zc, z, chunks, slice(0, LANES), total / masks.local_out)


def spatial_kernel(batch, chan, w, info, got, *refs):
    near, (tabs, counts, a, zc, stats, norms, held, z) = refs[:chan], refs[chan:]
    masks = Masks(info)
    count = counts[1:2, :]
    params = [norm_of(got, info, batch, chan, k, 0, masks.local_out, count) for k in range(chan)]
    store_norms(norms, params)
    rows, width = a.shape
    chunks = rows // CHUNK
    for tap in range(3):
        held[tap, 0:CHUNK, :] = jnp.zeros((CHUNK, width), BF)
        held[tap, rows + CHUNK : rows + 2 * CHUNK, :] = jnp.zeros((CHUNK, width), BF)

    def store(t, lanes, value):
        plain = flat(value).astype(BF)
        a[at(t, CHUNK), lanes] = plain
        held[1, at(t + 1, CHUNK), lanes] = plain
        held[0, at(t + 1, CHUNK), lanes] = flat(push_right(value)).astype(BF)
        held[2, at(t + 1, CHUNK), lanes] = flat(push_left(value)).astype(BF)

    activate_into(near, params, tabs, 2, chan, info, masks, chunks, store)
    a.send()
    acc = None
    w = w.use()
    for i in range(3):
        for j in range(3):
            term = dot(held[j, i * CHUNK : i * CHUNK + rows, :], w[i, j])
            acc = term if acc is None else acc + term
    z[...] = acc
    total, squares = sums_of(z, chunks, slice(0, LANES), masks.small)
    broadcast_rows(stats, (total, squares))
    centre_into(zc, z, chunks, slice(0, LANES), total / masks.local_out)


def last_kernel(batch, chan, w, info, got, *refs):
    near, (tabs, counts, a, z, stats, norms) = refs[:chan], refs[chan:]
    masks = Masks(info)
    count = counts[1:2, :]
    params = [norm_of(got, info, batch, chan, k, 0, masks.local_out, count) for k in range(chan)]
    store_norms(norms, params)
    chunks = a.shape[0] // CHUNK

    def store(t, lanes, value):
        a[at(t, CHUNK), lanes] = flat(value).astype(BF)

    activate_into(near, params, tabs, 3, chan, info, masks, chunks, store)
    a.send()
    z[...] = dot(a[...], w.use()[...])
    broadcast_rows(stats, wide_sums(z, None, chunks, masks))


def output_kernel(info, got, z, own, loss, tabs, counts, result, g, stats, norms):
    masks = Masks(info)
    own, loss = ready(own), ready(loss)
    count = counts[1:2, :]
    total = whole(got)
    rows, width = z.shape
    blocks = width // LANES
    chunks = rows // CHUNK
    mean = total[0:blocks] / count
    inverse = lax.rsqrt(total[blocks : 2 * blocks] / count - mean * mean + EPS)
    norms[0:blocks, :] = mean
    norms[blocks : 2 * blocks, :] = inverse
    gain = tabs[0, 8 + 2 * blocks : 8 + 3 * blocks, :]
    bias = tabs[0, 8 + 5 * blocks : 8 + 6 * blocks, :]
    small = result.shape[1]

    def step(t, carry):
        mask = masks.small(t)
        sums = []
        for q in range(blocks):
            lanes = slice(q * LANES, (q + 1) * LANES)
            zhat = (cube(z[at(t, CHUNK), lanes]) - mean[q : q + 1]) * inverse[q : q + 1]
            pre = zhat * gain[q : q + 1] + bias[q : q + 1] + cube(own[at(t, CHUNK), lanes])
            result[t, :, :, lanes] = keep(mask, gelu(pre))[:small].astype(BF)
            u = keep(mask, gelu_slope(pre)) * padded(loss[t, :, :, lanes].astype(F32))
            g[at(t, CHUNK), lanes] = flat(u)
            sums.append((carry[q][0] + total_of(u * zhat), carry[q][1] + total_of(u)))
        return tuple(sums)

    zero = jnp.zeros((IMAGES, LANES), F32)
    sums = repeat(chunks, step, ((zero, zero),) * blocks)
    broadcast_rows(stats, [row_sum(s[0]) for s in sums] + [row_sum(s[1]) for s in sums])


def share_stage(da, near, norms, tabs, gain, chan, batch, info, masks, chunks, pieces, stats):
    zero = jnp.zeros((IMAGES, LANES), F32)
    for k in range(chan):
        lanes = lane_block(info[0] ^ k)
        offset, inverse = norms[2 * k : 2 * k + 1, :], norms[2 * k + 1 : 2 * k + 2, :]
        scale, bias = tabs[k, gain : gain + 1, :], tabs[k, gain + 4 : gain + 5, :]

        def step(t, carry, k=k, lanes=lanes, offset=offset, inverse=inverse, scale=scale, bias=bias):
            share = da[at(t, CHUNK), lanes]
            zhat = (cube(near[k][at(t, CHUNK), :]) + offset) * inverse
            u = keep(masks.small(t), gelu_slope(zhat * scale + bias)) * cube(share)
            pieces[k][at(t, CHUNK), :] = share.astype(pieces[k].dtype)
            return carry[0] + total_of(u * zhat), carry[1] + total_of(u)

        first, second = repeat(chunks, step, (zero, zero))
        block = jnp.concatenate([row_sum(first), row_sum(second)], axis=0)
        for n in range(batch):
            stats[n * chan + (info[0] ^ k)] = block


def own_stage(got, parts, near, norms, tabs, gain, count, masks, chunks, sums, store):
    total = whole(got)
    gg, gb = total[0:1], total[1:2]
    fill_rows(sums, (gg, gb))
    offset, inverse = norms[0:1, :], norms[1:2, :]
    scale, bias = tabs[0, gain : gain + 1, :], tabs[0, gain + 4 : gain + 5, :]
    per_cell, per_hat = gb / count, gg / count
    front = scale * inverse

    def step(t, _):
        mask = masks.small(t)
        da = cube(parts[0][at(t, CHUNK), :])
        for part in parts[1:]:
            da = da + cube(part[at(t, CHUNK), :])
        zhat = (cube(near[at(t, CHUNK), :]) + offset) * inverse
        u = gelu_slope(zhat * scale + bias) * da
        store(t, keep(mask, front * (u - (per_cell + zhat * per_hat))))
        return 0

    repeat(chunks, step, 0)


def back_last_kernel(batch, chan, w, info, got, g, z, norms6, tabs, counts, *refs):
    near, (norms, dz, *pieces, stats, sums, da) = refs[:chan], refs[chan:]
    masks = Masks(info)
    z = ready(z)
    count = counts[1:2, :]
    total = whole(got)
    rows, width = z.shape
    blocks = width // LANES
    chunks = rows // CHUNK
    gg, gb = total[0:blocks] / count, total[blocks : 2 * blocks] / count
    sums[...] = total
    mean, inverse = norms6[0:blocks, :], norms6[blocks : 2 * blocks, :]
    front = tabs[0, 8 + 2 * blocks : 8 + 3 * blocks, :] * inverse

    def step(t, _):
        mask = masks.small(t)
        for q in range(blocks):
            lanes = slice(q * LANES, (q + 1) * LANES)
            zhat = (cube(z[at(t, CHUNK), lanes]) - mean[q : q + 1]) * inverse[q : q + 1]
            value = cube(g[at(t, CHUNK), lanes]) - (gb[q : q + 1] + zhat * gg[q : q + 1])
            dz[at(t, CHUNK), lanes] = flat(keep(mask, front[q : q + 1] * value)).astype(BF)
        return 0

    repeat(chunks, step, 0)
    dz.send()
    da[...] = dot(dz[...], w.use()[...], ((1,), (1,)))
    near = ready(near)
    share_stage(da, near, norms, tabs, 3, chan, batch, info, masks, chunks, pieces, stats)


def back_spatial_kernel(batch, chan, w, info, got, *refs):
    parts, refs = refs[:chan], refs[chan:]
    own, norms5, tabs, counts = refs[:4]
    near, (norms, spread, *pieces, stats, sums, held, da) = refs[4 : 4 + chan], refs[4 + chan :]
    masks = Masks(info)
    own = ready(own)
    rows = own.shape[0]
    chunks = rows // CHUNK
    for tap in range(3):
        held[tap, 0:CHUNK, :] = jnp.zeros((CHUNK, LANES), BF)
        held[tap, rows + CHUNK : rows + 2 * CHUNK, :] = jnp.zeros((CHUNK, LANES), BF)

    def store(t, value):
        held[1, at(t + 1, CHUNK), :] = flat(value).astype(BF)
        held[0, at(t + 1, CHUNK), :] = flat(push_left(value)).astype(BF)
        held[2, at(t + 1, CHUNK), :] = flat(push_right(value)).astype(BF)

    own_stage(got, parts, own, norms5, tabs, 3, counts[1:2, :], masks, chunks, sums, store)
    acc = None
    w = w.use()
    for i in range(3):
        for j in range(3):
            value = held[j, (2 - i) * CHUNK : (2 - i) * CHUNK + rows, :]
            spread[:, (3 * i + j) * LANES : (3 * i + j + 1) * LANES] = value
            term = dot(value, w[i, j], ((1,), (1,)))
            acc = term if acc is None else acc + term
    da[...] = acc
    spread.send()
    near = ready(near)
    share_stage(da, near, norms, tabs, 2, chan, batch, info, masks, chunks, pieces, stats)


def back_contract_kernel(info, got, *refs):
    *parts, own, norms, tabs, counts, dz, sums, copy = refs
    own = ready(own)
    masks = Masks(info)

    def store(t, value):
        plain = flat(value).astype(BF)
        dz[at(t, CHUNK), :] = plain
        copy[at(t, CHUNK), :] = plain

    own_stage(got, parts, own, norms, tabs, 2, counts[1:2, :], masks, own.shape[0] // CHUNK, sums, store)


def back_merge_kernel(chan, info, *refs):
    dz, w = refs[:chan], refs[chan : 2 * chan]
    g, near3, nears, norms, tabs, g1, stats, dy = refs[2 * chan :]
    masks = Masks(info)
    rows, width = dy.shape
    blocks = width // LANES
    chunks = rows // CHUNK
    acc = None
    for k in range(chan):
        term = dot(dz[k][...], ready(w[k])[...], ((1,), (1,)))
        acc = term if acc is None else acc + term
    dy[...] = acc
    g, near3, nears = ready(g), ready(near3), ready(nears)
    zero = jnp.zeros((IMAGES, LANES), F32)
    lines = [[], [], []]
    for q in range(blocks):
        lanes = slice(q * LANES, (q + 1) * LANES)
        off3, inv3, offs, invs = (norms[n * blocks + q : n * blocks + q + 1, :] for n in range(4))
        gain, bias = 8, 8 + 3 * blocks
        gain3, gains = tabs[0, gain + q : gain + q + 1, :], tabs[0, gain + blocks + q : gain + blocks + q + 1, :]
        shift = tabs[0, bias + q : bias + q + 1, :] + tabs[0, bias + blocks + q : bias + blocks + q + 1, :]

        def step(t, carry):
            zhat3 = (cube(near3[at(t, CHUNK), lanes]) + off3) * inv3
            zhats = (cube(nears[at(t, CHUNK), lanes]) + offs) * invs
            pre = zhat3 * gain3 + zhats * gains + shift
            up = cube(g[at(t, CHUNK), lanes]) + cube(dy[at(t, CHUNK), lanes])
            u = keep(masks.small(t), gelu_slope(pre)) * up
            g1[at(t, CHUNK), lanes] = flat(u)
            return (
                carry[0] + total_of(u * zhat3),
                carry[1] + total_of(u * zhats),
                carry[2] + total_of(u),
            )

        done = repeat(chunks, step, (zero, zero, zero))
        for n in range(3):
            lines[n].append(row_sum(done[n]))
    broadcast_rows(stats, lines[0] + lines[1] + lines[2])


def back_enlarge_kernel(batch, chan, w, info, got, g1, near3, nears, norms3, tabs, counts, *refs):
    near, (norms, dz3, dzs, *pieces, stats, sums, da) = refs[:chan], refs[chan:]
    masks = Masks(info)
    near3, nears = ready(near3), ready(nears)
    count = counts[1:2, :]
    total = whole(got)
    sums[...] = total
    rows, width = g1.shape
    blocks = width // LANES
    chunks = rows // CHUNK
    total = total / count
    gg3, ggs, gb = (total[n * blocks : (n + 1) * blocks] for n in range(3))
    off3, inv3, offs, invs = (norms3[n * blocks : (n + 1) * blocks, :] for n in range(4))
    front3 = tabs[0, 8 : 8 + blocks, :] * inv3
    fronts = tabs[0, 8 + blocks : 8 + 2 * blocks, :] * invs

    def step(t, _):
        mask = masks.small(t)
        for q in range(blocks):
            lanes = slice(q * LANES, (q + 1) * LANES)
            line = slice(q, q + 1)
            u = cube(g1[at(t, CHUNK), lanes]) - gb[line]
            zhat3 = (cube(near3[at(t, CHUNK), lanes]) + off3[line]) * inv3[line]
            zhats = (cube(nears[at(t, CHUNK), lanes]) + offs[line]) * invs[line]
            dz3[at(t, CHUNK), lanes] = flat(keep(mask, front3[line] * (u - zhat3 * gg3[line]))).astype(BF)
            dzs[at(t, CHUNK), lanes] = flat(keep(mask, fronts[line] * (u - zhats * ggs[line]))).astype(BF)
        return 0

    repeat(chunks, step, 0)
    dz3.send()
    dzs.send()
    da[...] = dot(dz3[...], w.use()[...], ((1,), (1,)))
    near = ready(near)
    share_stage(da, near, norms, tabs, 1, chan, batch, info, masks, chunks, pieces, stats)


def back_strided_kernel(info, got, *refs):
    *parts, own, norms, tabs, counts, dz, moved, sums, held = refs
    masks = Masks(info)
    own = ready(own)
    rows = own.shape[0]
    for tap in range(2):
        held[tap, rows : rows + CHUNK, :] = jnp.zeros((CHUNK, LANES), BF)

    def store(t, value):
        plain = flat(value).astype(BF)
        dz[at(t, CHUNK), :] = plain
        held[0, at(t, CHUNK), :] = plain
        held[1, at(t, CHUNK), :] = flat(push_left(value)).astype(BF)

    own_stage(got, parts, own, norms, tabs, 1, counts[1:2, :], masks, rows // CHUNK, sums, store)
    for down in range(2):
        for right in range(2):
            n = 2 * down + right
            moved[:, n * LANES : (n + 1) * LANES] = held[right, down * CHUNK : down * CHUNK + rows, :]


TAPS = {0: ((1, 0),), 1: ((2, 0), (0, 1))}


def back_first_kernel(chan, info, *refs):
    dz, w = refs[:chan], refs[chan : 2 * chan]
    near, norms, tabs, u_out, stats, held, joined, da = refs[2 * chan :]
    masks = Masks(info)
    rows = dz[0].shape[0]
    chunks = rows // CHUNK
    for tap in range(2):
        held[tap, rows : rows + CHUNK, :] = jnp.zeros((CHUNK, chan * LANES), BF)
    for k in range(chan):
        joined[:, :, :, k * LANES : (k + 1) * LANES] = ready(w[k])[...]
    near = ready(near)

    def shift(t, _):
        for k in range(chan):
            lanes = slice(k * LANES, (k + 1) * LANES)
            value = dz[k][at(t, CHUNK), :]
            held[0, at(t, CHUNK), lanes] = value
            held[1, at(t, CHUNK), lanes] = flat(push_left(cube(value))).astype(BF)
        return 0

    repeat(chunks, shift, 0)
    offset, inverse = norms[0:1, :], norms[1:2, :]
    scale, bias = tabs[0, 0:1, :], tabs[0, 4:5, :]
    zero = jnp.zeros((IMAGES, LANES), F32)
    sums = (zero, zero)
    for p in range(2):
        for q in range(2):
            acc = None
            for a, down in TAPS[p]:
                for b, right in TAPS[q]:
                    term = dot(
                        held[right, down * CHUNK : down * CHUNK + rows, :], joined[a, b], ((1,), (1,))
                    )
                    acc = term if acc is None else acc + term
            da[q] = acc

        def step(t, carry, p=p):
            r = 2 * t + p
            place = at(r, LINE)
            zhat = (cube(near[place, :]) + offset) * inverse
            up = merged(cube(da[0, at(t, CHUNK), :]), cube(da[1, at(t, CHUNK), :]))
            u = keep(masks.large(r), gelu_slope(zhat * scale + bias)) * up
            u_out[place, :] = flat(u)
            return carry[0] + total_of(u * zhat), carry[1] + total_of(u)

        sums = repeat(chunks, step, sums)
    broadcast_rows(stats, (row_sum(sums[0]), row_sum(sums[1])))


def back_first_own_kernel(info, got, u, near, norms, tabs, counts, dz, sums):
    masks = Masks(info)
    count = counts[0:1, :]
    total = whole(got)
    gg, gb = total[0:1], total[1:2]
    fill_rows(sums, (gg, gb))
    per_cell, per_hat = gb / count, gg / count
    near = ready(near)
    offset, inverse = norms[0:1, :], norms[1:2, :]
    front = tabs[0, 0:1, :] * inverse

    def step(r, _):
        place = at(r, LINE)
        zhat = (cube(near[place, :]) + offset) * inverse
        value = front * (cube(u[place, :]) - (per_cell + zhat * per_hat))
        dz[place, :] = flat(keep(masks.large(r), value)).astype(BF)
        return 0

    repeat(SIDE, step, 0)


def leave_kernel(chan, info, *refs):
    dz, dzs = refs[:chan], refs[chan : 2 * chan]
    w, ws = refs[2 * chan : 3 * chan], refs[3 * chan : 4 * chan]
    out, dm, extra = refs[4 * chan :]
    masks = Masks(info)
    acc = None
    for k in range(chan):
        term = dot(ready(dzs[k])[...], ready(ws[k])[...], ((1,), (1,)))
        acc = term if acc is None else acc + term
    extra[...] = acc
    width = out.shape[3]
    part = 2 * LINE
    w = ready(w)

    def product(t, _):
        total = None
        for k in range(chan):
            term = dot(dz[k][at(t, part), :], w[k][...], ((1,), (1,)))
            total = term if total is None else total + term
        dm[at(t, part), :] = total
        return 0

    repeat(dm.shape[0] // part, product, 0)

    def step(i, _):
        for p in range(2):
            r = 2 * i + p
            mask = masks.large(r)
            for q in range(width // LANES):
                lanes = slice(q * LANES, (q + 1) * LANES)
                value = cube(dm[at(r, LINE), lanes])
                if p == 0:
                    more = cube(extra[at(i, CHUNK), lanes])
                    value = value + merged(more, jnp.zeros_like(more))
                out[r, :, :, lanes] = keep(mask, value).astype(BF)
        return 0

    repeat(SIDE // 2, step, 0)


def radices_of(batch):
    sizes, units, unit = [], [], 1
    while unit < batch:
        size = 2 if not sizes or batch // unit == 2 else 4
        sizes.append(size)
        units.append(unit)
        unit *= size
    return sizes, units


def numbers_of(sizes, units):
    numbers = [0]
    for size, unit in reversed(list(zip(sizes, units))):
        numbers = [r + m * unit for m in range(size) for r in numbers]
    return numbers


def early_products(chan, info, ins, outs):
    outs[0][...] = dot(ins[0][...], ins[1][...], ((0,), (0,)))
    outs[1][...] = dot(ins[2][...], ins[3][...], ((0,), (0,)))


def rows_products(chan, info, ins, outs):
    *pieces, right = ins
    size = pieces[0].shape[1]
    for k, piece in enumerate(pieces):
        outs[0][at(info[0] ^ k, size), :] = dot(piece[...], right[...], ((0,), (0,)))


def wide_products(chan, info, ins, outs):
    a2, dz3, even, dzs = ins
    outs[0][...] = dot(a2[...], dz3[...], ((0,), (0,)))
    outs[1][...] = dot(even[...], dzs[...], ((0,), (0,)))


def strided_products(chan, info, ins, outs):
    a1, moved = ins
    rows = moved.shape[0]
    for p in range(2):
        for q in range(2):
            start = CHUNK if p else 0
            plane = a1[1 + q, 1 - p, start : start + rows, :]
            for a, down in TAPS[p]:
                for b, right in TAPS[q]:
                    n = 2 * down + right
                    tap = 3 * a + b
                    outs[0][:, tap * LANES : (tap + 1) * LANES] = dot(
                        plane, moved[:, n * LANES : (n + 1) * LANES], ((0,), (0,))
                    )


def cut_product(ref, number, batch):
    rows = ref.shape[0] // batch
    size = MID // batch
    for n in range(rows // size):
        for lane in range(0, ref.shape[1], LANES):
            first = number * rows + n * size
            yield ref[pl.ds(pl.multiple_of(first, size), size), lane : lane + LANES]


def place_chunk(blocks, outs, layout, number):
    blocks = list(blocks)
    for out, (taps, repeats) in zip(outs, layout):
        size = blocks[0].shape[0]
        for n in range(taps * repeats):
            for lane in range(0, out.shape[-1], LANES):
                value = blocks.pop(0).astype(F32)
                if taps > 1:
                    out[n, at(number, size), lane : lane + LANES] = value
                else:
                    first = (number * repeats + n) * size
                    out[pl.ds(pl.multiple_of(first, size), size), lane : lane + LANES] = value


def slot_kernel(batch, chan, plan, info, *refs):
    ins, outs = refs[: plan["ins"]], refs[plan["ins"] :]
    for job in plan["jobs"]:
        if job["kind"] == "pack":
            products = [outs[n] for n in job["products"]]
            job["compute"](chan, info, ready([ins[n] for n in job["ins"]]), products)
            for place, r in enumerate(job["numbers"]):
                number = info[1] ^ r
                blocks = [v for ref in products for v in cut_product(ref, number, batch)]
                for n, block in enumerate(blocks):
                    put(outs, job["targets"], place * len(blocks) + n, block.astype(BF))
        else:
            sources = [(ready(ins[n]), first) for n, first in job["sources"]]
            size = job.get("size")
            if job["kind"] == "fold":
                for n in range(size):
                    total = None
                    for ref, first in sources:
                        value = ref[first + n].astype(F32)
                        total = value if total is None else total + value
                    put(outs, job["targets"], n, total.astype(BF))
            elif job["kind"] == "join":
                for m, (ref, first) in enumerate(sources):
                    for n in range(size):
                        put(outs, job["targets"], m * size + n, ref[first + n])
            else:
                width = job["width"]
                finals = [outs[n] for n in job["finals"]]
                for (ref, first), numbers in zip(sources, job["numbers"]):
                    for place, r in enumerate(numbers):
                        start = first + place * width
                        place_chunk(
                            [ref[start + n] for n in range(width)], finals, job["layout"], info[1] ^ r
                        )


def put(outs, targets, n, block):
    for out, place, first, count in targets:
        if first <= n < first + count:
            outs[out][place + n - first] = block


def solution(mesh):
    batch = mesh.shape["batch"]
    chan = mesh.shape["chan"]
    everyone = ("batch", "chan")
    devices = batch * chan
    half = chan // 2
    pair = (0, half)

    def swap(v, mask, axis="chan"):
        return lax.ppermute(v, axis, [(k, k ^ mask) for k in range(mesh.shape[axis])])

    def widen(found):
        found = dict(found)
        mask = half // 2
        while mask:
            for k in list(found):
                found[k ^ mask] = swap(found[k], mask)
            mask //= 2
        return [found[k] for k in range(chan)]

    def gather(v):
        return widen({0: v, half: swap(v, half)})

    def gather_direct(v):
        return [v] + [swap(v, k) for k in range(1, chan)]

    def deliver(pieces):
        return [pieces[0]] + [swap(pieces[k], k) for k in range(1, chan)]

    def exchange(stats):
        return lax.all_to_all(stats, everyone, 0, 0)

    def exchange_batch(stats):
        return lax.all_to_all(stats, "batch", 0, 0)

    def cut(v, axis):
        size = v.shape[axis] // chan
        me = lax.axis_index("chan")
        return [lax.dynamic_slice_in_dim(v, (me ^ k) * size, size, axis) for k in range(chan)]

    sizes, units = radices_of(batch)
    levels = len(sizes)

    class Gradient:
        def __init__(self, compute, ins, products, layout, shapes, close=()):
            self.compute, self.ins, self.products = compute, ins, products
            self.layout, self.shapes = layout, shapes
            self.width = sum(math.prod(v) for v in products) // (MID * LANES)
            self.close = close
            self.started = 0
            self.result = None

        def partners(self, step):
            level = step if step < levels else 2 * levels - 1 - step
            return [m * units[level] for m in range(1, sizes[level])]

    def slot(info, gradients, last):
        ins, outs, scratch, jobs = [], [], [], []
        bundles = {}
        received = [v for g in gradients if g.started for v, _ in g.got] + [
            g.kept for g in gradients if g.started
        ] + [v for g in gradients if not g.started for v in g.close]
        size = MID // batch

        def give(array):
            for n, v in enumerate(ins):
                if v is array:
                    return n
            ins.append(array)
            return len(ins) - 1

        for g in gradients:
            job = {"targets": []}
            if not g.started:
                job.update(kind="pack", compute=g.compute, numbers=numbers_of(sizes, units))
                job["ins"] = [give(v) for v in g.ins]
                total = batch * g.width
            else:
                done = g.started - 1
                sources = [(give(g.kept), 0)] + [(give(v), first) for v, first in g.got]
                if done < levels:
                    total = g.amount
                    job.update(kind="fold", sources=sources, size=total)
                elif g.started < 2 * levels:
                    total = g.amount * len(sources)
                    job.update(kind="join", sources=sources, size=g.amount)
                    masks = [0] + g.partners(done)
                    g.numbers = [r ^ m for m in masks for r in g.numbers]
                else:
                    masks = [0] + g.partners(done)
                    job.update(kind="place", sources=sources, layout=g.layout, width=g.width)
                    job["numbers"] = [[r ^ m for r in g.numbers] for m in masks]
                    job["finals"] = g
                    jobs.append((g, job, None))
                    continue
            jobs.append((g, job, total))
        for g, job, total in jobs:
            if total is None:
                job["finals"] = list(range(len(outs), len(outs) + len(g.shapes)))
                outs += [(v, F32, "far") for v in g.shapes]
                continue
            step = g.started
            masks = g.partners(step)
            if step < levels:
                share = total // (len(masks) + 1)
                firsts = [share * m for m in range(len(masks) + 1)]
            else:
                share = total
                firsts = [0] * (len(masks) + 1)
                if step == levels:
                    g.numbers = [0]
            g.amount = share
            job["targets"].append((len(outs), 0, firsts[0], share))
            g.kept = len(outs)
            outs.append(((share, size, LANES), BF))
            g.next = []
            for mask, first in zip(masks, firsts[1:]):
                place = bundles.get(mask, 0)
                g.next.append((mask, place))
                bundles[mask] = place + share
                job["targets"].append((mask, place, first, share))
        order = sorted(bundles)
        where = {mask: len(outs) + n for n, mask in enumerate(order)}
        outs += [((bundles[mask], size, LANES), BF) for mask in order]
        for g, job, total in jobs:
            if total is not None:
                job["targets"] = [job["targets"][0]] + [(where[v[0]], *v[1:]) for v in job["targets"][1:]]
            if job["kind"] == "pack":
                job["products"] = list(range(len(outs) + len(scratch), len(outs) + len(scratch) + len(g.products)))
                scratch += [(v, F32) for v in g.products]
        plan = {"ins": len(ins), "jobs": [job for _, job, _ in jobs]}
        given = [v if any(v is w for w in received) else far(v) for v in ins]
        made = in_vmem(
            functools.partial(slot_kernel, batch, chan, plan),
            [info, *given],
            outs,
            scratch,
            after=[last],
            cost=SLOT_COST,
        )
        moved = {mask: swap(made[where[mask]], mask, "batch") for mask in order}
        for g, job, total in jobs:
            if total is None:
                g.result = [made[n] for n in job["finals"]]
            else:
                g.kept = made[g.kept]
                g.got = [(moved[mask], place) for mask, place in g.next]
                g.started += 1
        return made[0] if len(outs[0]) == 2 else far(made[0])

    def local(
        entry_activation,
        image_bounds,
        loss_sensitivity,
        first_contract_kernel,
        first_strided_kernel,
        first_enlarge_kernel,
        projection_kernel,
        second_contract_kernel,
        second_spatial_kernel,
        second_enlarge_kernel,
        bottleneck_gains,
        bottleneck_biases,
        wide_gain_vector,
        wide_bias_vector,
    ):
        images, side, _, quarter = entry_activation.shape
        small = side // 2
        wide = first_enlarge_kernel.shape[1]
        blocks = wide // LANES
        rows, large = small * CHUNK, side * LINE
        depth = quarter * chan
        mid = first_contract_kernel.shape[1] * chan
        assert mid == MID and images == IMAGES and side == SIDE
        piece, full, line = ((rows, LANES), BF), ((rows, wide), BF), ((large, LANES), BF)
        f32s = lambda *shape: (shape, F32)

        info = jnp.concatenate(
            [lax.axis_index("chan")[None], lax.axis_index("batch")[None], image_bounds.T.reshape(-1)]
        ).astype(jnp.int32)
        own = entry_activation.transpose(1, 2, 0, 3).reshape(large, quarter)
        found = {0: own, half: swap(own, half)}
        mask = half // 2
        while mask:
            found[mask] = swap(own, mask)
            mask //= 2
        table = jnp.concatenate(
            [
                bottleneck_gains,
                bottleneck_biases,
                wide_gain_vector.reshape(-1, LANES),
                wide_bias_vector.reshape(-1, LANES),
            ]
        )
        tabs = jnp.stack(gather_direct(table))
        loss = loss_sensitivity.transpose(1, 2, 0, 3)

        early_ks, late_ks = range(half), range(half, chan)
        (z1_part,) = in_vmem(
            functools.partial(first_part_kernel, chan, early_ks),
            [far(first_contract_kernel), info, *[found[k] for k in early_ks]],
            [f32s(large, LANES)],
        )
        found[half] = held_back(found[half], [z1_part])
        mask = half // 2
        while mask:
            found[half ^ mask] = swap(found[half], mask)
            mask //= 2
        source = [found[k] for k in range(chan)]
        z1, stats1 = in_vmem(
            functools.partial(first_kernel, chan, late_ks),
            [far(first_contract_kernel), info, z1_part, *source[half:]],
            [line, f32s(devices, 4, LANES)],
            [f32s(large, LANES)],
        )
        got1 = exchange(stats1)
        z1_far = swap(z1, pair[1])
        even, zs, stats_s, *source_far = in_vmem(
            functools.partial(shortcut_kernel, chan),
            [far(projection_kernel), info, *source],
            [((rows, depth), BF, "far"), (*full, "far"), f32s(2 * blocks, LANES)],
            [f32s(rows, wide)],
            save=range(2, 2 + chan),
        )
        zs_far = swap(zs, pair[1])
        *acts, norms1, counts, z1 = in_vmem(
            functools.partial(first_act_kernel, batch, chan, pair),
            [info, got1, z1, z1_far, tabs],
            [line, line, f32s(8, LANES), f32s(8, LANES)],
            after=[far(zs)],
            save=[2],
        )
        acts = widen(dict(zip(pair, acts)))
        a1, z2, stats2 = in_vmem(
            functools.partial(strided_kernel, chan),
            [far(first_strided_kernel), info, *acts, stats_s],
            [((3, 2, rows + CHUNK, mid), BF, "far"), piece, f32s(devices, 16, LANES)],
            [f32s(rows, LANES)],
        )
        got2 = exchange(stats2)
        near2 = gather_direct(z2)
        a2, z3, stats3, norms2, got2, *near2 = in_vmem(
            functools.partial(enlarge_kernel, batch, chan),
            [far(first_enlarge_kernel), info, got2, *near2, tabs, counts],
            [((rows, mid), BF, "far"), full, f32s(devices, 2 * blocks, LANES), f32s(2 * chan, LANES)],
            [f32s(rows, wide)],
            save=range(2, 3 + chan),
        )
        got3 = exchange(stats3)
        z3_far = swap(z3, pair[1])
        *y1, y1_own, norms3, z3 = in_vmem(
            functools.partial(merge_act_kernel, batch, chan, pair),
            [info, got3, far(got2), z3, z3_far, far(zs), far(zs_far), tabs, counts],
            [full, full, ((rows, wide), F32, "far"), f32s(4 * blocks, LANES)],
            save=[3],
        )
        y1 = widen(dict(zip(pair, y1)))
        z4, stats4, *y1 = in_vmem(
            functools.partial(contract_kernel, chan),
            [far(second_contract_kernel), info, *y1],
            [piece, f32s(devices, 2, LANES)],
            [f32s(rows, LANES)],
            save=range(2, 2 + chan),
        )

        got4 = exchange(stats4)
        near4 = gather_direct(z4)
        a4, z5, stats5, norms4, *near4 = in_vmem(
            functools.partial(spatial_kernel, batch, chan),
            [far(second_spatial_kernel), info, got4, *near4, tabs, counts],
            [((rows, mid), BF, "far"), piece, f32s(devices, 2, LANES), f32s(2 * chan, LANES)],
            [((3, rows + 2 * CHUNK, mid), BF), f32s(rows, LANES)],
            save=range(3, 3 + chan),
        )
        got5 = exchange(stats5)
        near5 = gather_direct(z5)
        a5, z6, stats6, norms5, *near5 = in_vmem(
            functools.partial(last_kernel, batch, chan),
            [far(second_enlarge_kernel), info, got5, *near5, tabs, counts],
            [
                ((rows, mid), BF, "far"),
                f32s(rows, wide),
                f32s(batch, 2 * blocks, LANES),
                f32s(2 * chan, LANES),
            ],
            save=range(3, 3 + chan),
        )
        got6 = exchange_batch(stats6)
        w1t = deliver(cut(first_contract_kernel, 0))
        w2t = deliver(cut(first_strided_kernel, 2))
        wpt = deliver(cut(projection_kernel, 0))
        w4t = deliver(cut(second_contract_kernel, 0))
        result, g2, stats7, norms6, z6 = in_vmem(
            output_kernel,
            [info, got6, z6, far(y1_own), far(loss), tabs, counts],
            [
                ((small, small, images, wide), BF, "far"),
                f32s(rows, wide),
                f32s(batch, 2 * blocks, LANES),
                f32s(2 * blocks, LANES),
            ],
            save=[2],
        )

        shares = [f32s(rows, LANES)] + [piece] * (chan - 1)
        routed = f32s(devices, 2, LANES)
        tap_lanes = 9 * LANES
        got7 = exchange_batch(stats7)
        dz6, *sent, stats8, sums6, g2 = in_vmem(
            functools.partial(back_last_kernel, batch, chan),
            [far(second_enlarge_kernel), info, got7, g2, far(z6), norms6, tabs, counts, *fars(near5), norms5],
            [(*full, "far"), *shares, routed, f32s(2 * blocks, LANES)],
            [f32s(rows, mid)],
            after=fars([*w2t, *w1t, *w4t]),
            save=[3],
        )
        got8 = exchange(stats8)
        parts = deliver(sent)
        spread5, *sent, stats9, sums5 = in_vmem(
            functools.partial(back_spatial_kernel, batch, chan),
            [
                far(second_spatial_kernel), info, got8, *parts, far(near5[0]), norms5, tabs, counts,
                *fars(near4), norms4,
            ],
            [((rows, tap_lanes), BF, "far"), *shares, routed, f32s(8, LANES)],
            [((3, rows + 2 * CHUNK, LANES), BF), f32s(rows, mid)],
            after=fars(wpt),
        )
        got9 = exchange(stats9)
        parts = deliver(sent)
        work = {}

        def slots(point, last):
            for names in SLOTS[point]:
                some = [work[n] for n in names if n in work and work[n].result is None]
                if some:
                    last = slot(info, some, last)
            return last

        work["early"] = Gradient(
            early_products,
            [a5, dz6, a4, spread5],
            [(mid, wide), (mid, tap_lanes)],
            ((1, 1), (9, 1)),
            [(mid, wide), (9, mid, LANES)],
        )
        last = slots("fifth", stats9)
        dz4, sums4, dz4_far = in_vmem(
            back_contract_kernel,
            [info, got9, *parts, far(near4[0]), norms4, tabs, counts],
            [piece, f32s(8, LANES), (*piece, "far")],
            after=[last],
        )
        dz4_all = gather_direct(dz4)
        work["narrowing"] = Gradient(
            rows_products, [*y1, dz4_far], [(wide * chan, LANES)], ((1, 4),), [(wide * chan, LANES)]
        )
        last = slots("fourth", dz4)
        g1, stats10 = in_vmem(
            functools.partial(back_merge_kernel, chan),
            [info, *dz4_all, *fars(w4t), far(g2), far(z3), far(zs), norms3, tabs],
            [f32s(rows, wide), f32s(batch, 4 * blocks, LANES)],
            [f32s(rows, wide)],
            after=[last],
        )
        got10 = exchange_batch(stats10)
        last = slots("merge", stats10)
        dz3, dzs, *sent, stats11, sums3 = in_vmem(
            functools.partial(back_enlarge_kernel, batch, chan),
            [
                far(first_enlarge_kernel), info, got10, g1, far(z3), far(zs), norms3, tabs, counts,
                *fars(near2), norms2,
            ],
            [(*full, "far"), (*full, "far"), *shares, routed, f32s(4 * blocks, LANES)],
            [f32s(rows, mid)],
            after=[last],
        )
        got11 = exchange(stats11)
        parts = deliver(sent)
        work["widening"] = Gradient(
            wide_products,
            [a2, dz3, even, dzs],
            [(mid, wide), (depth, wide)],
            ((1, 1), (1, 2)),
            [(mid, wide), (depth, wide)],
        )
        last = slots("third", stats11)
        last = slots("shares", got11) if SLOTS["shares"] else last
        dz2, moved2, sums2 = in_vmem(
            back_strided_kernel,
            [info, got11, *parts, far(near2[0]), norms2, tabs, counts],
            [piece, ((rows, 4 * LANES), BF, "far"), f32s(8, LANES)],
            [((2, rows + CHUNK, LANES), BF)],
            after=[last],
        )
        dz2_all = gather_direct(dz2)
        last = slots("second", dz2)
        u1, stats12 = in_vmem(
            functools.partial(back_first_kernel, chan),
            [info, *dz2_all, *fars(w2t), far(z1), norms1, tabs],
            [f32s(large, LANES), f32s(batch, 2, LANES)],
            [((2, rows + CHUNK, mid), BF), ((3, 3, LANES, mid), BF), f32s(2, rows, LANES)],
            after=[last],
        )
        got12 = exchange_batch(stats12)
        work["strided"] = Gradient(
            strided_products, [a1, moved2], [(mid, tap_lanes)], ((9, 1),), [(9, mid, LANES)]
        )
        last = slots("strided", stats12)
        dz1, sums1 = in_vmem(
            back_first_own_kernel,
            [info, got12, u1, far(z1), norms1, tabs, counts],
            [line, f32s(8, LANES)],
            after=[last],
        )
        dz1_all = gather(dz1)
        dzs_all = gather(dzs)
        work["reducing"] = Gradient(
            rows_products, [*source_far, dz1], [(depth, LANES)], ((1, 2),), [(depth, LANES)], [dz1]
        )
        last = slots("first", dz1)
        (inputs_grad,) = in_vmem(
            functools.partial(leave_kernel, chan),
            [info, *dz1_all, *fars(dzs_all), *fars(w1t), *fars(wpt)],
            [((side, side, images, quarter), BF, "far")],
            [f32s(large, quarter), f32s(rows, quarter)],
            after=[last],
            cost=LEAVE_COST,
        )
        last = slots("end", far(inputs_grad))
        while any(g.result is None for g in work.values()):
            last = slot(info, [g for g in work.values() if g.result is None], last)
        early, narrowing, widening, strided, reducing = (
            work[name] for name in ("early", "narrowing", "widening", "strided", "reducing")
        )
        (expanding_grad, middle_grad), (narrowing_grad,) = early.result, narrowing.result
        (widening_grad, shortcut_grad), (spatial_grad,), (reducing_grad,) = (
            g.result for g in (widening, strided, reducing)
        )
        tapped = (3, 3, mid, LANES)
        gains3, gains_s, shift3 = (sums3[n * blocks : (n + 1) * blocks].reshape(-1) for n in range(3))
        gains6, shift6 = sums6[:blocks].reshape(-1), sums6[blocks:].reshape(-1)
        return (
            result.transpose(2, 0, 1, 3),
            inputs_grad.transpose(2, 0, 1, 3),
            reducing_grad,
            spatial_grad.reshape(tapped),
            widening_grad,
            shortcut_grad,
            narrowing_grad,
            middle_grad.reshape(tapped),
            expanding_grad,
            jnp.stack([sums1[0], sums2[0], sums4[0], sums5[0]]),
            jnp.stack([sums1[1], sums2[1], sums4[1], sums5[1]]),
            jnp.stack([gains3, gains_s, gains6]),
            jnp.stack([shift3, shift3, shift6]),
        )

    wide_act = P("batch", None, None, "chan")
    cols = P(None, "chan")
    taps = P(None, None, None, "chan")
    return jax.shard_map(
        local,
        mesh=mesh,
        in_specs=(wide_act, P("batch", None), wide_act, cols, taps, cols, cols, cols, taps)
        + (cols,) * 5,
        out_specs=(wide_act, wide_act, cols, taps, cols, cols, cols, taps) + (cols,) * 5,
        check_vma=False,
    )
```

```python
import functools
import math

import jax
import jax.numpy as jnp
from jax import lax
from jax.experimental import pallas as pl
from jax.experimental.pallas import tpu as pltpu
from jax.sharding import PartitionSpec as P

EPS = 1e-05
BF = jnp.bfloat16
F32 = jnp.float32
GELU_A = 0.7978845608028654
GELU_B = 0.044715
LANES = 128
MID = 512
SIDE = 14
IMAGES = 8
CELLS = 8
CHUNK = CELLS * IMAGES
LINE = SIDE * IMAGES
SLOT_COST = 10**6
LEAVE_COST = 10**6
STEP_COST = 4 * 10**9
SLOTS = {
    "fifth": [["early"]],
    "fourth": [["narrowing"]],
    "merge": [["early", "narrowing"]],
    "third": [["widening"]],
    "shares": [],
    "second": [["early", "narrowing"]],
    "strided": [["strided", "widening"], ["early", "narrowing"]],
    "first": [["reducing"], ["strided"]],
    "end": [["widening"], ["strided"], ["early", "narrowing", "reducing"], ["widening"], ["strided"], ["reducing"], ["widening"], ["reducing"], ["strided"]],
}
VMEM_LIMIT = 20 * 1024 * 1024


def dot(a, b, dims=((1,), (0,))):
    return lax.dot_general(a, b, (dims, ((), ())), preferred_element_type=F32)


def gelu(v):
    return 0.5 * v * (1.0 + jnp.tanh(GELU_A * v * (1.0 + GELU_B * v * v)))


def gelu_slope(v):
    square = v * v
    t = jnp.tanh(GELU_A * v * (1.0 + GELU_B * square))
    return 0.5 * (1.0 + t) * (1.0 + v * (1.0 - t) * (GELU_A + 3.0 * GELU_A * GELU_B * square))


class Masks:
    def __init__(self, info):
        image = lax.broadcasted_iota(jnp.int32, (IMAGES, LANES), 0)
        high = jnp.zeros((IMAGES, LANES), jnp.int32)
        low = jnp.zeros((IMAGES, LANES), jnp.int32)
        inside = jnp.int32(0)
        outside = jnp.int32(0)
        for n in range(IMAGES):
            h, w = info[2 + n], info[2 + IMAGES + n]
            high = jnp.where(image == n, h, high)
            low = jnp.where(image == n, w, low)
            inside = inside + h * w
            outside = outside + lax.shift_right_logical(h + 1, 1) * lax.shift_right_logical(w + 1, 1)
        self.high = high[None]
        self.low = low[None]
        self.column = lax.broadcasted_iota(jnp.int32, (2 * CELLS, IMAGES, LANES), 0)
        self.local_in = inside.astype(F32)
        self.local_out = outside.astype(F32)

    def large(self, row):
        return (row < self.high) & (self.column[:SIDE] < self.low)

    def small(self, row):
        return (2 * row < self.high) & (2 * self.column[:CELLS] < self.low)


def repeat(count, step, init):
    return lax.fori_loop(0, count, step, init, unroll=count if count <= 7 else 2)


def keep(mask, value):
    return jnp.where(mask, value, 0.0)


def cube(rows):
    return rows.astype(F32).reshape(-1, IMAGES, LANES)


def flat(value):
    return value.reshape(-1, LANES)


def padded(value):
    return jnp.concatenate([value, jnp.zeros((1,) + value.shape[1:], F32)], axis=0)


def parted(value):
    pairs = value.reshape(CELLS - 1, 2, *value.shape[1:])
    return padded(pairs[:, 0]), padded(pairs[:, 1])


def merged(even, odd):
    pairs = jnp.stack([even[: CELLS - 1], odd[: CELLS - 1]], axis=1)
    return pairs.reshape(SIDE, *even.shape[1:])


def total_of(value):
    return jnp.sum(value, axis=0)


def row_sum(value):
    return jnp.sum(value, axis=0, keepdims=True)


def at(step, size):
    return pl.ds(pl.multiple_of(step * size, size), size)


def lane_block(index, width=LANES):
    return pl.ds(pl.multiple_of(index * width, width), width)


def push_left(value):
    return jnp.concatenate([value[1:], jnp.zeros((1, IMAGES, LANES), F32)], axis=0)


def push_right(value):
    return jnp.concatenate([jnp.zeros((1, IMAGES, LANES), F32), value[:-1]], axis=0)


def norm_of(got, info, batch, chan, k, row, local, count):
    column = info[0] ^ k
    total = got[column]
    for n in range(1, batch):
        total = total + got[n * chan + column]
    mine = got[info[1] * chan + column]
    mean = total[row : row + 1] / count
    inverse = lax.rsqrt(total[row + 1 : row + 2] / count - mean * mean + EPS)
    return mine[row : row + 1] / local - mean, inverse


def whole(got):
    total = got[0]
    for n in range(1, got.shape[0]):
        total = total + got[n]
    return total


class Late:
    def __init__(self, source, held, semaphore):
        self.copy = pltpu.make_async_copy(source, held, semaphore)
        self.held = held
        self.waiting = True
        self.copy.start()

    def use(self):
        if self.waiting:
            self.copy.wait()
            self.waiting = False
        return self.held


class Far:
    def __init__(self, held, target, semaphore):
        self.copy = pltpu.make_async_copy(held, target, semaphore)
        self.held = held
        self.sent = False
        self.shape = held.shape
        self.dtype = held.dtype

    def __getitem__(self, place):
        return self.held[place]

    def __setitem__(self, place, value):
        self.held[place] = value

    def send(self):
        self.sent = True
        self.copy.start()


def ready(value):
    if isinstance(value, (list, tuple)):
        return [ready(v) for v in value]
    return value.use() if isinstance(value, Late) else value


class far:
    def __init__(self, value):
        self.value = value


def fars(values):
    return [far(v) for v in values]


def in_vmem(kernel, ins, outs, scratch=(), after=(), save=(), cost=None):
    anywhere = pl.BlockSpec(memory_space=pl.ANY)
    inside = pl.BlockSpec(memory_space=pltpu.VMEM)
    args = [
        pltpu.with_memory_space_constraint(v.value, pltpu.HBM)
        if isinstance(v, far)
        else pltpu.with_memory_space_constraint(v, pltpu.VMEM)
        for v in after
    ]
    specs, late, buffers = [anywhere] * len(after), [], []
    for n, v in enumerate(ins):
        if isinstance(v, far):
            late.append(n)
            buffers.append(pltpu.VMEM(v.value.shape, v.value.dtype))
            args.append(pltpu.with_memory_space_constraint(v.value, pltpu.HBM))
            specs.append(anywhere)
        elif v.dtype == jnp.int32:
            args.append(v)
            specs.append(pl.BlockSpec(memory_space=pltpu.SMEM))
        else:
            args.append(pltpu.with_memory_space_constraint(v, pltpu.VMEM))
            specs.append(inside)
    distant = [n for n, out in enumerate(outs) if len(out) > 2]
    buffers += [pltpu.VMEM(*outs[n][:2]) for n in distant]
    shapes = [(pltpu.HBM if len(out) > 2 else pltpu.VMEM)(*out[:2]) for out in outs]
    shapes += [pltpu.HBM(ins[n].shape, ins[n].dtype) for n in save]
    out_specs = [anywhere if len(out) > 2 else inside for out in outs] + [anywhere] * len(save)
    semaphores = len(buffers) + len(save)

    def body(*refs):
        refs = list(refs[len(after) :])
        given, refs = refs[: len(ins)], refs[len(ins) :]
        made, refs = refs[: len(outs)], refs[len(outs) :]
        saved, refs = refs[: len(save)], refs[len(save) :]
        free, refs = refs[: len(scratch)], refs[len(scratch) :]
        held, marks = refs[: len(buffers)], refs[len(buffers) :]
        for place, n in enumerate(late):
            given[n] = Late(given[n], held[place], marks[place])
        for place, n in enumerate(distant, len(late)):
            made[n] = Far(held[place], made[n], marks[place])
        copies = [
            pltpu.make_async_copy(given[n], out, mark)
            for n, out, mark in zip(save, saved, marks[len(buffers) :])
        ]
        for copy in copies:
            copy.start()
        kernel(*given, *made, *free)
        for n in distant:
            if not made[n].sent:
                made[n].send()
        for n in late:
            given[n].use()
        for n in distant:
            made[n].copy.wait()
        for copy in copies:
            copy.wait()

    return pl.pallas_call(
        body,
        out_shape=shapes,
        in_specs=specs,
        out_specs=out_specs,
        scratch_shapes=[pltpu.VMEM(*v) for v in scratch] + buffers + [pltpu.SemaphoreType.DMA] * semaphores,
        compiler_params=pltpu.CompilerParams(vmem_limit_bytes=VMEM_LIMIT),
        cost_estimate=pl.CostEstimate(flops=cost or STEP_COST, bytes_accessed=0, transcendentals=0),
    )(*args)


def held_back(value, after):
    def body(*refs):
        del refs

    args = [pltpu.with_memory_space_constraint(v, pltpu.VMEM) for v in (value, *after)]
    anywhere = pl.BlockSpec(memory_space=pl.ANY)
    return pl.pallas_call(
        body,
        out_shape=pltpu.VMEM(value.shape, value.dtype),
        in_specs=[anywhere] * len(args),
        out_specs=anywhere,
        input_output_aliases={0: 0},
    )(*args)


def sums_of(z, chunks, lanes, mask=None, size=CHUNK):
    def step(t, carry):
        value = cube(z[at(t, size), lanes])
        if mask is not None:
            value = keep(mask(t), value)
        return carry[0] + total_of(value), carry[1] + total_of(value * value)

    zero = jnp.zeros((IMAGES, LANES), F32)
    total, squares = repeat(chunks, step, (zero, zero))
    return row_sum(total), row_sum(squares)


def centre_into(out, z, chunks, lanes, mean, size=CHUNK):
    def step(t, _):
        out[at(t, size), lanes] = (z[at(t, size), lanes] - mean).astype(BF)
        return 0

    repeat(chunks, step, 0)


def broadcast_rows(out, rows):
    block = jnp.concatenate(
        list(rows) + [jnp.zeros((out.shape[1] - len(rows), LANES), F32)]
        if len(rows) < out.shape[1]
        else list(rows),
        axis=0,
    )
    out[...] = jnp.broadcast_to(block[None], out.shape)


def fill_rows(out, rows):
    for n, row in enumerate(rows):
        out[n : n + 1, :] = row
    if len(rows) < out.shape[0]:
        out[len(rows) :, :] = jnp.zeros((out.shape[0] - len(rows), LANES), F32)


def first_part_kernel(chan, ks, w, info, *refs):
    source, (z,) = refs[: len(ks)], refs[len(ks) :]
    rows, depth = source[0].shape
    part = 2 * LINE
    w = w.use()

    def step(t, _):
        total = None
        for n, k in enumerate(ks):
            term = dot(source[n][at(t, part), :], w[at(info[0] ^ k, depth), :])
            total = term if total is None else total + term
        z[at(t, part), :] = total
        return 0

    repeat(rows // part, step, 0)


def first_kernel(chan, ks, w, info, part_z, *refs):
    source, (zc, stats, z) = refs[: len(ks)], refs[len(ks) :]
    masks = Masks(info)
    rows, depth = source[0].shape
    part = 2 * LINE
    w = w.use()

    def step(t, _):
        total = part_z[at(t, part), :]
        for n, k in enumerate(ks):
            total = total + dot(source[n][at(t, part), :], w[at(info[0] ^ k, depth), :])
        z[at(t, part), :] = total
        return 0

    repeat(rows // part, step, 0)
    total, squares = sums_of(z, SIDE, slice(0, LANES), masks.large, LINE)
    ones = jnp.ones((1, LANES), F32)
    broadcast_rows(stats, (total, squares, ones * masks.local_in, ones * masks.local_out))
    centre_into(zc, z, SIDE, slice(0, LANES), total / masks.local_in, LINE)


def shortcut_kernel(chan, w, info, *refs):
    source, (even, zc, stats, z) = refs[:chan], refs[chan:]
    masks = Masks(info)
    rows, width = z.shape
    depth = source[0].shape[1]
    chunks = rows // CHUNK

    def step(i, _):
        for k in range(chan):
            for q in range(depth // LANES):
                lanes = slice(q * LANES, (q + 1) * LANES)
                value, _ = parted(cube(source[k][at(2 * i, LINE), lanes]))
                place = lane_block((info[0] ^ k) * (depth // LANES) + q)
                even[at(i, CHUNK), place] = flat(value).astype(BF)
        return 0

    repeat(chunks, step, 0)
    even.send()
    z[...] = dot(even[...], w.use()[...])
    blocks = width // LANES
    for q in range(blocks):
        lanes = slice(q * LANES, (q + 1) * LANES)
        total, squares = sums_of(z, chunks, lanes, masks.small)
        stats[q : q + 1, :] = total
        stats[blocks + q : blocks + q + 1, :] = squares
        centre_into(zc, z, chunks, lanes, total / masks.local_out)


def first_act_kernel(batch, chan, pair, info, got, *refs):
    near, (tabs, *outs, norms, counts) = refs[: len(pair)], refs[len(pair) :]
    masks = Masks(info)
    total = whole(got)
    count_in, count_out = total[2:3] / chan, total[3:4] / chan
    fill_rows(counts, (count_in, count_out))
    params = [norm_of(got, info, batch, chan, k, 0, masks.local_in, count_in) for k in pair]
    norms[0:1, :] = params[0][0]
    norms[1:2, :] = params[0][1]

    def step(r, _):
        mask = masks.large(r)
        for n, k in enumerate(pair):
            scale = params[n][1] * tabs[k, 0:1, :]
            shift = params[n][0] * scale + tabs[k, 4:5, :]
            value = keep(mask, gelu(cube(near[n][at(r, LINE), :]) * scale + shift))
            outs[n][at(r, LINE), :] = flat(value).astype(BF)
        return 0

    repeat(SIDE, step, 0)


def strided_kernel(chan, w, info, *refs):
    pieces, (extra, a, zc, stats, z) = refs[:chan], refs[chan:]
    masks = Masks(info)
    width = a.shape[3]
    for tap in range(3):
        a[tap, 0, 0:CHUNK, :] = jnp.zeros((CHUNK, width), BF)

    def step(r, _):
        line = r + 1
        half, place = line & 1, lax.shift_right_logical(line, 1)
        for k in range(chan):
            lanes = lane_block(info[0] ^ k)
            even, odd = parted(cube(pieces[k][at(r, LINE), :]))
            a[0, half, at(place, CHUNK), lanes] = flat(push_right(odd)).astype(BF)
            a[1, half, at(place, CHUNK), lanes] = flat(even).astype(BF)
            a[2, half, at(place, CHUNK), lanes] = flat(odd).astype(BF)
        return 0

    repeat(SIDE, step, 0)
    a.send()
    rows = z.shape[0]
    acc = None
    w = w.use()
    for i, (half, first) in enumerate(((0, 0), (1, 0), (0, CHUNK))):
        for j in range(3):
            term = dot(a[j, half, first : first + rows, :], w[i, j])
            acc = term if acc is None else acc + term
    z[...] = acc
    chunks = rows // CHUNK
    total, squares = sums_of(z, chunks, slice(0, LANES), masks.small)
    block = jnp.concatenate([total, squares, jnp.zeros((6, LANES), F32), extra[...]], axis=0)
    stats[...] = jnp.broadcast_to(block[None], stats.shape)
    centre_into(zc, z, chunks, slice(0, LANES), total / masks.local_out)


def activate_into(near, params, tabs, gain, chan, info, masks, chunks, store):
    def step(t, _):
        mask = masks.small(t)
        for k in range(chan):
            scale = params[k][1] * tabs[k, gain : gain + 1, :]
            shift = params[k][0] * scale + tabs[k, gain + 4 : gain + 5, :]
            value = keep(mask, gelu(cube(near[k][at(t, CHUNK), :]) * scale + shift))
            store(t, lane_block(info[0] ^ k), value)
        return 0

    repeat(chunks, step, 0)


def store_norms(norms, params):
    for k, norm in enumerate(params):
        norms[2 * k : 2 * k + 1, :] = norm[0]
        norms[2 * k + 1 : 2 * k + 2, :] = norm[1]


def enlarge_kernel(batch, chan, w, info, got, *refs):
    near, (tabs, counts, a, zc, stats, norms, z) = refs[:chan], refs[chan:]
    masks = Masks(info)
    count = counts[1:2, :]
    params = [norm_of(got, info, batch, chan, k, 0, masks.local_out, count) for k in range(chan)]
    store_norms(norms, params)
    chunks = z.shape[0] // CHUNK

    def store(t, lanes, value):
        a[at(t, CHUNK), lanes] = flat(value).astype(BF)

    activate_into(near, params, tabs, 1, chan, info, masks, chunks, store)
    a.send()
    z[...] = dot(a[...], w.use()[...])
    rows = wide_sums(z, zc, chunks, masks)
    broadcast_rows(stats, rows)


def wide_sums(z, zc, chunks, masks):
    blocks = z.shape[1] // LANES
    totals, squares = [], []
    for q in range(blocks):
        lanes = slice(q * LANES, (q + 1) * LANES)
        total, square = sums_of(z, chunks, lanes)
        totals.append(total)
        squares.append(square)
        if zc is not None:
            centre_into(zc, z, chunks, lanes, total / masks.local_out)
    return totals + squares


def wide_norm(got, info, batch, chan, k, row, blocks, local, count):
    column = info[0] ^ k
    total = got[column]
    for n in range(1, batch):
        total = total + got[n * chan + column]
    mine = got[info[1] * chan + column]
    mean = total[row : row + blocks] / count
    inverse = lax.rsqrt(total[row + blocks : row + 2 * blocks] / count - mean * mean + EPS)
    return mine[row : row + blocks] / local - mean, inverse


def merge_act_kernel(batch, chan, pair, info, got3, got2, *refs):
    size = len(pair)
    near3, nears = refs[:size], refs[size : 2 * size]
    tabs, counts, *outs, own, norms = refs[2 * size :]
    nears, got2 = ready(nears), ready(got2)
    masks = Masks(info)
    count = counts[1:2, :]
    rows, width = near3[0].shape
    blocks = width // LANES
    lines = []
    for k in pair:
        one = wide_norm(got3, info, batch, chan, k, 0, blocks, masks.local_out, count)
        two = wide_norm(got2, info, batch, chan, k, 8, blocks, masks.local_out, count)
        if k == 0:
            for n, value in enumerate(one + two):
                norms[n * blocks : (n + 1) * blocks, :] = value
        gain, bias = 8, 8 + 3 * blocks
        scale3 = one[1] * tabs[k, gain : gain + blocks, :]
        scales = two[1] * tabs[k, gain + blocks : gain + 2 * blocks, :]
        shift = (
            one[0] * scale3
            + two[0] * scales
            + tabs[k, bias : bias + blocks, :]
            + tabs[k, bias + blocks : bias + 2 * blocks, :]
        )
        lines.append((scale3, scales, shift))

    def step(t, _):
        mask = masks.small(t)
        for n, k in enumerate(pair):
            scale3, scales, shift = lines[n]
            for q in range(blocks):
                lanes = slice(q * LANES, (q + 1) * LANES)
                pre = (
                    cube(near3[n][at(t, CHUNK), lanes]) * scale3[q : q + 1]
                    + cube(nears[n][at(t, CHUNK), lanes]) * scales[q : q + 1]
                    + shift[q : q + 1]
                )
                value = flat(keep(mask, gelu(pre)))
                if k == 0:
                    own[at(t, CHUNK), lanes] = value
                outs[n][at(t, CHUNK), lanes] = value.astype(BF)
        return 0

    repeat(rows // CHUNK, step, 0)


def contract_kernel(chan, w, info, *refs):
    y, (zc, stats, z) = refs[:chan], refs[chan:]
    masks = Masks(info)
    rows, width = y[0].shape
    chunks = rows // CHUNK
    w = w.use()
    total = None
    for k in range(chan):
        term = dot(y[k][...], w[at(info[0] ^ k, width), :])
        total = term if total is None else total + term
    z[...] = total
    total, squares = sums_of(z, chunks, slice(0, LANES))
    broadcast_rows(stats, (total, squares))
    centre_into(zc, z, chunks, slice(0, LANES), total / masks.local_out)


def spatial_kernel(batch, chan, w, info, got, *refs):
    near, (tabs, counts, a, zc, stats, norms, held, z) = refs[:chan], refs[chan:]
    masks = Masks(info)
    count = counts[1:2, :]
    params = [norm_of(got, info, batch, chan, k, 0, masks.local_out, count) for k in range(chan)]
    store_norms(norms, params)
    rows, width = a.shape
    chunks = rows // CHUNK
    for tap in range(3):
        held[tap, 0:CHUNK, :] = jnp.zeros((CHUNK, width), BF)
        held[tap, rows + CHUNK : rows + 2 * CHUNK, :] = jnp.zeros((CHUNK, width), BF)

    def store(t, lanes, value):
        plain = flat(value).astype(BF)
        a[at(t, CHUNK), lanes] = plain
        held[1, at(t + 1, CHUNK), lanes] = plain
        held[0, at(t + 1, CHUNK), lanes] = flat(push_right(value)).astype(BF)
        held[2, at(t + 1, CHUNK), lanes] = flat(push_left(value)).astype(BF)

    activate_into(near, params, tabs, 2, chan, info, masks, chunks, store)
    a.send()
    acc = None
    w = w.use()
    for i in range(3):
        for j in range(3):
            term = dot(held[j, i * CHUNK : i * CHUNK + rows, :], w[i, j])
            acc = term if acc is None else acc + term
    z[...] = acc
    total, squares = sums_of(z, chunks, slice(0, LANES), masks.small)
    broadcast_rows(stats, (total, squares))
    centre_into(zc, z, chunks, slice(0, LANES), total / masks.local_out)


def last_kernel(batch, chan, w, info, got, *refs):
    near, (tabs, counts, a, z, stats, norms) = refs[:chan], refs[chan:]
    masks = Masks(info)
    count = counts[1:2, :]
    params = [norm_of(got, info, batch, chan, k, 0, masks.local_out, count) for k in range(chan)]
    store_norms(norms, params)
    chunks = a.shape[0] // CHUNK

    def store(t, lanes, value):
        a[at(t, CHUNK), lanes] = flat(value).astype(BF)

    activate_into(near, params, tabs, 3, chan, info, masks, chunks, store)
    a.send()
    z[...] = dot(a[...], w.use()[...])
    broadcast_rows(stats, wide_sums(z, None, chunks, masks))


def output_kernel(info, got, z, own, loss, tabs, counts, result, g, stats, norms):
    masks = Masks(info)
    own, loss = ready(own), ready(loss)
    count = counts[1:2, :]
    total = whole(got)
    rows, width = z.shape
    blocks = width // LANES
    chunks = rows // CHUNK
    mean = total[0:blocks] / count
    inverse = lax.rsqrt(total[blocks : 2 * blocks] / count - mean * mean + EPS)
    norms[0:blocks, :] = mean
    norms[blocks : 2 * blocks, :] = inverse
    gain = tabs[0, 8 + 2 * blocks : 8 + 3 * blocks, :]
    bias = tabs[0, 8 + 5 * blocks : 8 + 6 * blocks, :]
    small = result.shape[1]

    def step(t, carry):
        mask = masks.small(t)
        sums = []
        for q in range(blocks):
            lanes = slice(q * LANES, (q + 1) * LANES)
            zhat = (cube(z[at(t, CHUNK), lanes]) - mean[q : q + 1]) * inverse[q : q + 1]
            pre = zhat * gain[q : q + 1] + bias[q : q + 1] + cube(own[at(t, CHUNK), lanes])
            result[t, :, :, lanes] = keep(mask, gelu(pre))[:small].astype(BF)
            u = keep(mask, gelu_slope(pre)) * padded(loss[t, :, :, lanes].astype(F32))
            g[at(t, CHUNK), lanes] = flat(u)
            sums.append((carry[q][0] + total_of(u * zhat), carry[q][1] + total_of(u)))
        return tuple(sums)

    zero = jnp.zeros((IMAGES, LANES), F32)
    sums = repeat(chunks, step, ((zero, zero),) * blocks)
    broadcast_rows(stats, [row_sum(s[0]) for s in sums] + [row_sum(s[1]) for s in sums])


def share_stage(da, near, norms, tabs, gain, chan, batch, info, masks, chunks, pieces, stats):
    zero = jnp.zeros((IMAGES, LANES), F32)
    for k in range(chan):
        lanes = lane_block(info[0] ^ k)
        offset, inverse = norms[2 * k : 2 * k + 1, :], norms[2 * k + 1 : 2 * k + 2, :]
        scale, bias = tabs[k, gain : gain + 1, :], tabs[k, gain + 4 : gain + 5, :]

        def step(t, carry, k=k, lanes=lanes, offset=offset, inverse=inverse, scale=scale, bias=bias):
            share = da[at(t, CHUNK), lanes]
            zhat = (cube(near[k][at(t, CHUNK), :]) + offset) * inverse
            u = keep(masks.small(t), gelu_slope(zhat * scale + bias)) * cube(share)
            pieces[k][at(t, CHUNK), :] = share.astype(pieces[k].dtype)
            return carry[0] + total_of(u * zhat), carry[1] + total_of(u)

        first, second = repeat(chunks, step, (zero, zero))
        block = jnp.concatenate([row_sum(first), row_sum(second)], axis=0)
        for n in range(batch):
            stats[n * chan + (info[0] ^ k)] = block


def own_stage(got, parts, near, norms, tabs, gain, count, masks, chunks, sums, store):
    total = whole(got)
    gg, gb = total[0:1], total[1:2]
    fill_rows(sums, (gg, gb))
    offset, inverse = norms[0:1, :], norms[1:2, :]
    scale, bias = tabs[0, gain : gain + 1, :], tabs[0, gain + 4 : gain + 5, :]
    per_cell, per_hat = gb / count, gg / count
    front = scale * inverse

    def step(t, _):
        mask = masks.small(t)
        da = cube(parts[0][at(t, CHUNK), :])
        for part in parts[1:]:
            da = da + cube(part[at(t, CHUNK), :])
        zhat = (cube(near[at(t, CHUNK), :]) + offset) * inverse
        u = gelu_slope(zhat * scale + bias) * da
        store(t, keep(mask, front * (u - (per_cell + zhat * per_hat))))
        return 0

    repeat(chunks, step, 0)


def back_last_kernel(batch, chan, w, info, got, g, z, norms6, tabs, counts, *refs):
    near, (norms, dz, *pieces, stats, sums, da) = refs[:chan], refs[chan:]
    masks = Masks(info)
    z = ready(z)
    count = counts[1:2, :]
    total = whole(got)
    rows, width = z.shape
    blocks = width // LANES
    chunks = rows // CHUNK
    gg, gb = total[0:blocks] / count, total[blocks : 2 * blocks] / count
    sums[...] = total
    mean, inverse = norms6[0:blocks, :], norms6[blocks : 2 * blocks, :]
    front = tabs[0, 8 + 2 * blocks : 8 + 3 * blocks, :] * inverse

    def step(t, _):
        mask = masks.small(t)
        for q in range(blocks):
            lanes = slice(q * LANES, (q + 1) * LANES)
            zhat = (cube(z[at(t, CHUNK), lanes]) - mean[q : q + 1]) * inverse[q : q + 1]
            value = cube(g[at(t, CHUNK), lanes]) - (gb[q : q + 1] + zhat * gg[q : q + 1])
            dz[at(t, CHUNK), lanes] = flat(keep(mask, front[q : q + 1] * value)).astype(BF)
        return 0

    repeat(chunks, step, 0)
    dz.send()
    da[...] = dot(dz[...], w.use()[...], ((1,), (1,)))
    near = ready(near)
    share_stage(da, near, norms, tabs, 3, chan, batch, info, masks, chunks, pieces, stats)


def back_spatial_kernel(batch, chan, w, info, got, *refs):
    parts, refs = refs[:chan], refs[chan:]
    own, norms5, tabs, counts = refs[:4]
    near, (norms, spread, *pieces, stats, sums, held, da) = refs[4 : 4 + chan], refs[4 + chan :]
    masks = Masks(info)
    own = ready(own)
    rows = own.shape[0]
    chunks = rows // CHUNK
    for tap in range(3):
        held[tap, 0:CHUNK, :] = jnp.zeros((CHUNK, LANES), BF)
        held[tap, rows + CHUNK : rows + 2 * CHUNK, :] = jnp.zeros((CHUNK, LANES), BF)

    def store(t, value):
        held[1, at(t + 1, CHUNK), :] = flat(value).astype(BF)
        held[0, at(t + 1, CHUNK), :] = flat(push_left(value)).astype(BF)
        held[2, at(t + 1, CHUNK), :] = flat(push_right(value)).astype(BF)

    own_stage(got, parts, own, norms5, tabs, 3, counts[1:2, :], masks, chunks, sums, store)
    w = w.use()
    for i in range(3):
        for j in range(3):
            value = held[j, (2 - i) * CHUNK : (2 - i) * CHUNK + rows, :]
            spread[:, (3 * i + j) * LANES : (3 * i + j + 1) * LANES] = value
    spread.send()
    taps = jnp.concatenate([w[i, j] for i in range(3) for j in range(3)], axis=1)
    da[...] = dot(spread[...], taps, ((1,), (1,)))
    near = ready(near)
    share_stage(da, near, norms, tabs, 2, chan, batch, info, masks, chunks, pieces, stats)


def back_contract_kernel(info, got, *refs):
    *parts, own, norms, tabs, counts, dz, sums, copy = refs
    own = ready(own)
    masks = Masks(info)

    def store(t, value):
        plain = flat(value).astype(BF)
        dz[at(t, CHUNK), :] = plain
        copy[at(t, CHUNK), :] = plain

    own_stage(got, parts, own, norms, tabs, 2, counts[1:2, :], masks, own.shape[0] // CHUNK, sums, store)


def back_merge_kernel(chan, info, *refs):
    dz, w = refs[:chan], refs[chan : 2 * chan]
    g, near3, nears, norms, tabs, g1, stats, dy = refs[2 * chan :]
    masks = Masks(info)
    rows, width = dy.shape
    blocks = width // LANES
    chunks = rows // CHUNK
    acc = None
    for k in range(chan):
        term = dot(dz[k][...], ready(w[k])[...], ((1,), (1,)))
        acc = term if acc is None else acc + term
    dy[...] = acc
    g, near3, nears = ready(g), ready(near3), ready(nears)
    zero = jnp.zeros((IMAGES, LANES), F32)
    lines = [[], [], []]
    for q in range(blocks):
        lanes = slice(q * LANES, (q + 1) * LANES)
        off3, inv3, offs, invs = (norms[n * blocks + q : n * blocks + q + 1, :] for n in range(4))
        gain, bias = 8, 8 + 3 * blocks
        gain3, gains = tabs[0, gain + q : gain + q + 1, :], tabs[0, gain + blocks + q : gain + blocks + q + 1, :]
        shift = tabs[0, bias + q : bias + q + 1, :] + tabs[0, bias + blocks + q : bias + blocks + q + 1, :]

        def step(t, carry):
            zhat3 = (cube(near3[at(t, CHUNK), lanes]) + off3) * inv3
            zhats = (cube(nears[at(t, CHUNK), lanes]) + offs) * invs
            pre = zhat3 * gain3 + zhats * gains + shift
            up = cube(g[at(t, CHUNK), lanes]) + cube(dy[at(t, CHUNK), lanes])
            u = keep(masks.small(t), gelu_slope(pre)) * up
            g1[at(t, CHUNK), lanes] = flat(u)
            return (
                carry[0] + total_of(u * zhat3),
                carry[1] + total_of(u * zhats),
                carry[2] + total_of(u),
            )

        done = repeat(chunks, step, (zero, zero, zero))
        for n in range(3):
            lines[n].append(row_sum(done[n]))
    broadcast_rows(stats, lines[0] + lines[1] + lines[2])


def back_enlarge_kernel(batch, chan, w, info, got, g1, near3, nears, norms3, tabs, counts, *refs):
    near, (norms, dz3, dzs, *pieces, stats, sums, da) = refs[:chan], refs[chan:]
    masks = Masks(info)
    near3, nears = ready(near3), ready(nears)
    count = counts[1:2, :]
    total = whole(got)
    sums[...] = total
    rows, width = g1.shape
    blocks = width // LANES
    chunks = rows // CHUNK
    total = total / count
    gg3, ggs, gb = (total[n * blocks : (n + 1) * blocks] for n in range(3))
    off3, inv3, offs, invs = (norms3[n * blocks : (n + 1) * blocks, :] for n in range(4))
    front3 = tabs[0, 8 : 8 + blocks, :] * inv3
    fronts = tabs[0, 8 + blocks : 8 + 2 * blocks, :] * invs

    def step(t, _):
        mask = masks.small(t)
        for q in range(blocks):
            lanes = slice(q * LANES, (q + 1) * LANES)
            line = slice(q, q + 1)
            u = cube(g1[at(t, CHUNK), lanes]) - gb[line]
            zhat3 = (cube(near3[at(t, CHUNK), lanes]) + off3[line]) * inv3[line]
            zhats = (cube(nears[at(t, CHUNK), lanes]) + offs[line]) * invs[line]
            dz3[at(t, CHUNK), lanes] = flat(keep(mask, front3[line] * (u - zhat3 * gg3[line]))).astype(BF)
            dzs[at(t, CHUNK), lanes] = flat(keep(mask, fronts[line] * (u - zhats * ggs[line]))).astype(BF)
        return 0

    repeat(chunks, step, 0)
    dz3.send()
    dzs.send()
    da[...] = dot(dz3[...], w.use()[...], ((1,), (1,)))
    near = ready(near)
    share_stage(da, near, norms, tabs, 1, chan, batch, info, masks, chunks, pieces, stats)


def back_strided_kernel(info, got, *refs):
    *parts, own, norms, tabs, counts, dz, moved, sums, held = refs
    masks = Masks(info)
    own = ready(own)
    rows = own.shape[0]
    for tap in range(2):
        held[tap, rows : rows + CHUNK, :] = jnp.zeros((CHUNK, LANES), BF)

    def store(t, value):
        plain = flat(value).astype(BF)
        dz[at(t, CHUNK), :] = plain
        held[0, at(t, CHUNK), :] = plain
        held[1, at(t, CHUNK), :] = flat(push_left(value)).astype(BF)

    own_stage(got, parts, own, norms, tabs, 1, counts[1:2, :], masks, rows // CHUNK, sums, store)
    for down in range(2):
        for right in range(2):
            n = 2 * down + right
            moved[:, n * LANES : (n + 1) * LANES] = held[right, down * CHUNK : down * CHUNK + rows, :]


TAPS = {0: ((1, 0),), 1: ((2, 0), (0, 1))}


def back_first_kernel(chan, info, *refs):
    dz, w = refs[:chan], refs[chan : 2 * chan]
    near, norms, tabs, u_out, stats, held, joined, da = refs[2 * chan :]
    masks = Masks(info)
    rows = dz[0].shape[0]
    chunks = rows // CHUNK
    for tap in range(2):
        held[tap, rows : rows + CHUNK, :] = jnp.zeros((CHUNK, chan * LANES), BF)
    for k in range(chan):
        joined[:, :, :, k * LANES : (k + 1) * LANES] = ready(w[k])[...]
    near = ready(near)

    def shift(t, _):
        for k in range(chan):
            lanes = slice(k * LANES, (k + 1) * LANES)
            value = dz[k][at(t, CHUNK), :]
            held[0, at(t, CHUNK), lanes] = value
            held[1, at(t, CHUNK), lanes] = flat(push_left(cube(value))).astype(BF)
        return 0

    repeat(chunks, shift, 0)
    offset, inverse = norms[0:1, :], norms[1:2, :]
    scale, bias = tabs[0, 0:1, :], tabs[0, 4:5, :]
    zero = jnp.zeros((IMAGES, LANES), F32)
    sums = (zero, zero)
    for p in range(2):
        for q in range(2):
            acc = None
            for a, down in TAPS[p]:
                for b, right in TAPS[q]:
                    term = dot(
                        held[right, down * CHUNK : down * CHUNK + rows, :], joined[a, b], ((1,), (1,))
                    )
                    acc = term if acc is None else acc + term
            da[q] = acc

        def step(t, carry, p=p):
            r = 2 * t + p
            place = at(r, LINE)
            zhat = (cube(near[place, :]) + offset) * inverse
            up = merged(cube(da[0, at(t, CHUNK), :]), cube(da[1, at(t, CHUNK), :]))
            u = keep(masks.large(r), gelu_slope(zhat * scale + bias)) * up
            u_out[place, :] = flat(u)
            return carry[0] + total_of(u * zhat), carry[1] + total_of(u)

        sums = repeat(chunks, step, sums)
    broadcast_rows(stats, (row_sum(sums[0]), row_sum(sums[1])))


def back_first_own_kernel(info, got, u, near, norms, tabs, counts, dz, sums):
    masks = Masks(info)
    count = counts[0:1, :]
    total = whole(got)
    gg, gb = total[0:1], total[1:2]
    fill_rows(sums, (gg, gb))
    per_cell, per_hat = gb / count, gg / count
    near = ready(near)
    offset, inverse = norms[0:1, :], norms[1:2, :]
    front = tabs[0, 0:1, :] * inverse

    def step(r, _):
        place = at(r, LINE)
        zhat = (cube(near[place, :]) + offset) * inverse
        value = front * (cube(u[place, :]) - (per_cell + zhat * per_hat))
        dz[place, :] = flat(keep(masks.large(r), value)).astype(BF)
        return 0

    repeat(SIDE, step, 0)


def leave_kernel(chan, info, *refs):
    dz, dzs = refs[:chan], refs[chan : 2 * chan]
    w, ws = refs[2 * chan : 3 * chan], refs[3 * chan : 4 * chan]
    out, dm, extra = refs[4 * chan :]
    masks = Masks(info)
    acc = None
    for k in range(chan):
        term = dot(ready(dzs[k])[...], ready(ws[k])[...], ((1,), (1,)))
        acc = term if acc is None else acc + term
    extra[...] = acc
    width = out.shape[3]
    part = 2 * LINE
    w = ready(w)

    def product(t, _):
        total = None
        for k in range(chan):
            term = dot(dz[k][at(t, part), :], w[k][...], ((1,), (1,)))
            total = term if total is None else total + term
        dm[at(t, part), :] = total
        return 0

    repeat(dm.shape[0] // part, product, 0)

    def step(i, _):
        for p in range(2):
            r = 2 * i + p
            mask = masks.large(r)
            for q in range(width // LANES):
                lanes = slice(q * LANES, (q + 1) * LANES)
                value = cube(dm[at(r, LINE), lanes])
                if p == 0:
                    more = cube(extra[at(i, CHUNK), lanes])
                    value = value + merged(more, jnp.zeros_like(more))
                out[r, :, :, lanes] = keep(mask, value).astype(BF)
        return 0

    repeat(SIDE // 2, step, 0)


def radices_of(batch):
    sizes, units, unit = [], [], 1
    while unit < batch:
        size = 2 if not sizes or batch // unit == 2 else 4
        sizes.append(size)
        units.append(unit)
        unit *= size
    return sizes, units


def numbers_of(sizes, units):
    numbers = [0]
    for size, unit in reversed(list(zip(sizes, units))):
        numbers = [r + m * unit for m in range(size) for r in numbers]
    return numbers


def early_products(chan, info, ins, outs):
    outs[0][...] = dot(ins[0][...], ins[1][...], ((0,), (0,)))
    outs[1][...] = dot(ins[2][...], ins[3][...], ((0,), (0,)))


def rows_products(chan, info, ins, outs):
    *pieces, right = ins
    size = pieces[0].shape[1]
    for k, piece in enumerate(pieces):
        outs[0][at(info[0] ^ k, size), :] = dot(piece[...], right[...], ((0,), (0,)))


def wide_products(chan, info, ins, outs):
    a2, dz3, even, dzs = ins
    outs[0][...] = dot(a2[...], dz3[...], ((0,), (0,)))
    outs[1][...] = dot(even[...], dzs[...], ((0,), (0,)))


def strided_products(chan, info, ins, outs):
    a1, moved = ins
    rows = moved.shape[0]
    for p in range(2):
        for q in range(2):
            start = CHUNK if p else 0
            plane = a1[1 + q, 1 - p, start : start + rows, :]
            for a, down in TAPS[p]:
                for b, right in TAPS[q]:
                    n = 2 * down + right
                    tap = 3 * a + b
                    outs[0][:, tap * LANES : (tap + 1) * LANES] = dot(
                        plane, moved[:, n * LANES : (n + 1) * LANES], ((0,), (0,))
                    )


def cut_product(ref, number, batch):
    rows = ref.shape[0] // batch
    size = MID // batch
    for n in range(rows // size):
        for lane in range(0, ref.shape[1], LANES):
            first = number * rows + n * size
            yield ref[pl.ds(pl.multiple_of(first, size), size), lane : lane + LANES]


def place_chunk(blocks, outs, layout, number):
    blocks = list(blocks)
    for out, (taps, repeats) in zip(outs, layout):
        size = blocks[0].shape[0]
        for n in range(taps * repeats):
            for lane in range(0, out.shape[-1], LANES):
                value = blocks.pop(0).astype(F32)
                if taps > 1:
                    out[n, at(number, size), lane : lane + LANES] = value
                else:
                    first = (number * repeats + n) * size
                    out[pl.ds(pl.multiple_of(first, size), size), lane : lane + LANES] = value


def slot_kernel(batch, chan, plan, info, *refs):
    ins, outs = refs[: plan["ins"]], refs[plan["ins"] :]
    for job in plan["jobs"]:
        if job["kind"] == "pack":
            products = [outs[n] for n in job["products"]]
            job["compute"](chan, info, ready([ins[n] for n in job["ins"]]), products)
            for place, r in enumerate(job["numbers"]):
                number = info[1] ^ r
                blocks = [v for ref in products for v in cut_product(ref, number, batch)]
                for n, block in enumerate(blocks):
                    put(outs, job["targets"], place * len(blocks) + n, block.astype(BF))
        else:
            sources = [(ready(ins[n]), first) for n, first in job["sources"]]
            size = job.get("size")
            if job["kind"] == "fold":
                for n in range(size):
                    total = None
                    for ref, first in sources:
                        value = ref[first + n].astype(F32)
                        total = value if total is None else total + value
                    put(outs, job["targets"], n, total.astype(BF))
            elif job["kind"] == "join":
                for m, (ref, first) in enumerate(sources):
                    for n in range(size):
                        put(outs, job["targets"], m * size + n, ref[first + n])
            else:
                width = job["width"]
                finals = [outs[n] for n in job["finals"]]
                for (ref, first), numbers in zip(sources, job["numbers"]):
                    for place, r in enumerate(numbers):
                        start = first + place * width
                        place_chunk(
                            [ref[start + n] for n in range(width)], finals, job["layout"], info[1] ^ r
                        )


def put(outs, targets, n, block):
    for out, place, first, count in targets:
        if first <= n < first + count:
            outs[out][place + n - first] = block


def solution(mesh):
    batch = mesh.shape["batch"]
    chan = mesh.shape["chan"]
    everyone = ("batch", "chan")
    devices = batch * chan
    half = chan // 2
    pair = (0, half)

    def swap(v, mask, axis="chan"):
        return lax.ppermute(v, axis, [(k, k ^ mask) for k in range(mesh.shape[axis])])

    def widen(found):
        found = dict(found)
        mask = half // 2
        while mask:
            for k in list(found):
                found[k ^ mask] = swap(found[k], mask)
            mask //= 2
        return [found[k] for k in range(chan)]

    def gather(v):
        return widen({0: v, half: swap(v, half)})

    def gather_direct(v):
        return [v] + [swap(v, k) for k in range(1, chan)]

    def deliver(pieces):
        return [pieces[0]] + [swap(pieces[k], k) for k in range(1, chan)]

    def exchange(stats):
        return lax.all_to_all(stats, everyone, 0, 0)

    def exchange_batch(stats):
        return lax.all_to_all(stats, "batch", 0, 0)

    def cut(v, axis):
        size = v.shape[axis] // chan
        me = lax.axis_index("chan")
        return [lax.dynamic_slice_in_dim(v, (me ^ k) * size, size, axis) for k in range(chan)]

    sizes, units = radices_of(batch)
    levels = len(sizes)

    class Gradient:
        def __init__(self, compute, ins, products, layout, shapes, close=()):
            self.compute, self.ins, self.products = compute, ins, products
            self.layout, self.shapes = layout, shapes
            self.width = sum(math.prod(v) for v in products) // (MID * LANES)
            self.close = close
            self.started = 0
            self.result = None

        def partners(self, step):
            level = step if step < levels else 2 * levels - 1 - step
            return [m * units[level] for m in range(1, sizes[level])]

    def slot(info, gradients, last):
        ins, outs, scratch, jobs = [], [], [], []
        bundles = {}
        received = [v for g in gradients if g.started for v, _ in g.got] + [
            g.kept for g in gradients if g.started
        ] + [v for g in gradients if not g.started for v in g.close]
        size = MID // batch

        def give(array):
            for n, v in enumerate(ins):
                if v is array:
                    return n
            ins.append(array)
            return len(ins) - 1

        for g in gradients:
            job = {"targets": []}
            if not g.started:
                job.update(kind="pack", compute=g.compute, numbers=numbers_of(sizes, units))
                job["ins"] = [give(v) for v in g.ins]
                total = batch * g.width
            else:
                done = g.started - 1
                sources = [(give(g.kept), 0)] + [(give(v), first) for v, first in g.got]
                if done < levels:
                    total = g.amount
                    job.update(kind="fold", sources=sources, size=total)
                elif g.started < 2 * levels:
                    total = g.amount * len(sources)
                    job.update(kind="join", sources=sources, size=g.amount)
                    masks = [0] + g.partners(done)
                    g.numbers = [r ^ m for m in masks for r in g.numbers]
                else:
                    masks = [0] + g.partners(done)
                    job.update(kind="place", sources=sources, layout=g.layout, width=g.width)
                    job["numbers"] = [[r ^ m for r in g.numbers] for m in masks]
                    job["finals"] = g
                    jobs.append((g, job, None))
                    continue
            jobs.append((g, job, total))
        for g, job, total in jobs:
            if total is None:
                job["finals"] = list(range(len(outs), len(outs) + len(g.shapes)))
                outs += [(v, F32, "far") for v in g.shapes]
                continue
            step = g.started
            masks = g.partners(step)
            if step < levels:
                share = total // (len(masks) + 1)
                firsts = [share * m for m in range(len(masks) + 1)]
            else:
                share = total
                firsts = [0] * (len(masks) + 1)
                if step == levels:
                    g.numbers = [0]
            g.amount = share
            job["targets"].append((len(outs), 0, firsts[0], share))
            g.kept = len(outs)
            outs.append(((share, size, LANES), BF))
            g.next = []
            for mask, first in zip(masks, firsts[1:]):
                place = bundles.get(mask, 0)
                g.next.append((mask, place))
                bundles[mask] = place + share
                job["targets"].append((mask, place, first, share))
        order = sorted(bundles)
        where = {mask: len(outs) + n for n, mask in enumerate(order)}
        outs += [((bundles[mask], size, LANES), BF) for mask in order]
        for g, job, total in jobs:
            if total is not None:
                job["targets"] = [job["targets"][0]] + [(where[v[0]], *v[1:]) for v in job["targets"][1:]]
            if job["kind"] == "pack":
                job["products"] = list(range(len(outs) + len(scratch), len(outs) + len(scratch) + len(g.products)))
                scratch += [(v, F32) for v in g.products]
        plan = {"ins": len(ins), "jobs": [job for _, job, _ in jobs]}
        given = [v if any(v is w for w in received) else far(v) for v in ins]
        made = in_vmem(
            functools.partial(slot_kernel, batch, chan, plan),
            [info, *given],
            outs,
            scratch,
            after=[last],
            cost=SLOT_COST,
        )
        moved = {mask: swap(made[where[mask]], mask, "batch") for mask in order}
        for g, job, total in jobs:
            if total is None:
                g.result = [made[n] for n in job["finals"]]
            else:
                g.kept = made[g.kept]
                g.got = [(moved[mask], place) for mask, place in g.next]
                g.started += 1
        return made[0] if len(outs[0]) == 2 else far(made[0])

    def local(
        entry_activation,
        image_bounds,
        loss_sensitivity,
        first_contract_kernel,
        first_strided_kernel,
        first_enlarge_kernel,
        projection_kernel,
        second_contract_kernel,
        second_spatial_kernel,
        second_enlarge_kernel,
        bottleneck_gains,
        bottleneck_biases,
        wide_gain_vector,
        wide_bias_vector,
    ):
        images, side, _, quarter = entry_activation.shape
        small = side // 2
        wide = first_enlarge_kernel.shape[1]
        blocks = wide // LANES
        rows, large = small * CHUNK, side * LINE
        depth = quarter * chan
        mid = first_contract_kernel.shape[1] * chan
        assert mid == MID and images == IMAGES and side == SIDE
        piece, full, line = ((rows, LANES), BF), ((rows, wide), BF), ((large, LANES), BF)
        f32s = lambda *shape: (shape, F32)

        info = jnp.concatenate(
            [lax.axis_index("chan")[None], lax.axis_index("batch")[None], image_bounds.T.reshape(-1)]
        ).astype(jnp.int32)
        own = entry_activation.transpose(1, 2, 0, 3).reshape(large, quarter)
        found = {0: own, half: swap(own, half)}
        mask = half // 2
        while mask:
            found[mask] = swap(own, mask)
            mask //= 2
        table = jnp.concatenate(
            [
                bottleneck_gains,
                bottleneck_biases,
                wide_gain_vector.reshape(-1, LANES),
                wide_bias_vector.reshape(-1, LANES),
            ]
        )
        tabs = jnp.stack(gather_direct(table))
        loss = loss_sensitivity.transpose(1, 2, 0, 3)

        early_ks, late_ks = range(half), range(half, chan)
        (z1_part,) = in_vmem(
            functools.partial(first_part_kernel, chan, early_ks),
            [far(first_contract_kernel), info, *[found[k] for k in early_ks]],
            [f32s(large, LANES)],
        )
        found[half] = held_back(found[half], [z1_part])
        mask = half // 2
        while mask:
            found[half ^ mask] = swap(found[half], mask)
            mask //= 2
        source = [found[k] for k in range(chan)]
        z1, stats1 = in_vmem(
            functools.partial(first_kernel, chan, late_ks),
            [far(first_contract_kernel), info, z1_part, *source[half:]],
            [line, f32s(devices, 4, LANES)],
            [f32s(large, LANES)],
        )
        got1 = exchange(stats1)
        z1_far = swap(z1, pair[1])
        even, zs, stats_s, *source_far = in_vmem(
            functools.partial(shortcut_kernel, chan),
            [far(projection_kernel), info, *source],
            [((rows, depth), BF, "far"), (*full, "far"), f32s(2 * blocks, LANES)],
            [f32s(rows, wide)],
            save=range(2, 2 + chan),
        )
        zs_far = swap(zs, pair[1])
        *acts, norms1, counts, z1 = in_vmem(
            functools.partial(first_act_kernel, batch, chan, pair),
            [info, got1, z1, z1_far, tabs],
            [line, line, f32s(8, LANES), f32s(8, LANES)],
            after=[far(zs)],
            save=[2],
        )
        acts = widen(dict(zip(pair, acts)))
        a1, z2, stats2 = in_vmem(
            functools.partial(strided_kernel, chan),
            [far(first_strided_kernel), info, *acts, stats_s],
            [((3, 2, rows + CHUNK, mid), BF, "far"), piece, f32s(devices, 16, LANES)],
            [f32s(rows, LANES)],
        )
        got2 = exchange(stats2)
        near2 = gather_direct(z2)
        a2, z3, stats3, norms2, got2, *near2 = in_vmem(
            functools.partial(enlarge_kernel, batch, chan),
            [far(first_enlarge_kernel), info, got2, *near2, tabs, counts],
            [((rows, mid), BF, "far"), full, f32s(devices, 2 * blocks, LANES), f32s(2 * chan, LANES)],
            [f32s(rows, wide)],
            save=range(2, 3 + chan),
        )
        got3 = exchange(stats3)
        z3_far = swap(z3, pair[1])
        *y1, y1_own, norms3, z3 = in_vmem(
            functools.partial(merge_act_kernel, batch, chan, pair),
            [info, got3, far(got2), z3, z3_far, far(zs), far(zs_far), tabs, counts],
            [full, full, ((rows, wide), F32, "far"), f32s(4 * blocks, LANES)],
            save=[3],
        )
        y1 = widen(dict(zip(pair, y1)))
        z4, stats4, *y1 = in_vmem(
            functools.partial(contract_kernel, chan),
            [far(second_contract_kernel), info, *y1],
            [piece, f32s(devices, 2, LANES)],
            [f32s(rows, LANES)],
            save=range(2, 2 + chan),
        )

        got4 = exchange(stats4)
        near4 = gather_direct(z4)
        a4, z5, stats5, norms4, *near4 = in_vmem(
            functools.partial(spatial_kernel, batch, chan),
            [far(second_spatial_kernel), info, got4, *near4, tabs, counts],
            [((rows, mid), BF, "far"), piece, f32s(devices, 2, LANES), f32s(2 * chan, LANES)],
            [((3, rows + 2 * CHUNK, mid), BF), f32s(rows, LANES)],
            save=range(3, 3 + chan),
        )
        got5 = exchange(stats5)
        near5 = gather_direct(z5)
        a5, z6, stats6, norms5, *near5 = in_vmem(
            functools.partial(last_kernel, batch, chan),
            [far(second_enlarge_kernel), info, got5, *near5, tabs, counts],
            [
                ((rows, mid), BF, "far"),
                f32s(rows, wide),
                f32s(batch, 2 * blocks, LANES),
                f32s(2 * chan, LANES),
            ],
            save=range(3, 3 + chan),
        )
        got6 = exchange_batch(stats6)
        w1t = deliver(cut(first_contract_kernel, 0))
        w2t = deliver(cut(first_strided_kernel, 2))
        wpt = deliver(cut(projection_kernel, 0))
        w4t = deliver(cut(second_contract_kernel, 0))
        result, g2, stats7, norms6, z6 = in_vmem(
            output_kernel,
            [info, got6, z6, far(y1_own), far(loss), tabs, counts],
            [
                ((small, small, images, wide), BF, "far"),
                f32s(rows, wide),
                f32s(batch, 2 * blocks, LANES),
                f32s(2 * blocks, LANES),
            ],
            save=[2],
        )

        shares = [f32s(rows, LANES)] + [piece] * (chan - 1)
        routed = f32s(devices, 2, LANES)
        tap_lanes = 9 * LANES
        got7 = exchange_batch(stats7)
        dz6, *sent, stats8, sums6, g2 = in_vmem(
            functools.partial(back_last_kernel, batch, chan),
            [far(second_enlarge_kernel), info, got7, g2, far(z6), norms6, tabs, counts, *fars(near5), norms5],
            [(*full, "far"), *shares, routed, f32s(2 * blocks, LANES)],
            [f32s(rows, mid)],
            after=fars([*w2t, *w1t, *w4t]),
            save=[3],
        )
        got8 = exchange(stats8)
        parts = deliver(sent)
        spread5, *sent, stats9, sums5 = in_vmem(
            functools.partial(back_spatial_kernel, batch, chan),
            [
                far(second_spatial_kernel), info, got8, *parts, far(near5[0]), norms5, tabs, counts,
                *fars(near4), norms4,
            ],
            [((rows, tap_lanes), BF, "far"), *shares, routed, f32s(8, LANES)],
            [((3, rows + 2 * CHUNK, LANES), BF), f32s(rows, mid)],
            after=fars(wpt),
        )
        got9 = exchange(stats9)
        parts = deliver(sent)
        work = {}

        def slots(point, last):
            for names in SLOTS[point]:
                some = [work[n] for n in names if n in work and work[n].result is None]
                if some:
                    last = slot(info, some, last)
            return last

        work["early"] = Gradient(
            early_products,
            [a5, dz6, a4, spread5],
            [(mid, wide), (mid, tap_lanes)],
            ((1, 1), (9, 1)),
            [(mid, wide), (9, mid, LANES)],
        )
        last = slots("fifth", stats9)
        dz4, sums4, dz4_far = in_vmem(
            back_contract_kernel,
            [info, got9, *parts, far(near4[0]), norms4, tabs, counts],
            [piece, f32s(8, LANES), (*piece, "far")],
            after=[last],
        )
        dz4_all = gather_direct(dz4)
        work["narrowing"] = Gradient(
            rows_products, [*y1, dz4_far], [(wide * chan, LANES)], ((1, 4),), [(wide * chan, LANES)]
        )
        last = slots("fourth", dz4)
        g1, stats10 = in_vmem(
            functools.partial(back_merge_kernel, chan),
            [info, *dz4_all, *fars(w4t), far(g2), far(z3), far(zs), norms3, tabs],
            [f32s(rows, wide), f32s(batch, 4 * blocks, LANES)],
            [f32s(rows, wide)],
            after=[last],
        )
        got10 = exchange_batch(stats10)
        last = slots("merge", stats10)
        dz3, dzs, *sent, stats11, sums3 = in_vmem(
            functools.partial(back_enlarge_kernel, batch, chan),
            [
                far(first_enlarge_kernel), info, got10, g1, far(z3), far(zs), norms3, tabs, counts,
                *fars(near2), norms2,
            ],
            [(*full, "far"), (*full, "far"), *shares, routed, f32s(4 * blocks, LANES)],
            [f32s(rows, mid)],
            after=[last],
        )
        got11 = exchange(stats11)
        parts = deliver(sent)
        work["widening"] = Gradient(
            wide_products,
            [a2, dz3, even, dzs],
            [(mid, wide), (depth, wide)],
            ((1, 1), (1, 2)),
            [(mid, wide), (depth, wide)],
        )
        last = slots("third", stats11)
        last = slots("shares", got11) if SLOTS["shares"] else last
        dz2, moved2, sums2 = in_vmem(
            back_strided_kernel,
            [info, got11, *parts, far(near2[0]), norms2, tabs, counts],
            [piece, ((rows, 4 * LANES), BF, "far"), f32s(8, LANES)],
            [((2, rows + CHUNK, LANES), BF)],
            after=[last],
        )
        dz2_all = gather_direct(dz2)
        last = slots("second", dz2)
        u1, stats12 = in_vmem(
            functools.partial(back_first_kernel, chan),
            [info, *dz2_all, *fars(w2t), far(z1), norms1, tabs],
            [f32s(large, LANES), f32s(batch, 2, LANES)],
            [((2, rows + CHUNK, mid), BF), ((3, 3, LANES, mid), BF), f32s(2, rows, LANES)],
            after=[last],
        )
        got12 = exchange_batch(stats12)
        work["strided"] = Gradient(
            strided_products, [a1, moved2], [(mid, tap_lanes)], ((9, 1),), [(9, mid, LANES)]
        )
        last = slots("strided", stats12)
        dz1, sums1 = in_vmem(
            back_first_own_kernel,
            [info, got12, u1, far(z1), norms1, tabs, counts],
            [line, f32s(8, LANES)],
            after=[last],
        )
        dz1_all = gather(dz1)
        dzs_all = gather(dzs)
        work["reducing"] = Gradient(
            rows_products, [*source_far, dz1], [(depth, LANES)], ((1, 2),), [(depth, LANES)], [dz1]
        )
        last = slots("first", dz1)
        (inputs_grad,) = in_vmem(
            functools.partial(leave_kernel, chan),
            [info, *dz1_all, *fars(dzs_all), *fars(w1t), *fars(wpt)],
            [((side, side, images, quarter), BF, "far")],
            [f32s(large, quarter), f32s(rows, quarter)],
            after=[last],
            cost=LEAVE_COST,
        )
        last = slots("end", far(inputs_grad))
        while any(g.result is None for g in work.values()):
            last = slot(info, [g for g in work.values() if g.result is None], last)
        early, narrowing, widening, strided, reducing = (
            work[name] for name in ("early", "narrowing", "widening", "strided", "reducing")
        )
        (expanding_grad, middle_grad), (narrowing_grad,) = early.result, narrowing.result
        (widening_grad, shortcut_grad), (spatial_grad,), (reducing_grad,) = (
            g.result for g in (widening, strided, reducing)
        )
        tapped = (3, 3, mid, LANES)
        gains3, gains_s, shift3 = (sums3[n * blocks : (n + 1) * blocks].reshape(-1) for n in range(3))
        gains6, shift6 = sums6[:blocks].reshape(-1), sums6[blocks:].reshape(-1)
        return (
            result.transpose(2, 0, 1, 3),
            inputs_grad.transpose(2, 0, 1, 3),
            reducing_grad,
            spatial_grad.reshape(tapped),
            widening_grad,
            shortcut_grad,
            narrowing_grad,
            middle_grad.reshape(tapped),
            expanding_grad,
            jnp.stack([sums1[0], sums2[0], sums4[0], sums5[0]]),
            jnp.stack([sums1[1], sums2[1], sums4[1], sums5[1]]),
            jnp.stack([gains3, gains_s, gains6]),
            jnp.stack([shift3, shift3, shift6]),
        )

    wide_act = P("batch", None, None, "chan")
    cols = P(None, "chan")
    taps = P(None, None, None, "chan")
    return jax.shard_map(
        local,
        mesh=mesh,
        in_specs=(wide_act, P("batch", None), wide_act, cols, taps, cols, cols, cols, taps)
        + (cols,) * 5,
        out_specs=(wide_act, wide_act, cols, taps, cols, cols, cols, taps) + (cols,) * 5,
        check_vma=False,
    )
```
